32 devices in a mesh: view: 4 (over x, core), vol: 8 (over z, y).
Axes of the slice: x: 2, y: 2, z: 4, core: 2. Of those that a mesh axis runs over, the one named last changes fastest.
Arguments:
- raw_views: bfloat16 [12, 256, 64, 128], P('view', 'vol'), may hold values from 0.18 to 5.41, as said below
- weights: float32 [12, 64, 8], P('view'), may hold values from 0.05 to 1
- offsets: int32 [12, 64], P('view'), may hold values from 0 to 56, as said below
- psf_taps: float32 [12, 3, 9], P('view'), may hold values from 0.01 to 1
Outputs:
- joined_volume: float32 [256, 64, 128], P(None, 'vol')
The draws below stay inside these ranges and needn't reach their ends.
Inputs may be any that keep to these rules, and one draw needn't show every extreme that they name: offsets[v, x] - x + 4 lies in -3 to 4 except where clipped to 0 or 56. `raw_views`: positive intensities.
All inputs are finite; a program needn't handle non-finite values.
Results may differ from the reference program's by a relative error of at most 0.0003.
The reference program's roundings to bfloat16 on the way (of `resampled`) count: a program that leaves them out, or rounds other values in their place, can miss the bound.
Values may be sent and summed in bfloat16 or wider, within the bound.
No kernel may reach another device: no remote copies, remote signals or barrier semaphores. Data moves between devices by JAX's collectives and lax.ppermute only.
A program may use at most 64 MiB of HBM per device.

```python
import math
import jax
import jax.numpy as jnp
from jax import lax

VIEWS = 12
BAND = 8
TAPS = 9
ITERS = 2
NY = 128
NZ = 256
NX = 64


def draw_offsets(key, part):
    key_shift, key_jitter = jax.random.split(key)
    offset_shift = jax.random.randint(key_shift, (VIEWS, 1), -2, 4)
    jitter = jax.random.randint(key_jitter, (VIEWS, NX), -1, 2)
    position = jnp.arange(NX, dtype=jnp.int32)[None, :]
    return jnp.clip(position - BAND // 2 + offset_shift + jitter, 0, NX - BAND).astype(jnp.int32)


def draw_raw_views(key, part):
    key_object = jax.random.fold_in(key, 11)
    key_factor = jax.random.fold_in(key, 23)
    common = jnp.exp(jax.random.uniform(key_object, (1, NZ, NX, NY), jnp.float32, jnp.log(0.25), jnp.log(4.0)))
    factor = jnp.exp(jax.random.uniform(key_factor, (VIEWS, NZ, NX, NY), jnp.float32, -0.3, 0.3))
    return (common * factor).astype(jnp.bfloat16)


def levels(own_key, shape, cuts, smallest, top_value):
    def one(axis_at, shards_of):
        draws = jax.random.uniform(jax.random.fold_in(jax.random.fold_in(own_key, 6), axis_at), (shards_of,), jnp.float32, smallest / len(cuts), top_value / len(cuts))
        return jnp.repeat(jnp.exp(draws), shape[axis_at] // shards_of).reshape((-1,) + (1,) * (len(shape) - axis_at - 1))

    level = one(*cuts[0])
    for cut in cuts[1:]:
        level = level * one(*cut)
    return level


def setup_inputs(seed: int = 0) -> dict:
    keys = jax.random.split(jax.random.key(seed), 5)
    raw_views = draw_raw_views(jax.random.fold_in(keys[4], 71), 0)
    weights = jnp.clip(jnp.exp(math.log(1.0) - 2.9957323 * jax.random.uniform(keys[1], (VIEWS, NX, BAND), jnp.float32) ** levels(keys[1], (VIEWS, NX, BAND), ((0, 4),), -0.2, 0.2)), 0.05, 1.0)
    offsets = draw_offsets(jax.random.fold_in(keys[4], 71), 0)
    psf_taps = jnp.clip(jnp.exp(math.log(1.0) - 4.6051702 * jax.random.uniform(keys[3], (VIEWS, 3, TAPS), jnp.float32) ** levels(keys[3], (VIEWS, 3, TAPS), ((0, 4),), -0.2, 0.2)), 0.01, 1.0)
    return dict(raw_views=raw_views, weights=weights, offsets=offsets, psf_taps=psf_taps)


def pad_axis(field, axis, width):
    widths = [(0, 0)] * field.ndim
    widths[axis] = (width, width)
    return jnp.pad(field, widths)


def correlate(extended, taps, axis, length):
    result = taps[0] * lax.slice_in_dim(extended, 0, length, axis=axis)
    for offset in range(1, taps.shape[0]):
        result = result + taps[offset] * lax.slice_in_dim(extended, offset, offset + length, axis=axis)
    return result


def blur_forward(extended, taps, length):
    rim_width = (taps.shape[1] - 1) // 2
    along_x = correlate(extended, taps[1], 1, length)
    along_z = correlate(pad_axis(along_x, 0, rim_width), taps[0], 0, along_x.shape[0])
    return correlate(pad_axis(along_z, 2, rim_width), taps[2], 2, along_z.shape[2])


def blur_back_yz(field, taps):
    rim_width = (taps.shape[1] - 1) // 2
    along_y = correlate(pad_axis(field, 2, rim_width), taps[2][::-1], 2, field.shape[2])
    return correlate(pad_axis(along_y, 0, rim_width), taps[0][::-1], 0, field.shape[0])


def resample_view(planes, weight_rows, first_rows):
    result = jnp.zeros((planes.shape[0], first_rows.shape[0], planes.shape[2]), jnp.float32)
    for offset in range(weight_rows.shape[1]):
        gathered = jnp.take(planes, first_rows + offset, axis=1).astype(jnp.float32)
        result = result + weight_rows[None, :, offset, None] * gathered
    return result.astype(jnp.bfloat16)


def reference(raw_views, weights, offsets, psf_taps):
    weight_norm = weights / jnp.sum(weights, axis=-1, keepdims=True)
    taps_norm = psf_taps / jnp.sum(psf_taps, axis=-1, keepdims=True)
    resampled = lax.map(lambda items: resample_view(items[0], items[1], items[2]), (raw_views, weight_norm, offsets))
    rim_width = (TAPS - 1) // 2

    def add_view(total, view_data):
        return total + view_data.astype(jnp.float32), None

    start_sum, _ = lax.scan(add_view, jnp.zeros(resampled.shape[1:], jnp.float32), resampled)
    joined_volume = start_sum / VIEWS
    width = joined_volume.shape[1]
    for turn in range(ITERS):
        extended = pad_axis(joined_volume, 1, rim_width)

        def one_view(logs, items):
            view_data, taps = items
            blurred = blur_forward(extended, taps, width)
            ratio = view_data.astype(jnp.float32) / blurred
            partial_value = blur_back_yz(ratio, taps)
            back = correlate(pad_axis(partial_value, 1, rim_width), taps[1][::-1], 1, width)
            return logs + jnp.log(back), None

        logs, _ = lax.scan(one_view, jnp.zeros(joined_volume.shape, jnp.float32), (resampled, taps_norm))
        joined_volume = joined_volume * jnp.exp(logs / VIEWS)
    return joined_volume
```

```python
import functools

import jax
import jax.numpy as jnp
from jax import lax
from jax.experimental import pallas as pl
from jax.experimental.pallas import tpu as pltpu
from jax.sharding import PartitionSpec as P

ITERS = 2
CORES = 2
VMEM = pl.BlockSpec(memory_space=pltpu.VMEM)
SMEM = pl.BlockSpec(memory_space=pltpu.SMEM)
PARAMS = pltpu.CompilerParams(vmem_limit_bytes=48 * 1024 * 1024)


def halves(value):
    high = value.astype(jnp.bfloat16)
    low = (value - high.astype(jnp.float32)).astype(jnp.bfloat16)
    return high, low


def resample_kernel(weights_ref, offsets_ref, raw_ref, out_ref):
    weights = weights_ref[0]
    rows, band = weights.shape
    weights = weights / jnp.sum(weights, axis=-1, keepdims=True)
    first = offsets_ref[0]
    source = lax.broadcasted_iota(jnp.int32, (rows, rows), 1)
    matrix = jnp.zeros((rows, rows), jnp.float32)
    for k in range(band):
        matrix = jnp.where(source == first + k, weights[:, k : k + 1], matrix)
    high = matrix.astype(jnp.bfloat16)
    rest = matrix - high.astype(jnp.float32)
    middle = rest.astype(jnp.bfloat16)
    low = (rest - middle.astype(jnp.float32)).astype(jnp.bfloat16)
    left = jnp.concatenate([high, middle, low], axis=0)

    def two_planes(step, carry):
        z = step * 2
        planes = jnp.concatenate([raw_ref[0, z], raw_ref[0, z + 1]], axis=1)
        parts = jnp.dot(left, planes, preferred_element_type=jnp.float32)
        total = parts[:rows] + (parts[rows : 2 * rows] + parts[2 * rows :])
        total = total.astype(jnp.bfloat16)
        width = raw_ref.shape[3]
        out_ref[0, z] = total[:, :width]
        out_ref[0, z + 1] = total[:, width:]
        return carry

    lax.fori_loop(0, raw_ref.shape[1] // 2, two_planes, 0)


def resample(raw, weights, offsets):
    views, planes, rows, width = raw.shape
    block = lambda v: (v, 0, 0, 0)
    return pl.pallas_call(
        resample_kernel,
        grid=(views,),
        out_shape=jax.ShapeDtypeStruct(raw.shape, jnp.bfloat16),
        in_specs=[
            pl.BlockSpec((1,) + weights.shape[1:], lambda v: (v, 0, 0)),
            pl.BlockSpec((1, rows, 1), lambda v: (v, 0, 0)),
            pl.BlockSpec((1, planes, rows, width), block),
        ],
        out_specs=pl.BlockSpec((1, planes, rows, width), block),
        compiler_params=PARAMS,
    )(weights, offsets[:, :, None], raw)


def bands_kernel(taps_ref, out_ref):
    view = pl.program_id(0)
    count = taps_ref.shape[2]
    width = out_ref.shape[2] // 2
    shape = (width, width)
    shift = lax.broadcasted_iota(jnp.int32, shape, 0) - lax.broadcasted_iota(jnp.int32, shape, 1)
    for way in range(2):
        band = jnp.zeros(shape, jnp.float32)
        for t in range(count):
            at = t - count // 2
            band = jnp.where(shift == (-at if way else at), taps_ref[view, 2, t], band)
        high, low = halves(band)
        out_ref[0, way, :width, :width] = high
        out_ref[0, way, width:, :width] = high
        out_ref[0, way, :width, width:] = low
        out_ref[0, way, width:, width:] = jnp.zeros_like(low)


def bands(taps, width):
    views = taps.shape[0]
    return pl.pallas_call(
        bands_kernel,
        grid=(views,),
        out_shape=jax.ShapeDtypeStruct((views, 2, 2 * width, 2 * width), jnp.bfloat16),
        in_specs=[SMEM],
        out_specs=pl.BlockSpec((1, 2, 2 * width, 2 * width), lambda v: (v, 0, 0, 0)),
        compiler_params=PARAMS,
    )(taps)


def start_kernel(views, place_ref, *refs):
    mains, rims, (out_ref, start_ref, window) = refs[:4], refs[4:8], refs[8:]
    step = pl.program_id(0)
    chip, core = place_ref[0], place_ref[1]
    planes = start_ref.shape[0]
    main, rim = mains[0].shape[1], rims[0].shape[1]

    @pl.when(step == 0)
    def _():
        start_ref[...] = jnp.zeros_like(start_ref)

    for group in range(4):
        for z in range(main):
            window[rim * (1 - chip) + z] = mains[group][0, z]
        for z in range(rim):
            window[main * chip + z] = rims[group][0, z]
        for z in range(planes + 2 * rim):
            plane = window[planes * core + z]
            out_ref[group, 0, z] = plane
            if rim <= z < rim + planes:
                start_ref[z - rim] += plane.astype(jnp.float32)

    @pl.when(step == pl.num_programs(0) - 1)
    def _():
        start_ref[...] = start_ref[...] / views


def gather_start(place, mains, rims, planes):
    count, main, rows, width = mains[0].shape
    rim = rims[0].shape[1]
    take = lambda v: (v, 0, 0, 0)
    bricks, start = pl.pallas_call(
        functools.partial(start_kernel, 4 * count),
        grid=(count,),
        out_shape=(
            jax.ShapeDtypeStruct((4, count, planes + 2 * rim, rows, width), jnp.bfloat16),
            jax.ShapeDtypeStruct((planes, rows, width), jnp.float32),
        ),
        in_specs=[SMEM]
        + [pl.BlockSpec((1, main, rows, width), take)] * 4
        + [pl.BlockSpec((1, rim, rows, width), take)] * 4,
        out_specs=(
            pl.BlockSpec((4, 1, planes + 2 * rim, rows, width), lambda v: (0, v, 0, 0, 0)),
            pl.BlockSpec((planes, rows, width), lambda v: (0, 0, 0)),
        ),
        scratch_shapes=[pltpu.VMEM((main + rim, rows, width), jnp.bfloat16)],
        compiler_params=PARAMS,
    )(place, *mains, *rims)
    return bricks.reshape((4 * count,) + bricks.shape[2:]), start


def update_kernel(taps_ref, bands_ref, brick_ref, before_ref, own_ref, after_ref, out_ref, wide, left, ratio, back, logs):
    view = pl.program_id(0)
    taps = taps_ref.shape[2]
    rim = taps // 2
    planes, rows, width = own_ref.shape
    outer = planes + 2 * rim
    edge = 8

    @pl.when(view == 0)
    def _():
        logs[...] = jnp.zeros_like(logs)
        for scratch in (wide, back):
            depth = scratch.shape[0]
            scratch[:, :edge, :] = jnp.zeros((depth, edge, width), jnp.float32)
            scratch[:, edge + rows :, :] = jnp.zeros((depth, edge, width), jnp.float32)

    gain_z = [taps_ref[view, 0, t] for t in range(taps)]
    gain_x = [taps_ref[view, 1, t] for t in range(taps)]

    def correlate(gains, terms):
        total = gains[0] * terms[0]
        for t in range(1, taps):
            total = total + gains[t] * terms[t]
        return total

    def along_z(k, carry):
        at = pl.ds(pl.multiple_of(k * 8, 8), 8)
        column = [ref[z, at, :] for ref in (before_ref, own_ref, after_ref) for z in range(ref.shape[0])]
        for z in range(outer):
            wide[z, pl.ds(pl.multiple_of(k * 8, 8) + edge, 8), :] = correlate(gain_z, column[z : z + taps])
        return carry

    lax.fori_loop(0, rows // 8, along_z, 0)

    def along_x(source, gains, z):
        for k in range(rows // 16):
            parts = []
            for half in range(2):
                first = edge - rim + 16 * k + 8 * half
                parts.append(correlate(gains, [source[z, pl.ds(first + t, 8), :] for t in range(taps)]))
            high, low = halves(jnp.concatenate(parts, axis=0))
            at = pl.ds(pl.multiple_of(z * rows + 16 * k, 16), 16)
            left[at, :width] = high
            left[at, width:] = low

    def forward_x(z, carry):
        along_x(wide, gain_x, z)
        return carry

    lax.fori_loop(0, outer, forward_x, 0)

    product = jnp.dot(left[...], bands_ref[0, 0], preferred_element_type=jnp.float32)
    blurred = product[:, :width] + product[:, width:]
    ratio[...] = brick_ref[0].astype(jnp.float32) / blurred.reshape(outer, rows, width)

    def back_z(k, carry):
        at = pl.ds(pl.multiple_of(k * 8, 8), 8)
        column = [ratio[z, at, :] for z in range(outer)]
        for z in range(planes):
            back[z, pl.ds(pl.multiple_of(k * 8, 8) + edge, 8), :] = correlate(gain_z[::-1], column[z : z + taps])
        return carry

    lax.fori_loop(0, rows // 8, back_z, 0)

    def back_x(z, carry):
        along_x(back, gain_x[::-1], z)
        return carry

    lax.fori_loop(0, planes, back_x, 0)

    product = jnp.dot(left[: planes * rows, :], bands_ref[0, 1], preferred_element_type=jnp.float32)
    logs[...] += jnp.log(product[:, :width] + product[:, width:]).reshape(logs.shape)

    @pl.when(view == pl.num_programs(0) - 1)
    def _():
        out_ref[...] = own_ref[...] * jnp.exp(logs[...] / pl.num_programs(0))


def update(taps, band, bricks, before, own, after):
    views, outer, rows, width = bricks.shape
    planes = own.shape[0]
    return pl.pallas_call(
        update_kernel,
        grid=(views,),
        out_shape=jax.ShapeDtypeStruct(own.shape, jnp.float32),
        in_specs=[
            SMEM,
            pl.BlockSpec((1,) + band.shape[1:], lambda v: (v, 0, 0, 0)),
            pl.BlockSpec((1, outer, rows, width), lambda v: (v, 0, 0, 0)),
            VMEM,
            VMEM,
            VMEM,
        ],
        out_specs=VMEM,
        scratch_shapes=[
            pltpu.VMEM((outer, rows + 16, width), jnp.float32),
            pltpu.VMEM((outer * rows, 2 * width), jnp.bfloat16),
            pltpu.VMEM((outer, rows, width), jnp.float32),
            pltpu.VMEM((planes, rows + 16, width), jnp.float32),
            pltpu.VMEM((planes, rows, width), jnp.float32),
        ],
        compiler_params=PARAMS,
    )(taps, band, bricks, before, own, after)


def partner(value, bit, members):
    return lax.ppermute(value, "view", [(i, i ^ bit) for i in range(members)])


def z_rims(own, width, members, blocks):
    planes = own.shape[0]
    hops = -(-width // planes)
    axes = ("view", "vol")
    at = lambda line: (line % members) * blocks + line // members
    total = members * blocks
    before, after = [], []
    for hop in range(hops, 0, -1):
        count = min(planes, width - (hop - 1) * planes)
        up = [(at(i), at(i + hop)) for i in range(total - hop)]
        before.append(lax.ppermute(own[planes - count :], axes, up))
    for hop in range(1, hops + 1):
        count = min(planes, width - (hop - 1) * planes)
        down = [(at(i + hop), at(i)) for i in range(total - hop)]
        after.append(lax.ppermute(own[:count], axes, down))
    join = lambda parts: parts[0] if len(parts) == 1 else jnp.concatenate(parts)
    return join(before), join(after)


def per_device(raw_views, weights, offsets, psf_taps):
    views, depth, rows, width = raw_views.shape
    members, blocks = lax.axis_size("view"), lax.axis_size("vol")
    rim = (psf_taps.shape[2] - 1) // 2
    planes = depth // members
    me = lax.axis_index("view")
    chip, core = me // CORES, me % CORES

    up = [(i, i + 1) for i in range(blocks - 1)]
    down = [(i + 1, i) for i in range(blocks - 1)]
    raw_rims = jnp.concatenate(
        [
            lax.ppermute(raw_views[:, depth - rim :], "vol", up),
            lax.ppermute(raw_views[:, :rim], "vol", down),
        ],
        axis=1,
    )
    all_taps = lax.all_gather(psf_taps, "view")
    all_taps = jnp.concatenate([all_taps[me ^ k] for k in range(members)])
    all_taps = all_taps / jnp.sum(all_taps, axis=-1, keepdims=True)
    band = bands(all_taps, width)

    inner = resample(raw_views, weights, offsets)
    main = 2 * planes + rim
    step = 2 * planes - rim
    own_main = lax.dynamic_slice_in_dim(inner, chip * step, main, axis=1)
    far_main = partner(lax.dynamic_slice_in_dim(inner, (1 - chip) * step, main, axis=1), 2, members)
    rims = resample(raw_rims, weights, offsets)
    own_rim = lax.dynamic_slice_in_dim(rims, chip * rim, rim, axis=1)
    far_rim = partner(lax.dynamic_slice_in_dim(rims, (1 - chip) * rim, rim, axis=1), 2, members)
    mains = [own_main, partner(own_main, 1, members), far_main, partner(far_main, 1, members)]
    rims = [own_rim, partner(own_rim, 1, members), far_rim, partner(far_rim, 1, members)]
    place = jnp.stack([chip, core]).astype(jnp.int32)
    bricks, joined = gather_start(place, mains, rims, planes)

    for turn in range(ITERS):
        before, after = z_rims(joined, 2 * rim, members, blocks)
        joined = update(all_taps, band, bricks, before, joined, after)

    columns = lax.all_to_all(joined, "vol", split_axis=1, concat_axis=0, tiled=True)
    far = partner(columns, 2, members)
    pair = jnp.stack([columns, far])
    parts = [columns, None, far, None]
    near = partner(pair, 1, members)
    parts[1], parts[3] = near[0], near[1]
    width_x = columns.shape[1]
    result = jnp.zeros((blocks, members, planes, width_x, width), jnp.float32)
    for k in range(members):
        piece = parts[k].reshape(blocks, 1, planes, width_x, width)
        result = lax.dynamic_update_slice(result, piece, (0, me ^ k, 0, 0, 0))
    return result.reshape(blocks * depth, width_x, width)


def solution(mesh):
    placed = (
        P("view", "vol", None, None),
        P("view", None, None),
        P("view", None),
        P("view", None, None),
    )
    return jax.shard_map(
        per_device, mesh=mesh, in_specs=placed, out_specs=P(None, "vol", None), check_vma=False
    )
```

```python
import functools

import jax
import jax.numpy as jnp
from jax import lax
from jax.experimental import pallas as pl
from jax.experimental.pallas import tpu as pltpu
from jax.sharding import PartitionSpec as P

ITERS = 2
CORES = 2
VMEM = pl.BlockSpec(memory_space=pltpu.VMEM)
SMEM = pl.BlockSpec(memory_space=pltpu.SMEM)
PARAMS = pltpu.CompilerParams(vmem_limit_bytes=48 * 1024 * 1024)


def halves(value):
    high = value.astype(jnp.bfloat16)
    low = (value - high.astype(jnp.float32)).astype(jnp.bfloat16)
    return high, low


def resample_kernel(weights_ref, offsets_ref, raw_ref, out_ref):
    weights = weights_ref[0]
    rows, band = weights.shape
    weights = weights / jnp.sum(weights, axis=-1, keepdims=True)
    first = offsets_ref[0]
    source = lax.broadcasted_iota(jnp.int32, (rows, rows), 1)
    matrix = jnp.zeros((rows, rows), jnp.float32)
    for k in range(band):
        matrix = jnp.where(source == first + k, weights[:, k : k + 1], matrix)
    high = matrix.astype(jnp.bfloat16)
    rest = matrix - high.astype(jnp.float32)
    middle = rest.astype(jnp.bfloat16)
    low = (rest - middle.astype(jnp.float32)).astype(jnp.bfloat16)
    left = jnp.concatenate([high, middle, low], axis=1)
    width = raw_ref.shape[3]

    def eight_planes(step, carry):
        for pair in range(4):
            z = step * 8 + pair * 2
            planes = jnp.concatenate([raw_ref[0, z], raw_ref[0, z + 1]], axis=1)
            planes = jnp.concatenate([planes, planes, planes], axis=0)
            total = jnp.dot(left, planes, preferred_element_type=jnp.float32).astype(jnp.bfloat16)
            out_ref[0, z] = total[:, :width]
            out_ref[0, z + 1] = total[:, width:]
        return carry

    lax.fori_loop(0, raw_ref.shape[1] // 8, eight_planes, 0)


def resample(raw, weights, offsets):
    views, planes, rows, width = raw.shape
    block = lambda v: (v, 0, 0, 0)
    return pl.pallas_call(
        resample_kernel,
        grid=(views,),
        out_shape=jax.ShapeDtypeStruct(raw.shape, jnp.bfloat16),
        in_specs=[
            pl.BlockSpec((1,) + weights.shape[1:], lambda v: (v, 0, 0)),
            pl.BlockSpec((1, rows, 1), lambda v: (v, 0, 0)),
            pl.BlockSpec((1, planes, rows, width), block),
        ],
        out_specs=pl.BlockSpec((1, planes, rows, width), block),
        compiler_params=PARAMS,
        cost_estimate=pl.CostEstimate(flops=0, bytes_accessed=16 * raw.size, transcendentals=0),
    )(weights, offsets[:, :, None], raw)


def bands_kernel(taps_ref, out_ref):
    view = pl.program_id(0)
    count = taps_ref.shape[2]
    width = out_ref.shape[2] // 2
    shape = (width, width)
    shift = lax.broadcasted_iota(jnp.int32, shape, 0) - lax.broadcasted_iota(jnp.int32, shape, 1)
    for way in range(2):
        band = jnp.zeros(shape, jnp.float32)
        for t in range(count):
            at = t - count // 2
            band = jnp.where(shift == (-at if way else at), taps_ref[view, 2, t], band)
        high, low = halves(band)
        out_ref[0, way, :width, :width] = high
        out_ref[0, way, width:, :width] = high
        out_ref[0, way, :width, width:] = low
        out_ref[0, way, width:, width:] = jnp.zeros_like(low)


def bands(taps, width):
    views = taps.shape[0]
    return pl.pallas_call(
        bands_kernel,
        grid=(views,),
        out_shape=jax.ShapeDtypeStruct((views, 2, 2 * width, 2 * width), jnp.bfloat16),
        in_specs=[SMEM],
        out_specs=pl.BlockSpec((1, 2, 2 * width, 2 * width), lambda v: (v, 0, 0, 0)),
        compiler_params=PARAMS,
    )(taps)


def start_kernel(views, place_ref, *refs):
    mains, rims, (out_ref, start_ref, window) = refs[:4], refs[4:8], refs[8:]
    step = pl.program_id(0)
    chip, core = place_ref[0], place_ref[1]
    planes = start_ref.shape[0]
    main, rim = mains[0].shape[1], rims[0].shape[1]

    @pl.when(step == 0)
    def _():
        start_ref[...] = jnp.zeros_like(start_ref)

    for group in range(4):
        for z in range(main):
            window[rim * (1 - chip) + z] = mains[group][0, z]
        for z in range(rim):
            window[main * chip + z] = rims[group][0, z]
        for z in range(planes + 2 * rim):
            plane = window[planes * core + z]
            out_ref[group, 0, z] = plane
            if rim <= z < rim + planes:
                start_ref[z - rim] += plane.astype(jnp.float32)

    @pl.when(step == pl.num_programs(0) - 1)
    def _():
        start_ref[...] = start_ref[...] / views


def gather_start(place, mains, rims, planes):
    count, main, rows, width = mains[0].shape
    rim = rims[0].shape[1]
    take = lambda v: (v, 0, 0, 0)
    bricks, start = pl.pallas_call(
        functools.partial(start_kernel, 4 * count),
        grid=(count,),
        out_shape=(
            jax.ShapeDtypeStruct((4, count, planes + 2 * rim, rows, width), jnp.bfloat16),
            jax.ShapeDtypeStruct((planes, rows, width), jnp.float32),
        ),
        in_specs=[SMEM]
        + [pl.BlockSpec((1, main, rows, width), take)] * 4
        + [pl.BlockSpec((1, rim, rows, width), take)] * 4,
        out_specs=(
            pl.BlockSpec((4, 1, planes + 2 * rim, rows, width), lambda v: (0, v, 0, 0, 0)),
            pl.BlockSpec((planes, rows, width), lambda v: (0, 0, 0)),
        ),
        scratch_shapes=[pltpu.VMEM((main + rim, rows, width), jnp.bfloat16)],
        compiler_params=PARAMS,
    )(place, *mains, *rims)
    return bricks.reshape((4 * count,) + bricks.shape[2:]), start


def update_kernel(taps_ref, bands_ref, brick_ref, before_ref, own_ref, after_ref, out_ref, wide, left, ratio, back, logs):
    view = pl.program_id(0)
    taps = taps_ref.shape[2]
    rim = taps // 2
    planes, rows, width = own_ref.shape
    outer = planes + 2 * rim
    edge = 8

    @pl.when(view == 0)
    def _():
        logs[...] = jnp.zeros_like(logs)
        for scratch in (wide, back):
            depth = scratch.shape[0]
            scratch[:, :edge, :] = jnp.zeros((depth, edge, width), jnp.float32)
            scratch[:, edge + rows :, :] = jnp.zeros((depth, edge, width), jnp.float32)

    gain_z = [taps_ref[view, 0, t] for t in range(taps)]
    gain_x = [taps_ref[view, 1, t] for t in range(taps)]

    def correlate(gains, terms):
        total = gains[0] * terms[0]
        for t in range(1, taps):
            total = total + gains[t] * terms[t]
        return total

    def along_z(k, carry):
        at = pl.ds(pl.multiple_of(k * 8, 8), 8)
        column = [ref[z, at, :] for ref in (before_ref, own_ref, after_ref) for z in range(ref.shape[0])]
        for z in range(outer):
            wide[z, pl.ds(pl.multiple_of(k * 8, 8) + edge, 8), :] = correlate(gain_z, column[z : z + taps])
        return carry

    lax.fori_loop(0, rows // 8, along_z, 0)

    def along_x(source, gains, z):
        for k in range(rows // 16):
            parts = []
            for half in range(2):
                first = edge - rim + 16 * k + 8 * half
                parts.append(correlate(gains, [source[z, pl.ds(first + t, 8), :] for t in range(taps)]))
            high, low = halves(jnp.concatenate(parts, axis=0))
            at = pl.ds(pl.multiple_of(z * rows + 16 * k, 16), 16)
            left[at, :width] = high
            left[at, width:] = low

    def forward_x(z, carry):
        along_x(wide, gain_x, z)
        return carry

    lax.fori_loop(0, outer, forward_x, 0)

    product = jnp.dot(left[...], bands_ref[0, 0], preferred_element_type=jnp.float32)
    blurred = product[:, :width] + product[:, width:]
    ratio[...] = brick_ref[0].astype(jnp.float32) / blurred.reshape(outer, rows, width)

    def back_z(k, carry):
        at = pl.ds(pl.multiple_of(k * 8, 8), 8)
        column = [ratio[z, at, :] for z in range(outer)]
        for z in range(planes):
            back[z, pl.ds(pl.multiple_of(k * 8, 8) + edge, 8), :] = correlate(gain_z[::-1], column[z : z + taps])
        return carry

    lax.fori_loop(0, rows // 8, back_z, 0)

    def back_x(z, carry):
        along_x(back, gain_x[::-1], z)
        return carry

    lax.fori_loop(0, planes, back_x, 0)

    product = jnp.dot(left[: planes * rows, :], bands_ref[0, 1], preferred_element_type=jnp.float32)
    logs[...] += jnp.log(product[:, :width] + product[:, width:]).reshape(logs.shape)

    @pl.when(view == pl.num_programs(0) - 1)
    def _():
        out_ref[...] = own_ref[...] * jnp.exp(logs[...] / pl.num_programs(0))


def update(taps, band, bricks, before, own, after):
    views, outer, rows, width = bricks.shape
    planes = own.shape[0]
    return pl.pallas_call(
        update_kernel,
        grid=(views,),
        out_shape=jax.ShapeDtypeStruct(own.shape, jnp.float32),
        in_specs=[
            SMEM,
            pl.BlockSpec((1,) + band.shape[1:], lambda v: (v, 0, 0, 0)),
            pl.BlockSpec((1, outer, rows, width), lambda v: (v, 0, 0, 0)),
            VMEM,
            VMEM,
            VMEM,
        ],
        out_specs=VMEM,
        scratch_shapes=[
            pltpu.VMEM((outer, rows + 16, width), jnp.float32),
            pltpu.VMEM((outer * rows, 2 * width), jnp.bfloat16),
            pltpu.VMEM((outer, rows, width), jnp.float32),
            pltpu.VMEM((planes, rows + 16, width), jnp.float32),
            pltpu.VMEM((planes, rows, width), jnp.float32),
        ],
        compiler_params=PARAMS,
    )(taps, band, bricks, before, own, after)


def partner(value, bit, members):
    return lax.ppermute(value, "view", [(i, i ^ bit) for i in range(members)])


def z_rims(own, width, members, blocks):
    planes = own.shape[0]
    hops = -(-width // planes)
    axes = ("view", "vol")
    at = lambda line: (line % members) * blocks + line // members
    total = members * blocks
    before, after = [], []
    for hop in range(hops, 0, -1):
        count = min(planes, width - (hop - 1) * planes)
        up = [(at(i), at(i + hop)) for i in range(total - hop)]
        before.append(lax.ppermute(own[planes - count :], axes, up))
    for hop in range(1, hops + 1):
        count = min(planes, width - (hop - 1) * planes)
        down = [(at(i + hop), at(i)) for i in range(total - hop)]
        after.append(lax.ppermute(own[:count], axes, down))
    join = lambda parts: parts[0] if len(parts) == 1 else jnp.concatenate(parts)
    return join(before), join(after)


def per_device(raw_views, weights, offsets, psf_taps):
    views, depth, rows, width = raw_views.shape
    members, blocks = lax.axis_size("view"), lax.axis_size("vol")
    rim = (psf_taps.shape[2] - 1) // 2
    planes = depth // members
    me = lax.axis_index("view")
    chip, core = me // CORES, me % CORES

    up = [(i, i + 1) for i in range(blocks - 1)]
    down = [(i + 1, i) for i in range(blocks - 1)]
    raw_rims = jnp.concatenate(
        [
            lax.ppermute(raw_views[:, depth - rim :], "vol", up),
            lax.ppermute(raw_views[:, :rim], "vol", down),
        ],
        axis=1,
    )
    pair_taps = jnp.stack([psf_taps, partner(psf_taps, 2, members)])
    near_taps = partner(pair_taps, 1, members)
    all_taps = jnp.stack([pair_taps[0], near_taps[0], pair_taps[1], near_taps[1]])
    all_taps = all_taps.reshape((-1,) + psf_taps.shape[1:])
    all_taps = all_taps / jnp.sum(all_taps, axis=-1, keepdims=True)
    band = bands(all_taps, width)

    inner = resample(raw_views, weights, offsets)
    main = 2 * planes + rim
    step = 2 * planes - rim
    inner, raw_rims = lax.optimization_barrier((inner, raw_rims))
    own_main = lax.dynamic_slice_in_dim(inner, chip * step, main, axis=1)
    far_main = partner(lax.dynamic_slice_in_dim(inner, (1 - chip) * step, main, axis=1), 2, members)
    rims = resample(raw_rims, weights, offsets)
    own_rim = lax.dynamic_slice_in_dim(rims, chip * rim, rim, axis=1)
    far_rim = partner(lax.dynamic_slice_in_dim(rims, (1 - chip) * rim, rim, axis=1), 2, members)
    far_main, band, own_rim = lax.optimization_barrier((far_main, band, own_rim))
    mains = [own_main, partner(own_main, 1, members), far_main, partner(far_main, 1, members)]
    rims = [own_rim, partner(own_rim, 1, members), far_rim, partner(far_rim, 1, members)]
    place = jnp.stack([chip, core]).astype(jnp.int32)
    bricks, joined = gather_start(place, mains, rims, planes)

    for turn in range(ITERS):
        before, after = z_rims(joined, 2 * rim, members, blocks)
        joined = update(all_taps, band, bricks, before, joined, after)

    columns = lax.all_to_all(joined, "vol", split_axis=1, concat_axis=0, tiled=True)
    far = partner(columns, 2, members)
    pair = jnp.stack([columns, far])
    parts = [columns, None, far, None]
    near = partner(pair, 1, members)
    parts[1], parts[3] = near[0], near[1]
    width_x = columns.shape[1]
    result = jnp.zeros((blocks, members, planes, width_x, width), jnp.float32)
    for k in range(members):
        piece = parts[k].reshape(blocks, 1, planes, width_x, width)
        result = lax.dynamic_update_slice(result, piece, (0, me ^ k, 0, 0, 0))
    return result.reshape(blocks * depth, width_x, width)


def solution(mesh):
    placed = (
        P("view", "vol", None, None),
        P("view", None, None),
        P("view", None),
        P("view", None, None),
    )
    return jax.shard_map(
        per_device, mesh=mesh, in_specs=placed, out_specs=P(None, "vol", None), check_vma=False
    )
```

```python
import functools

import jax
import jax.numpy as jnp
from jax import lax
from jax.experimental import pallas as pl
from jax.experimental.pallas import tpu as pltpu
from jax.sharding import PartitionSpec as P

ITERS = 2
CORES = 2
VMEM = pl.BlockSpec(memory_space=pltpu.VMEM)
SMEM = pl.BlockSpec(memory_space=pltpu.SMEM)
PARAMS = pltpu.CompilerParams(vmem_limit_bytes=48 * 1024 * 1024)


def halves(value):
    high = value.astype(jnp.bfloat16)
    low = (value - high.astype(jnp.float32)).astype(jnp.bfloat16)
    return high, low


def resample_kernel(place_ref, weights_ref, offsets_ref, before_ref, raw_ref, after_ref, own_ref, far_ref, wide):
    weights = weights_ref[0]
    band, rows = weights.shape
    width = raw_ref.shape[3]
    weights = weights / jnp.sum(weights, axis=0, keepdims=True)
    first = offsets_ref[0]
    source = lax.broadcasted_iota(jnp.int32, (rows, rows), 0)
    matrix = jnp.zeros((rows, rows), jnp.float32)
    for k in range(band):
        matrix = jnp.where(source == first + k, weights[k : k + 1, :], matrix)
    matrix = matrix.T
    high = matrix.astype(jnp.bfloat16)
    rest = matrix - high.astype(jnp.float32)
    middle = rest.astype(jnp.bfloat16)
    low = (rest - middle.astype(jnp.float32)).astype(jnp.bfloat16)
    left = jnp.concatenate([high, middle, low], axis=1)

    def four_planes(ref, base, first_z):
        for pair in range(2):
            z = first_z + pair * 2
            planes = jnp.concatenate([ref[0, z], ref[0, z + 1]], axis=1)
            planes = jnp.concatenate([planes, planes, planes], axis=0)
            total = jnp.dot(left, planes, preferred_element_type=jnp.float32).astype(jnp.bfloat16)
            wide[base + z] = total[:, :width]
            wide[base + z + 1] = total[:, width:]

    rim, depth = before_ref.shape[1], raw_ref.shape[1]
    four_planes(before_ref, 0, 0)
    four_planes(after_ref, rim + depth, 0)

    def eight_planes(step, carry):
        four_planes(raw_ref, rim, step * 8)
        four_planes(raw_ref, rim, step * 8 + 4)
        return carry

    lax.fori_loop(0, depth // 8, eight_planes, 0)
    chip = place_ref[0]
    half = depth // 2
    for z in range(own_ref.shape[1]):
        own_ref[0, z] = wide[half * chip + z]
        far_ref[0, z] = wide[half * (1 - chip) + z]


def resample(place, weights, offsets, before, raw, after):
    views, depth, rows, width = raw.shape
    rim, band = before.shape[1], weights.shape[2]
    window = depth // 2 + 2 * rim
    block = lambda planes: pl.BlockSpec((1, planes, rows, width), lambda v: (v, 0, 0, 0))
    shape = jax.ShapeDtypeStruct((views, window, rows, width), jnp.bfloat16)
    return pl.pallas_call(
        resample_kernel,
        grid=(views,),
        out_shape=(shape, shape),
        in_specs=[
            SMEM,
            pl.BlockSpec((1, band, rows), lambda v: (v, 0, 0)),
            pl.BlockSpec((1, 1, rows), lambda v: (v, 0, 0)),
            block(rim),
            block(depth),
            block(rim),
        ],
        out_specs=(block(window), block(window)),
        scratch_shapes=[pltpu.VMEM((depth + 2 * rim, rows, width), jnp.bfloat16)],
        compiler_params=PARAMS,
    )(place, weights.transpose(0, 2, 1), offsets[:, None, :], before, raw, after)


def bands_kernel(taps_ref, out_ref):
    view = pl.program_id(0)
    count = taps_ref.shape[2]
    width = out_ref.shape[2] // 2
    shape = (width, width)
    shift = lax.broadcasted_iota(jnp.int32, shape, 0) - lax.broadcasted_iota(jnp.int32, shape, 1)
    for way in range(2):
        band = jnp.zeros(shape, jnp.float32)
        for t in range(count):
            at = t - count // 2
            band = jnp.where(shift == (-at if way else at), taps_ref[view, 2, t], band)
        high, low = halves(band)
        out_ref[0, way, :width, :width] = high
        out_ref[0, way, width:, :width] = high
        out_ref[0, way, :width, width:] = low
        out_ref[0, way, width:, width:] = jnp.zeros_like(low)


def bands(taps, width):
    views = taps.shape[0]
    return pl.pallas_call(
        bands_kernel,
        grid=(views,),
        out_shape=jax.ShapeDtypeStruct((views, 2, 2 * width, 2 * width), jnp.bfloat16),
        in_specs=[SMEM],
        out_specs=pl.BlockSpec((1, 2, 2 * width, 2 * width), lambda v: (v, 0, 0, 0)),
        compiler_params=PARAMS,
    )(taps)


def start_kernel(views, planes, place_ref, *refs):
    windows, start_ref = refs[:-1], refs[-1]
    step = pl.program_id(0)
    core = place_ref[1]
    for z in range(start_ref.shape[0]):
        total = windows[0][0, planes * core + z].astype(jnp.float32)
        for window in windows[1:]:
            total = total + window[0, planes * core + z].astype(jnp.float32)

        @pl.when(step == 0)
        def _():
            start_ref[z] = total

        @pl.when(step > 0)
        def _():
            start_ref[z] += total

    @pl.when(step == pl.num_programs(0) - 1)
    def _():
        start_ref[...] = start_ref[...] / views


def sum_views(place, windows, planes, rim):
    count, window, rows, width = windows[0].shape
    return pl.pallas_call(
        functools.partial(start_kernel, len(windows) * count, planes),
        grid=(count,),
        out_shape=jax.ShapeDtypeStruct((planes + 2 * rim, rows, width), jnp.float32),
        in_specs=[SMEM] + [pl.BlockSpec((1, window, rows, width), lambda v: (v, 0, 0, 0))] * len(windows),
        out_specs=VMEM,
        compiler_params=PARAMS,
    )(place, *windows)


def update_kernel(count, place_ref, taps_ref, *refs):
    bands_ref, windows, parts = refs[0], refs[1 : 1 + count], refs[1 + count : 4 + count]
    out_ref, wide, left, ratio, back, logs = refs[4 + count :]
    step = pl.program_id(0)
    taps = taps_ref.shape[2]
    rim = taps // 2
    planes, rows, width = out_ref.shape
    outer = planes + 2 * rim
    edge = 8
    volume = [(ref, z) for ref in parts for z in range(ref.shape[0])]

    @pl.when(step == 0)
    def _():
        logs[...] = jnp.zeros_like(logs)
        for scratch in (wide, back):
            depth = scratch.shape[0]
            scratch[:, :edge, :] = jnp.zeros((depth, edge, width), jnp.float32)
            scratch[:, edge + rows :, :] = jnp.zeros((depth, edge, width), jnp.float32)

    def correlate(gains, terms):
        total = gains[0] * terms[0]
        for t in range(1, taps):
            total = total + gains[t] * terms[t]
        return total

    def along_x(source, gains, z):
        for k in range(rows // 16):
            halved = []
            for half in range(2):
                first = edge - rim + 16 * k + 8 * half
                halved.append(correlate(gains, [source[z, pl.ds(first + t, 8), :] for t in range(taps)]))
            high, low = halves(jnp.concatenate(halved, axis=0))
            at = pl.ds(pl.multiple_of(z * rows + 16 * k, 16), 16)
            left[at, :width] = high
            left[at, width:] = low

    for group in range(count):
        view = group * pl.num_programs(0) + step
        gain_z = [taps_ref[view, 0, t] for t in range(taps)]
        gain_x = [taps_ref[view, 1, t] for t in range(taps)]

        def along_z(k, carry):
            row = pl.multiple_of(k * 8, 8)
            column = [ref[z, pl.ds(row, 8), :] for ref, z in volume]
            for z in range(outer):
                wide[z, pl.ds(row + edge, 8), :] = correlate(gain_z, column[z : z + taps])
            return carry

        lax.fori_loop(0, rows // 8, along_z, 0)

        def forward_x(z, carry):
            along_x(wide, gain_x, z)
            return carry

        lax.fori_loop(0, outer, forward_x, 0)

        product = jnp.dot(left[...], bands_ref[group, 0, 0], preferred_element_type=jnp.float32)
        blurred = (product[:, :width] + product[:, width:]).reshape(outer, rows, width)
        for z in range(outer):
            ratio[z] = windows[group][0, planes * place_ref[1] + z].astype(jnp.float32) / blurred[z]

        def back_z(k, carry):
            row = pl.multiple_of(k * 8, 8)
            column = [ratio[z, pl.ds(row, 8), :] for z in range(outer)]
            for z in range(planes):
                back[z, pl.ds(row + edge, 8), :] = correlate(gain_z[::-1], column[z : z + taps])
            return carry

        lax.fori_loop(0, rows // 8, back_z, 0)

        def back_x(z, carry):
            along_x(back, gain_x[::-1], z)
            return carry

        lax.fori_loop(0, planes, back_x, 0)

        product = jnp.dot(left[: planes * rows, :], bands_ref[group, 0, 1], preferred_element_type=jnp.float32)
        logs[...] += jnp.log(product[:, :width] + product[:, width:]).reshape(logs.shape)

    @pl.when(step == pl.num_programs(0) - 1)
    def _():
        for z in range(planes):
            ref, at = volume[2 * rim + z]
            out_ref[z] = ref[at] * jnp.exp(logs[z] / (count * pl.num_programs(0)))


def update(place, taps, band, windows, volume, planes):
    groups = len(windows)
    count, window, rows, width = windows[0].shape
    outer = planes + taps.shape[2] - 1
    band = band.reshape((groups, count) + band.shape[1:])
    return pl.pallas_call(
        functools.partial(update_kernel, groups),
        grid=(count,),
        out_shape=jax.ShapeDtypeStruct((planes, rows, width), jnp.float32),
        in_specs=[SMEM, SMEM, pl.BlockSpec((groups, 1) + band.shape[2:], lambda v: (0, v, 0, 0, 0))]
        + [pl.BlockSpec((1, window, rows, width), lambda v: (v, 0, 0, 0))] * groups
        + [VMEM] * 3,
        out_specs=VMEM,
        scratch_shapes=[
            pltpu.VMEM((outer, rows + 16, width), jnp.float32),
            pltpu.VMEM((outer * rows, 2 * width), jnp.bfloat16),
            pltpu.VMEM((outer, rows, width), jnp.float32),
            pltpu.VMEM((planes, rows + 16, width), jnp.float32),
            pltpu.VMEM((planes, rows, width), jnp.float32),
        ],
        compiler_params=PARAMS,
    )(place, taps, band, *windows, *volume)


def partner(value, bit, members):
    return lax.ppermute(value, "view", [(i, i ^ bit) for i in range(members)])


def z_rims(own, inner, outer, members, blocks):
    planes = own.shape[0]
    axes = ("view", "vol")
    at = lambda line: (line % members) * blocks + line // members
    total = members * blocks
    before, after = [], []
    for hop in range(inner // planes + 1, -(-outer // planes) + 1):
        near, far = max((hop - 1) * planes, inner), min(hop * planes, outer)
        up = [(at(i), at(i + hop)) for i in range(total - hop)]
        down = [(at(i + hop), at(i)) for i in range(total - hop)]
        before.append(lax.ppermute(own[hop * planes - far : hop * planes - near], axes, up))
        after.append(lax.ppermute(own[near - (hop - 1) * planes : far - (hop - 1) * planes], axes, down))
    join = lambda parts: parts[0] if len(parts) == 1 else jnp.concatenate(parts)
    return join(before[::-1]), join(after)


def per_device(raw_views, weights, offsets, psf_taps):
    views, depth, rows, width = raw_views.shape
    members, blocks = lax.axis_size("view"), lax.axis_size("vol")
    rim = (psf_taps.shape[2] - 1) // 2
    planes = depth // members
    me = lax.axis_index("view")
    place = jnp.stack([me // CORES, me % CORES]).astype(jnp.int32)

    up = [(i, i + 1) for i in range(blocks - 1)]
    down = [(i + 1, i) for i in range(blocks - 1)]
    raw_before = lax.ppermute(raw_views[:, depth - rim :], "vol", up)
    raw_after = lax.ppermute(raw_views[:, :rim], "vol", down)
    all_taps = [psf_taps] + [partner(psf_taps, bit, members) for bit in range(1, members)]
    own, far = resample(place, weights, offsets, raw_before, raw_views, raw_after)
    own, far, all_taps = lax.optimization_barrier((own, far, all_taps))
    far = partner(far, 2, members)
    near = partner(own, 1, members)
    all_taps = jnp.concatenate(all_taps)
    all_taps = all_taps / jnp.sum(all_taps, axis=-1, keepdims=True)
    far, band = lax.optimization_barrier((far, bands(all_taps, width)))
    windows = [own, near, far, partner(far, 1, members)]
    start = sum_views(place, windows, planes, rim)
    before, after = z_rims(start[rim : rim + planes], rim, 2 * rim, members, blocks)
    joined = update(place, all_taps, band, windows, (before, start, after), planes)
    for turn in range(1, ITERS):
        before, after = z_rims(joined, 0, 2 * rim, members, blocks)
        joined = update(place, all_taps, band, windows, (before, joined, after), planes)

    columns = lax.all_to_all(joined, "vol", split_axis=1, concat_axis=0, tiled=True)
    far = partner(columns, 2, members)
    near = partner(columns, 1, members)
    parts = [columns, near, far, partner(far, 1, members)]
    width_x = columns.shape[1]
    result = jnp.zeros((blocks, members, planes, width_x, width), jnp.float32)
    for k in range(members):
        piece = parts[k].reshape(blocks, 1, planes, width_x, width)
        result = lax.dynamic_update_slice(result, piece, (0, me ^ k, 0, 0, 0))
    return result.reshape(blocks * depth, width_x, width)


def solution(mesh):
    placed = (
        P("view", "vol", None, None),
        P("view", None, None),
        P("view", None),
        P("view", None, None),
    )
    return jax.shard_map(
        per_device, mesh=mesh, in_specs=placed, out_specs=P(None, "vol", None), check_vma=False
    )
```

```python
import functools

import jax
import jax.numpy as jnp
from jax import lax
from jax.experimental import pallas as pl
from jax.experimental.pallas import tpu as pltpu
from jax.sharding import PartitionSpec as P

ITERS = 2
CORES = 2
VMEM = pl.BlockSpec(memory_space=pltpu.VMEM)
SMEM = pl.BlockSpec(memory_space=pltpu.SMEM)
PARAMS = pltpu.CompilerParams(vmem_limit_bytes=48 * 1024 * 1024)


def halves(value):
    high = value.astype(jnp.bfloat16)
    low = (value - high.astype(jnp.float32)).astype(jnp.bfloat16)
    return high, low


def resample_kernel(place_ref, weights_ref, offsets_ref, *refs):
    sources, (own_ref, far_ref, wide) = refs[:-3], refs[-3:]
    weights = weights_ref[0]
    band, rows = weights.shape
    width = wide.shape[2]
    weights = weights / jnp.sum(weights, axis=0, keepdims=True)
    first = offsets_ref[0]
    source = lax.broadcasted_iota(jnp.int32, (rows, rows), 0)
    matrix = jnp.zeros((rows, rows), jnp.float32)
    for k in range(band):
        matrix = jnp.where(source == first + k, weights[k : k + 1, :], matrix)
    matrix = matrix.T
    high = matrix.astype(jnp.bfloat16)
    rest = matrix - high.astype(jnp.float32)
    middle = rest.astype(jnp.bfloat16)
    low = (rest - middle.astype(jnp.float32)).astype(jnp.bfloat16)
    left = jnp.concatenate([high, middle, low], axis=1)

    def four_planes(ref, base, first_z):
        for pair in range(2):
            z = first_z + pair * 2
            planes = jnp.concatenate([ref[0, z], ref[0, z + 1]], axis=1)
            planes = jnp.concatenate([planes, planes, planes], axis=0)
            total = jnp.dot(left, planes, preferred_element_type=jnp.float32).astype(jnp.bfloat16)
            wide[base + z] = total[:, :width]
            wide[base + z + 1] = total[:, width:]

    base = 0
    for ref in sources:
        depth = ref.shape[1]
        if depth % 8:
            for z in range(0, depth, 4):
                four_planes(ref, base, z)
        else:

            def eight_planes(step, carry, ref=ref, base=base):
                four_planes(ref, base, step * 8)
                four_planes(ref, base, step * 8 + 4)
                return carry

            lax.fori_loop(0, depth // 8, eight_planes, 0)
        base += depth
    chip = place_ref[0]
    count = own_ref.shape[1]
    step = base - count
    for z in range(count):
        own_ref[0, z] = wide[step * chip + z]
        far_ref[0, z] = wide[step * (1 - chip) + z]


def resample(place, weights, offsets, sources, count):
    views, _, rows, width = sources[0].shape
    band = weights.shape[2]
    depths = [source.shape[1] for source in sources]
    block = lambda planes: pl.BlockSpec((1, planes, rows, width), lambda v: (v, 0, 0, 0))
    shape = jax.ShapeDtypeStruct((views, count, rows, width), jnp.bfloat16)
    return pl.pallas_call(
        resample_kernel,
        grid=(views,),
        out_shape=(shape, shape),
        in_specs=[
            SMEM,
            pl.BlockSpec((1, band, rows), lambda v: (v, 0, 0)),
            pl.BlockSpec((1, 1, rows), lambda v: (v, 0, 0)),
        ]
        + [block(depth) for depth in depths],
        out_specs=(block(count), block(count)),
        scratch_shapes=[pltpu.VMEM((sum(depths), rows, width), jnp.bfloat16)],
        compiler_params=PARAMS,
    )(place, weights.transpose(0, 2, 1), offsets[:, None, :], *sources)


def bands_kernel(taps_ref, out_ref):
    view = pl.program_id(0)
    count = taps_ref.shape[2]
    width = out_ref.shape[2] // 2
    shape = (width, width)
    shift = lax.broadcasted_iota(jnp.int32, shape, 0) - lax.broadcasted_iota(jnp.int32, shape, 1)
    for way in range(2):
        band = jnp.zeros(shape, jnp.float32)
        for t in range(count):
            at = t - count // 2
            band = jnp.where(shift == (-at if way else at), taps_ref[view, 2, t], band)
        high, low = halves(band)
        out_ref[0, way, :width, :width] = high
        out_ref[0, way, width:, :width] = high
        out_ref[0, way, :width, width:] = low
        out_ref[0, way, width:, width:] = jnp.zeros_like(low)


def bands(taps, width):
    views = taps.shape[0]
    return pl.pallas_call(
        bands_kernel,
        grid=(views,),
        out_shape=jax.ShapeDtypeStruct((views, 2, 2 * width, 2 * width), jnp.bfloat16),
        in_specs=[SMEM],
        out_specs=pl.BlockSpec((1, 2, 2 * width, 2 * width), lambda v: (v, 0, 0, 0)),
        compiler_params=PARAMS,
    )(taps)


def window_plane(place_ref, main_ref, rim_ref, planes, z):
    chip, core = place_ref[0], place_ref[1]
    rim, main = rim_ref.shape[1], main_ref.shape[1]
    at = planes * core + z
    inside = jnp.clip(at - rim * (1 - chip), 0, main - 1)
    value = main_ref[0, inside].astype(jnp.float32)
    if rim <= z < rim + planes:
        return value
    edge = at - main * chip
    outside = (edge >= 0) & (edge < rim)
    other = rim_ref[0, jnp.clip(edge, 0, rim - 1)].astype(jnp.float32)
    return jnp.where(outside, other, value)


def start_kernel(views, planes, place_ref, *refs):
    count = len(refs) // 2
    windows, start_ref = list(zip(refs[:count], refs[count:-1])), refs[-1]
    step = pl.program_id(0)
    for z in range(start_ref.shape[0]):
        total = window_plane(place_ref, *windows[0], planes, z)
        for window in windows[1:]:
            total = total + window_plane(place_ref, *window, planes, z)

        @pl.when(step == 0)
        def _():
            start_ref[z] = total

        @pl.when(step > 0)
        def _():
            start_ref[z] += total

    @pl.when(step == pl.num_programs(0) - 1)
    def _():
        start_ref[...] = start_ref[...] / views


def window_specs(mains, rims):
    return [pl.BlockSpec((1,) + part.shape[1:], lambda v: (v, 0, 0, 0)) for part in mains + rims]


def sum_views(place, mains, rims, planes):
    count, _, rows, width = mains[0].shape
    rim = rims[0].shape[1]
    return pl.pallas_call(
        functools.partial(start_kernel, len(mains) * count, planes),
        grid=(count,),
        out_shape=jax.ShapeDtypeStruct((planes + 2 * rim, rows, width), jnp.float32),
        in_specs=[SMEM] + window_specs(mains, rims),
        out_specs=VMEM,
        compiler_params=PARAMS,
    )(place, *mains, *rims)


def update_kernel(count, place_ref, taps_ref, *refs):
    bands_ref, windows = refs[0], list(zip(refs[1 : 1 + count], refs[1 + count : 1 + 2 * count]))
    parts = refs[1 + 2 * count : 4 + 2 * count]
    out_ref, wide, left, ratio, back, logs = refs[4 + 2 * count :]
    step = pl.program_id(0)
    taps = taps_ref.shape[2]
    rim = taps // 2
    planes, rows, width = out_ref.shape
    outer = planes + 2 * rim
    edge = 8
    volume = [(ref, z) for ref in parts for z in range(ref.shape[0])]

    @pl.when(step == 0)
    def _():
        logs[...] = jnp.zeros_like(logs)
        for scratch in (wide, back):
            depth = scratch.shape[0]
            scratch[:, :edge, :] = jnp.zeros((depth, edge, width), jnp.float32)
            scratch[:, edge + rows :, :] = jnp.zeros((depth, edge, width), jnp.float32)

    def correlate(gains, terms):
        total = gains[0] * terms[0]
        for t in range(1, taps):
            total = total + gains[t] * terms[t]
        return total

    def along_x(source, gains, z):
        for k in range(rows // 16):
            halved = []
            for half in range(2):
                first = edge - rim + 16 * k + 8 * half
                halved.append(correlate(gains, [source[z, pl.ds(first + t, 8), :] for t in range(taps)]))
            high, low = halves(jnp.concatenate(halved, axis=0))
            at = pl.ds(pl.multiple_of(z * rows + 16 * k, 16), 16)
            left[at, :width] = high
            left[at, width:] = low

    for group in range(count):
        view = group * pl.num_programs(0) + step
        gain_z = [taps_ref[view, 0, t] for t in range(taps)]
        gain_x = [taps_ref[view, 1, t] for t in range(taps)]

        def along_z(k, carry):
            row = pl.multiple_of(k * 8, 8)
            column = [ref[z, pl.ds(row, 8), :] for ref, z in volume]
            for z in range(outer):
                wide[z, pl.ds(row + edge, 8), :] = correlate(gain_z, column[z : z + taps])
            return carry

        lax.fori_loop(0, rows // 8, along_z, 0)

        def forward_x(z, carry):
            along_x(wide, gain_x, z)
            return carry

        lax.fori_loop(0, outer, forward_x, 0)

        product = jnp.dot(left[...], bands_ref[group, 0, 0], preferred_element_type=jnp.float32)
        blurred = (product[:, :width] + product[:, width:]).reshape(outer, rows, width)
        for z in range(outer):
            ratio[z] = window_plane(place_ref, *windows[group], planes, z) / blurred[z]

        def back_z(k, carry):
            row = pl.multiple_of(k * 8, 8)
            column = [ratio[z, pl.ds(row, 8), :] for z in range(outer)]
            for z in range(planes):
                back[z, pl.ds(row + edge, 8), :] = correlate(gain_z[::-1], column[z : z + taps])
            return carry

        lax.fori_loop(0, rows // 8, back_z, 0)

        def back_x(z, carry):
            along_x(back, gain_x[::-1], z)
            return carry

        lax.fori_loop(0, planes, back_x, 0)

        product = jnp.dot(left[: planes * rows, :], bands_ref[group, 0, 1], preferred_element_type=jnp.float32)
        logs[...] += jnp.log(product[:, :width] + product[:, width:]).reshape(logs.shape)

    @pl.when(step == pl.num_programs(0) - 1)
    def _():
        for z in range(planes):
            ref, at = volume[2 * rim + z]
            out_ref[z] = ref[at] * jnp.exp(logs[z] / (count * pl.num_programs(0)))


def update(place, taps, band, mains, rims, volume, planes):
    groups = len(mains)
    count, _, rows, width = mains[0].shape
    outer = planes + taps.shape[2] - 1
    band = band.reshape((groups, count) + band.shape[1:])
    return pl.pallas_call(
        functools.partial(update_kernel, groups),
        grid=(count,),
        out_shape=jax.ShapeDtypeStruct((planes, rows, width), jnp.float32),
        in_specs=[SMEM, SMEM, pl.BlockSpec((groups, 1) + band.shape[2:], lambda v: (0, v, 0, 0, 0))]
        + window_specs(mains, rims)
        + [VMEM] * 3,
        out_specs=VMEM,
        scratch_shapes=[
            pltpu.VMEM((outer, rows + 16, width), jnp.float32),
            pltpu.VMEM((outer * rows, 2 * width), jnp.bfloat16),
            pltpu.VMEM((outer, rows, width), jnp.float32),
            pltpu.VMEM((planes, rows + 16, width), jnp.float32),
            pltpu.VMEM((planes, rows, width), jnp.float32),
        ],
        compiler_params=PARAMS,
    )(place, taps, band, *mains, *rims, *volume)


def partner(value, bit, members):
    return lax.ppermute(value, "view", [(i, i ^ bit) for i in range(members)])


def z_rims(own, inner, outer, members, blocks):
    planes = own.shape[0]
    axes = ("view", "vol")
    at = lambda line: (line % members) * blocks + line // members
    total = members * blocks
    before, after = [], []
    for hop in range(inner // planes + 1, -(-outer // planes) + 1):
        near, far = max((hop - 1) * planes, inner), min(hop * planes, outer)
        up = [(at(i), at(i + hop)) for i in range(total - hop)]
        down = [(at(i + hop), at(i)) for i in range(total - hop)]
        before.append(lax.ppermute(own[hop * planes - far : hop * planes - near], axes, up))
        after.append(lax.ppermute(own[near - (hop - 1) * planes : far - (hop - 1) * planes], axes, down))
    join = lambda parts: parts[0] if len(parts) == 1 else jnp.concatenate(parts)
    return join(before[::-1]), join(after)


def per_device(raw_views, weights, offsets, psf_taps):
    views, depth, rows, width = raw_views.shape
    members, blocks = lax.axis_size("view"), lax.axis_size("vol")
    rim = (psf_taps.shape[2] - 1) // 2
    planes = depth // members
    me = lax.axis_index("view")
    place = jnp.stack([me // CORES, me % CORES]).astype(jnp.int32)

    near_bit, far_bit = 1, CORES
    own_main, far_main = resample(place, weights, offsets, [raw_views], 2 * planes + rim)
    own_main, far_main, raw_later, taps_later = lax.optimization_barrier((own_main, far_main, raw_views, psf_taps))
    far_main = partner(far_main, far_bit, members)
    up = [(i, i + 1) for i in range(blocks - 1)]
    down = [(i + 1, i) for i in range(blocks - 1)]
    raw_before = lax.ppermute(raw_later[:, depth - rim :], "vol", up)
    raw_after = lax.ppermute(raw_later[:, :rim], "vol", down)
    near_main = partner(own_main, near_bit, members)
    cross_taps = partner(taps_later, near_bit + far_bit, members)
    pair_taps = partner(jnp.stack([psf_taps, cross_taps]), near_bit, members)
    all_taps = jnp.concatenate([psf_taps, pair_taps[0], pair_taps[1], cross_taps])
    all_taps = all_taps / jnp.sum(all_taps, axis=-1, keepdims=True)
    band = bands(all_taps, width)
    own_rim, far_rim = resample(place, weights, offsets, [raw_before, raw_after], rim)
    cross_rim = partner(far_rim, near_bit + far_bit, members)
    near_rim = partner(own_rim, near_bit, members)
    far_main, band, own_rim = lax.optimization_barrier((far_main, band, own_rim))
    far_rim = partner(cross_rim, near_bit, members)
    mains = [own_main, near_main, far_main, partner(far_main, near_bit, members)]
    rims = [own_rim, near_rim, far_rim, cross_rim]
    start = sum_views(place, mains, rims, planes)
    before, after = z_rims(start[rim : rim + planes], rim, 2 * rim, members, blocks)
    joined = update(place, all_taps, band, mains, rims, (before, start, after), planes)
    for turn in range(1, ITERS):
        before, after = z_rims(joined, 0, 2 * rim, members, blocks)
        joined = update(place, all_taps, band, mains, rims, (before, joined, after), planes)

    columns = lax.all_to_all(joined, "vol", split_axis=1, concat_axis=0, tiled=True)
    far = partner(columns, far_bit, members)
    near = partner(columns, near_bit, members)
    parts = [columns, near, far, partner(far, near_bit, members)]
    width_x = columns.shape[1]
    result = jnp.zeros((blocks, members, planes, width_x, width), jnp.float32)
    for k in range(members):
        piece = parts[k].reshape(blocks, 1, planes, width_x, width)
        result = lax.dynamic_update_slice(result, piece, (0, me ^ k, 0, 0, 0))
    return result.reshape(blocks * depth, width_x, width)


def solution(mesh):
    placed = (
        P("view", "vol", None, None),
        P("view", None, None),
        P("view", None),
        P("view", None, None),
    )
    return jax.shard_map(
        per_device, mesh=mesh, in_specs=placed, out_specs=P(None, "vol", None), check_vma=False
    )
```

```python
import functools

import jax
import jax.numpy as jnp
from jax import lax
from jax.experimental import pallas as pl
from jax.experimental.pallas import tpu as pltpu
from jax.sharding import PartitionSpec as P

ITERS = 2
CORES = 2
VMEM = pl.BlockSpec(memory_space=pltpu.VMEM)
SMEM = pl.BlockSpec(memory_space=pltpu.SMEM)
PARAMS = pltpu.CompilerParams(vmem_limit_bytes=48 * 1024 * 1024)


def halves(value):
    high = value.astype(jnp.bfloat16)
    low = (value - high.astype(jnp.float32)).astype(jnp.bfloat16)
    return high, low


def resample_kernel(place_ref, weights_ref, offsets_ref, *refs):
    sources, (own_ref, far_ref, wide) = refs[:-3], refs[-3:]
    weights = weights_ref[0]
    band, rows = weights.shape
    width = wide.shape[2]
    weights = weights / jnp.sum(weights, axis=0, keepdims=True)
    first = offsets_ref[0]
    source = lax.broadcasted_iota(jnp.int32, (rows, rows), 0)
    matrix = jnp.zeros((rows, rows), jnp.float32)
    for k in range(band):
        matrix = jnp.where(source == first + k, weights[k : k + 1, :], matrix)
    matrix = matrix.T
    high = matrix.astype(jnp.bfloat16)
    rest = matrix - high.astype(jnp.float32)
    middle = rest.astype(jnp.bfloat16)
    low = (rest - middle.astype(jnp.float32)).astype(jnp.bfloat16)
    left = jnp.concatenate([high, middle, low], axis=1)

    def four_planes(ref, base, first_z):
        for pair in range(2):
            z = first_z + pair * 2
            planes = jnp.concatenate([ref[0, z], ref[0, z + 1]], axis=1)
            planes = jnp.concatenate([planes, planes, planes], axis=0)
            total = jnp.dot(left, planes, preferred_element_type=jnp.float32).astype(jnp.bfloat16)
            wide[base + z] = total[:, :width]
            wide[base + z + 1] = total[:, width:]

    base = 0
    for ref in sources:
        depth = ref.shape[1]
        if depth % 8:
            for z in range(0, depth, 4):
                four_planes(ref, base, z)
        else:

            def eight_planes(step, carry, ref=ref, base=base):
                four_planes(ref, base, step * 8)
                four_planes(ref, base, step * 8 + 4)
                return carry

            lax.fori_loop(0, depth // 8, eight_planes, 0)
        base += depth
    chip = place_ref[0]
    count = own_ref.shape[1]
    step = base - count
    for z in range(count):
        own_ref[0, z] = wide[step * chip + z]
        far_ref[0, z] = wide[step * (1 - chip) + z]


def resample(place, weights, offsets, sources, count):
    views, _, rows, width = sources[0].shape
    band = weights.shape[2]
    depths = [source.shape[1] for source in sources]
    block = lambda planes: pl.BlockSpec((1, planes, rows, width), lambda v: (v, 0, 0, 0))
    shape = jax.ShapeDtypeStruct((views, count, rows, width), jnp.bfloat16)
    return pl.pallas_call(
        resample_kernel,
        grid=(views,),
        out_shape=(shape, shape),
        in_specs=[
            SMEM,
            pl.BlockSpec((1, band, rows), lambda v: (v, 0, 0)),
            pl.BlockSpec((1, 1, rows), lambda v: (v, 0, 0)),
        ]
        + [block(depth) for depth in depths],
        out_specs=(block(count), block(count)),
        scratch_shapes=[pltpu.VMEM((sum(depths), rows, width), jnp.bfloat16)],
        compiler_params=PARAMS,
    )(place, weights.transpose(0, 2, 1), offsets[:, None, :], *sources)


def bands_kernel(taps_ref, out_ref):
    view = pl.program_id(0)
    count = taps_ref.shape[2]
    width = out_ref.shape[2] // 2
    shape = (width, width)
    shift = lax.broadcasted_iota(jnp.int32, shape, 0) - lax.broadcasted_iota(jnp.int32, shape, 1)
    for way in range(2):
        band = jnp.zeros(shape, jnp.float32)
        for t in range(count):
            at = t - count // 2
            band = jnp.where(shift == (-at if way else at), taps_ref[view, 2, t], band)
        high, low = halves(band)
        out_ref[0, way, :width, :width] = high
        out_ref[0, way, width:, :width] = high
        out_ref[0, way, :width, width:] = low
        out_ref[0, way, width:, width:] = jnp.zeros_like(low)


def bands(taps, width):
    views = taps.shape[0]
    return pl.pallas_call(
        bands_kernel,
        grid=(views,),
        out_shape=jax.ShapeDtypeStruct((views, 2, 2 * width, 2 * width), jnp.bfloat16),
        in_specs=[SMEM],
        out_specs=pl.BlockSpec((1, 2, 2 * width, 2 * width), lambda v: (v, 0, 0, 0)),
        compiler_params=PARAMS,
    )(taps)


def window_plane(place_ref, main_ref, rim_ref, planes, z):
    chip, core = place_ref[0], place_ref[1]
    rim, main = rim_ref.shape[1], main_ref.shape[1]
    at = planes * core + z
    inside = jnp.clip(at - rim * (1 - chip), 0, main - 1)
    value = main_ref[0, inside].astype(jnp.float32)
    if rim <= z < rim + planes:
        return value
    edge = at - main * chip
    outside = (edge >= 0) & (edge < rim)
    other = rim_ref[0, jnp.clip(edge, 0, rim - 1)].astype(jnp.float32)
    return jnp.where(outside, other, value)


def start_kernel(views, planes, place_ref, *refs):
    count = len(refs) // 2
    windows, start_ref = list(zip(refs[:count], refs[count:-1])), refs[-1]
    step = pl.program_id(0)
    for z in range(start_ref.shape[0]):
        total = window_plane(place_ref, *windows[0], planes, z)
        for window in windows[1:]:
            total = total + window_plane(place_ref, *window, planes, z)

        @pl.when(step == 0)
        def _():
            start_ref[z] = total

        @pl.when(step > 0)
        def _():
            start_ref[z] += total

    @pl.when(step == pl.num_programs(0) - 1)
    def _():
        start_ref[...] = start_ref[...] / views


def window_specs(mains, rims):
    return [pl.BlockSpec((1,) + part.shape[1:], lambda v: (v, 0, 0, 0)) for part in mains + rims]


def sum_views(place, mains, rims, planes):
    count, _, rows, width = mains[0].shape
    rim = rims[0].shape[1]
    return pl.pallas_call(
        functools.partial(start_kernel, len(mains) * count, planes),
        grid=(count,),
        out_shape=jax.ShapeDtypeStruct((planes + 2 * rim, rows, width), jnp.float32),
        in_specs=[SMEM] + window_specs(mains, rims),
        out_specs=VMEM,
        compiler_params=PARAMS,
    )(place, *mains, *rims)


def update_kernel(count, place_ref, taps_ref, *refs):
    bands_ref, windows = refs[0], list(zip(refs[1 : 1 + count], refs[1 + count : 1 + 2 * count]))
    parts = refs[1 + 2 * count : 4 + 2 * count]
    out_ref, wide, left, ratio, back, logs = refs[4 + 2 * count :]
    step = pl.program_id(0)
    taps = taps_ref.shape[2]
    rim = taps // 2
    planes, rows, width = out_ref.shape
    outer = planes + 2 * rim
    edge = 8
    volume = [(ref, z) for ref in parts for z in range(ref.shape[0])]

    @pl.when(step == 0)
    def _():
        logs[...] = jnp.zeros_like(logs)
        for scratch in (wide, back):
            depth = scratch.shape[0]
            scratch[:, :edge, :] = jnp.zeros((depth, edge, width), jnp.float32)
            scratch[:, edge + rows :, :] = jnp.zeros((depth, edge, width), jnp.float32)

    def correlate(gains, terms):
        total = gains[0] * terms[0]
        for t in range(1, taps):
            total = total + gains[t] * terms[t]
        return total

    def along_x(source, gains, z):
        for k in range(rows // 16):
            halved = []
            for half in range(2):
                first = edge - rim + 16 * k + 8 * half
                halved.append(correlate(gains, [source[z, pl.ds(first + t, 8), :] for t in range(taps)]))
            high, low = halves(jnp.concatenate(halved, axis=0))
            at = pl.ds(pl.multiple_of(z * rows + 16 * k, 16), 16)
            left[at, :width] = high
            left[at, width:] = low

    for group in range(count):
        view = group * pl.num_programs(0) + step
        gain_z = [taps_ref[view, 0, t] for t in range(taps)]
        gain_x = [taps_ref[view, 1, t] for t in range(taps)]

        def along_z(k, carry):
            row = pl.multiple_of(k * 8, 8)
            column = [ref[z, pl.ds(row, 8), :] for ref, z in volume]
            for z in range(outer):
                wide[z, pl.ds(row + edge, 8), :] = correlate(gain_z, column[z : z + taps])
            return carry

        lax.fori_loop(0, rows // 8, along_z, 0)

        def forward_x(z, carry):
            along_x(wide, gain_x, z)
            return carry

        lax.fori_loop(0, outer, forward_x, 0)

        product = jnp.dot(left[...], bands_ref[group, 0, 0], preferred_element_type=jnp.float32)
        blurred = (product[:, :width] + product[:, width:]).reshape(outer, rows, width)
        for z in range(outer):
            ratio[z] = window_plane(place_ref, *windows[group], planes, z) / blurred[z]

        def back_z(k, carry):
            row = pl.multiple_of(k * 8, 8)
            column = [ratio[z, pl.ds(row, 8), :] for z in range(outer)]
            for z in range(planes):
                back[z, pl.ds(row + edge, 8), :] = correlate(gain_z[::-1], column[z : z + taps])
            return carry

        lax.fori_loop(0, rows // 8, back_z, 0)

        def back_x(z, carry):
            along_x(back, gain_x[::-1], z)
            return carry

        lax.fori_loop(0, planes, back_x, 0)

        product = jnp.dot(left[: planes * rows, :], bands_ref[group, 0, 1], preferred_element_type=jnp.float32)
        logs[...] += jnp.log(product[:, :width] + product[:, width:]).reshape(logs.shape)

    @pl.when(step == pl.num_programs(0) - 1)
    def _():
        for z in range(planes):
            ref, at = volume[2 * rim + z]
            out_ref[z] = ref[at] * jnp.exp(logs[z] / (count * pl.num_programs(0)))


def update(place, taps, band, mains, rims, volume, planes):
    groups = len(mains)
    count, _, rows, width = mains[0].shape
    outer = planes + taps.shape[2] - 1
    band = band.reshape((groups, count) + band.shape[1:])
    return pl.pallas_call(
        functools.partial(update_kernel, groups),
        grid=(count,),
        out_shape=jax.ShapeDtypeStruct((planes, rows, width), jnp.float32),
        in_specs=[SMEM, SMEM, pl.BlockSpec((groups, 1) + band.shape[2:], lambda v: (0, v, 0, 0, 0))]
        + window_specs(mains, rims)
        + [VMEM] * 3,
        out_specs=VMEM,
        scratch_shapes=[
            pltpu.VMEM((outer, rows + 16, width), jnp.float32),
            pltpu.VMEM((outer * rows, 2 * width), jnp.bfloat16),
            pltpu.VMEM((outer, rows, width), jnp.float32),
            pltpu.VMEM((planes, rows + 16, width), jnp.float32),
            pltpu.VMEM((planes, rows, width), jnp.float32),
        ],
        compiler_params=PARAMS,
    )(place, taps, band, *mains, *rims, *volume)


def partner(value, bit, members):
    return lax.ppermute(value, "view", [(i, i ^ bit) for i in range(members)])


def z_rims(own, inner, outer, members, blocks):
    planes = own.shape[0]
    axes = ("view", "vol")
    at = lambda line: (line % members) * blocks + line // members
    total = members * blocks
    before, after = [], []
    for hop in range(inner // planes + 1, -(-outer // planes) + 1):
        near, far = max((hop - 1) * planes, inner), min(hop * planes, outer)
        up = [(at(i), at(i + hop)) for i in range(total - hop)]
        down = [(at(i + hop), at(i)) for i in range(total - hop)]
        before.append(lax.ppermute(own[hop * planes - far : hop * planes - near], axes, up))
        after.append(lax.ppermute(own[near - (hop - 1) * planes : far - (hop - 1) * planes], axes, down))
    join = lambda parts: parts[0] if len(parts) == 1 else jnp.concatenate(parts)
    return join(before[::-1]), join(after)


def per_device(raw_views, weights, offsets, psf_taps):
    views, depth, rows, width = raw_views.shape
    members, blocks = lax.axis_size("view"), lax.axis_size("vol")
    rim = (psf_taps.shape[2] - 1) // 2
    planes = depth // members
    me = lax.axis_index("view")
    place = jnp.stack([me // CORES, me % CORES]).astype(jnp.int32)

    near_bit, far_bit = 1, CORES
    cross_taps = partner(psf_taps, near_bit + far_bit, members)
    own_main, far_main = resample(place, weights, offsets, [raw_views], 2 * planes + rim)
    own_main, far_main, raw_later, cross_taps = lax.optimization_barrier(
        (own_main, far_main, raw_views, cross_taps)
    )
    far_main = partner(far_main, far_bit, members)
    up = [(i, i + 1) for i in range(blocks - 1)]
    down = [(i + 1, i) for i in range(blocks - 1)]
    raw_before = lax.ppermute(raw_later[:, depth - rim :], "vol", up)
    raw_after = lax.ppermute(raw_later[:, :rim], "vol", down)
    near_main = partner(own_main, near_bit, members)
    pair_taps = partner(jnp.stack([psf_taps, cross_taps]), near_bit, members)
    all_taps = jnp.concatenate([psf_taps, pair_taps[0], pair_taps[1], cross_taps])
    all_taps = all_taps / jnp.sum(all_taps, axis=-1, keepdims=True)
    band = bands(all_taps, width)
    own_rim, far_rim = resample(place, weights, offsets, [raw_before, raw_after], rim)
    cross_rim = partner(far_rim, near_bit + far_bit, members)
    near_rim = partner(own_rim, near_bit, members)
    far_main, band, own_rim = lax.optimization_barrier((far_main, band, own_rim))
    far_rim = partner(cross_rim, near_bit, members)
    mains = [own_main, near_main, far_main, partner(far_main, near_bit, members)]
    rims = [own_rim, near_rim, far_rim, cross_rim]
    start = sum_views(place, mains, rims, planes)
    before, after = z_rims(start[rim : rim + planes], rim, 2 * rim, members, blocks)
    joined = update(place, all_taps, band, mains, rims, (before, start, after), planes)
    for turn in range(1, ITERS):
        before, after = z_rims(joined, 0, 2 * rim, members, blocks)
        joined = update(place, all_taps, band, mains, rims, (before, joined, after), planes)

    columns = lax.all_to_all(joined, "vol", split_axis=1, concat_axis=0, tiled=True)
    far = partner(columns, far_bit, members)
    near = partner(columns, near_bit, members)
    parts = [columns, near, far, partner(far, near_bit, members)]
    width_x = columns.shape[1]
    result = jnp.zeros((blocks, members, planes, width_x, width), jnp.float32)
    for k in range(members):
        piece = parts[k].reshape(blocks, 1, planes, width_x, width)
        result = lax.dynamic_update_slice(result, piece, (0, me ^ k, 0, 0, 0))
    return result.reshape(blocks * depth, width_x, width)


def solution(mesh):
    placed = (
        P("view", "vol", None, None),
        P("view", None, None),
        P("view", None),
        P("view", None, None),
    )
    return jax.shard_map(
        per_device, mesh=mesh, in_specs=placed, out_specs=P(None, "vol", None), check_vma=False
    )
```

```python
import functools

import jax
import jax.numpy as jnp
from jax import lax
from jax.experimental import pallas as pl
from jax.experimental.pallas import tpu as pltpu
from jax.sharding import PartitionSpec as P

ITERS = 2
CORES = 2
VMEM = pl.BlockSpec(memory_space=pltpu.VMEM)
SMEM = pl.BlockSpec(memory_space=pltpu.SMEM)
PARAMS = pltpu.CompilerParams(vmem_limit_bytes=48 * 1024 * 1024)


def halves(value):
    high = value.astype(jnp.bfloat16)
    low = (value - high.astype(jnp.float32)).astype(jnp.bfloat16)
    return high, low


def resample_kernel(place_ref, weights_ref, offsets_ref, *refs):
    sources, (own_ref, far_ref, wide) = refs[:-3], refs[-3:]
    weights = weights_ref[0]
    band, rows = weights.shape
    width = wide.shape[2]
    weights = weights / jnp.sum(weights, axis=0, keepdims=True)
    first = offsets_ref[0]
    source = lax.broadcasted_iota(jnp.int32, (rows, rows), 0)
    matrix = jnp.zeros((rows, rows), jnp.float32)
    for k in range(band):
        matrix = jnp.where(source == first + k, weights[k : k + 1, :], matrix)
    matrix = matrix.T
    high = matrix.astype(jnp.bfloat16)
    rest = matrix - high.astype(jnp.float32)
    middle = rest.astype(jnp.bfloat16)
    low = (rest - middle.astype(jnp.float32)).astype(jnp.bfloat16)
    left = jnp.concatenate([high, middle, low], axis=1)

    def four_planes(ref, base, first_z):
        for pair in range(2):
            z = first_z + pair * 2
            planes = jnp.concatenate([ref[0, z], ref[0, z + 1]], axis=1)
            planes = jnp.concatenate([planes, planes, planes], axis=0)
            total = jnp.dot(left, planes, preferred_element_type=jnp.float32).astype(jnp.bfloat16)
            wide[base + z] = total[:, :width]
            wide[base + z + 1] = total[:, width:]

    base = 0
    for ref in sources:
        depth = ref.shape[1]
        if depth % 8:
            for z in range(0, depth, 4):
                four_planes(ref, base, z)
        else:

            def eight_planes(step, carry, ref=ref, base=base):
                four_planes(ref, base, step * 8)
                four_planes(ref, base, step * 8 + 4)
                return carry

            lax.fori_loop(0, depth // 8, eight_planes, 0)
        base += depth
    chip = place_ref[0]
    count = own_ref.shape[1]
    step = base - count
    for z in range(count):
        own_ref[0, z] = wide[step * chip + z]
        far_ref[0, z] = wide[step * (1 - chip) + z]


def resample(place, weights, offsets, sources, count):
    views, _, rows, width = sources[0].shape
    band = weights.shape[2]
    depths = [source.shape[1] for source in sources]
    block = lambda planes: pl.BlockSpec((1, planes, rows, width), lambda v: (v, 0, 0, 0))
    shape = jax.ShapeDtypeStruct((views, count, rows, width), jnp.bfloat16)
    return pl.pallas_call(
        resample_kernel,
        grid=(views,),
        out_shape=(shape, shape),
        in_specs=[
            SMEM,
            pl.BlockSpec((1, band, rows), lambda v: (v, 0, 0)),
            pl.BlockSpec((1, 1, rows), lambda v: (v, 0, 0)),
        ]
        + [block(depth) for depth in depths],
        out_specs=(block(count), block(count)),
        scratch_shapes=[pltpu.VMEM((sum(depths), rows, width), jnp.bfloat16)],
        compiler_params=PARAMS,
    )(place, weights.transpose(0, 2, 1), offsets[:, None, :], *sources)


def bands_kernel(taps_ref, out_ref):
    view = pl.program_id(0)
    count = taps_ref.shape[2]
    width = out_ref.shape[2] // 2
    shape = (width, width)
    shift = lax.broadcasted_iota(jnp.int32, shape, 0) - lax.broadcasted_iota(jnp.int32, shape, 1)
    for way in range(2):
        band = jnp.zeros(shape, jnp.float32)
        for t in range(count):
            at = t - count // 2
            band = jnp.where(shift == (-at if way else at), taps_ref[view, 2, t], band)
        high, low = halves(band)
        out_ref[0, way, :width, :width] = high
        out_ref[0, way, width:, :width] = high
        out_ref[0, way, :width, width:] = low
        out_ref[0, way, width:, width:] = jnp.zeros_like(low)


def bands(taps, width):
    views = taps.shape[0]
    return pl.pallas_call(
        bands_kernel,
        grid=(views,),
        out_shape=jax.ShapeDtypeStruct((views, 2, 2 * width, 2 * width), jnp.bfloat16),
        in_specs=[SMEM],
        out_specs=pl.BlockSpec((1, 2, 2 * width, 2 * width), lambda v: (v, 0, 0, 0)),
        compiler_params=PARAMS,
    )(taps)


def window_plane(place_ref, main_ref, rim_ref, planes, z):
    chip, core = place_ref[0], place_ref[1]
    rim, main = rim_ref.shape[1], main_ref.shape[1]
    at = planes * core + z
    inside = jnp.clip(at - rim * (1 - chip), 0, main - 1)
    value = main_ref[0, inside].astype(jnp.float32)
    if rim <= z < rim + planes:
        return value
    edge = at - main * chip
    outside = (edge >= 0) & (edge < rim)
    other = rim_ref[0, jnp.clip(edge, 0, rim - 1)].astype(jnp.float32)
    return jnp.where(outside, other, value)


def start_kernel(views, planes, place_ref, *refs):
    count = len(refs) // 2
    windows, start_ref = list(zip(refs[:count], refs[count:-1])), refs[-1]
    step = pl.program_id(0)
    for z in range(start_ref.shape[0]):
        total = window_plane(place_ref, *windows[0], planes, z)
        for window in windows[1:]:
            total = total + window_plane(place_ref, *window, planes, z)

        @pl.when(step == 0)
        def _():
            start_ref[z] = total

        @pl.when(step > 0)
        def _():
            start_ref[z] += total

    @pl.when(step == pl.num_programs(0) - 1)
    def _():
        start_ref[...] = start_ref[...] / views


def window_specs(mains, rims):
    return [pl.BlockSpec((1,) + part.shape[1:], lambda v: (v, 0, 0, 0)) for part in mains + rims]


def sum_views(place, mains, rims, planes):
    count, _, rows, width = mains[0].shape
    rim = rims[0].shape[1]
    return pl.pallas_call(
        functools.partial(start_kernel, len(mains) * count, planes),
        grid=(count,),
        out_shape=jax.ShapeDtypeStruct((planes + 2 * rim, rows, width), jnp.float32),
        in_specs=[SMEM] + window_specs(mains, rims),
        out_specs=VMEM,
        compiler_params=PARAMS,
    )(place, *mains, *rims)


def update_kernel(count, place_ref, taps_ref, *refs):
    bands_ref, windows = refs[0], list(zip(refs[1 : 1 + count], refs[1 + count : 1 + 2 * count]))
    parts = refs[1 + 2 * count : 4 + 2 * count]
    out_ref, wides, lefts, ratios, backs, logs = refs[4 + 2 * count :]
    step = pl.program_id(0)
    taps = taps_ref.shape[2]
    rim = taps // 2
    planes, rows, width = out_ref.shape
    outer = planes + 2 * rim
    edge = 8
    volume = [(ref, z) for ref in parts for z in range(ref.shape[0])]

    @pl.when(step == 0)
    def _():
        logs[...] = jnp.zeros_like(logs)
        for scratch in (wides, backs):
            zeros = jnp.zeros(scratch.shape[:2] + (edge, width), jnp.float32)
            scratch[:, :, :edge, :] = zeros
            scratch[:, :, edge + rows :, :] = zeros

    def correlate(gains, terms):
        total = gains[0] * terms[0]
        for t in range(1, taps):
            total = total + gains[t] * terms[t]
        return total

    def along_x(source, left, gains, z):
        for k in range(rows // 16):
            halved = []
            for half in range(2):
                first = edge - rim + 16 * k + 8 * half
                halved.append(correlate(gains, [source[z, pl.ds(first + t, 8), :] for t in range(taps)]))
            high, low = halves(jnp.concatenate(halved, axis=0))
            at = pl.ds(z * rows + 16 * k, 16)
            left[at, :width] = high
            left[at, width:] = low

    held = None
    for group in range(count):
        view = group * pl.num_programs(0) + step
        wide, left, ratio, back = (scratch.at[group % 2] for scratch in (wides, lefts, ratios, backs))
        gain_z = [taps_ref[view, 0, t] for t in range(taps)]
        gain_x = [taps_ref[view, 1, t] for t in range(taps)]
        for k in range(rows // 8):
            column = [ref[z, pl.ds(k * 8, 8), :] for ref, z in volume]
            for z in range(outer):
                wide[z, pl.ds(k * 8 + edge, 8), :] = correlate(gain_z, column[z : z + taps])
        for z in range(outer):
            along_x(wide, left, gain_x, z)
        product = jnp.dot(left[...], bands_ref[group, 0, 0], preferred_element_type=jnp.float32)
        blurred = (product[:, :width] + product[:, width:]).reshape(outer, rows, width)
        for z in range(outer):
            ratio[z] = window_plane(place_ref, *windows[group], planes, z) / blurred[z]
        for k in range(rows // 8):
            column = [ratio[z, pl.ds(k * 8, 8), :] for z in range(outer)]
            for z in range(planes):
                back[z, pl.ds(k * 8 + edge, 8), :] = correlate(gain_z[::-1], column[z : z + taps])
        for z in range(planes):
            along_x(back, left, gain_x[::-1], z)
        product = jnp.dot(left[: planes * rows, :], bands_ref[group, 0, 1], preferred_element_type=jnp.float32)
        total = (product[:, :width] + product[:, width:]).reshape(logs.shape)
        if group % 2 == 0:
            held = total
        else:
            logs[...] += jnp.log(held * total)

    @pl.when(step == pl.num_programs(0) - 1)
    def _():
        for z in range(planes):
            ref, at = volume[2 * rim + z]
            out_ref[z] = ref[at] * jnp.exp(logs[z] / (count * pl.num_programs(0)))


def update(place, taps, band, mains, rims, volume, planes):
    groups = len(mains)
    count, _, rows, width = mains[0].shape
    outer = planes + taps.shape[2] - 1
    band = band.reshape((groups, count) + band.shape[1:])
    return pl.pallas_call(
        functools.partial(update_kernel, groups),
        grid=(count,),
        out_shape=jax.ShapeDtypeStruct((planes, rows, width), jnp.float32),
        in_specs=[SMEM, SMEM, pl.BlockSpec((groups, 1) + band.shape[2:], lambda v: (0, v, 0, 0, 0))]
        + window_specs(mains, rims)
        + [VMEM] * 3,
        out_specs=VMEM,
        scratch_shapes=[
            pltpu.VMEM((2, outer, rows + 16, width), jnp.float32),
            pltpu.VMEM((2, outer * rows, 2 * width), jnp.bfloat16),
            pltpu.VMEM((2, outer, rows, width), jnp.float32),
            pltpu.VMEM((2, planes, rows + 16, width), jnp.float32),
            pltpu.VMEM((planes, rows, width), jnp.float32),
        ],
        compiler_params=PARAMS,
    )(place, taps, band, *mains, *rims, *volume)


def partner(value, bit, members):
    return lax.ppermute(value, "view", [(i, i ^ bit) for i in range(members)])


def z_rims(own, inner, outer, members, blocks):
    planes = own.shape[0]
    axes = ("view", "vol")
    at = lambda line: (line % members) * blocks + line // members
    total = members * blocks
    before, after = [], []
    for hop in range(inner // planes + 1, -(-outer // planes) + 1):
        near, far = max((hop - 1) * planes, inner), min(hop * planes, outer)
        up = [(at(i), at(i + hop)) for i in range(total - hop)]
        down = [(at(i + hop), at(i)) for i in range(total - hop)]
        before.append(lax.ppermute(own[hop * planes - far : hop * planes - near], axes, up))
        after.append(lax.ppermute(own[near - (hop - 1) * planes : far - (hop - 1) * planes], axes, down))
    join = lambda parts: parts[0] if len(parts) == 1 else jnp.concatenate(parts)
    return join(before[::-1]), join(after)


def per_device(raw_views, weights, offsets, psf_taps):
    views, depth, rows, width = raw_views.shape
    members, blocks = lax.axis_size("view"), lax.axis_size("vol")
    rim = (psf_taps.shape[2] - 1) // 2
    planes = depth // members
    me = lax.axis_index("view")
    place = jnp.stack([me // CORES, me % CORES]).astype(jnp.int32)

    near_bit, far_bit = 1, CORES
    cross_taps = partner(psf_taps, near_bit + far_bit, members)
    own_main, far_main = resample(place, weights, offsets, [raw_views], 2 * planes + rim)
    own_main, far_main, raw_later, cross_taps = lax.optimization_barrier(
        (own_main, far_main, raw_views, cross_taps)
    )
    far_main = partner(far_main, far_bit, members)
    up = [(i, i + 1) for i in range(blocks - 1)]
    down = [(i + 1, i) for i in range(blocks - 1)]
    raw_before = lax.ppermute(raw_later[:, depth - rim :], "vol", up)
    raw_after = lax.ppermute(raw_later[:, :rim], "vol", down)
    near_main = partner(own_main, near_bit, members)
    pair_taps = partner(jnp.stack([psf_taps, cross_taps]), near_bit, members)
    all_taps = jnp.concatenate([psf_taps, pair_taps[0], pair_taps[1], cross_taps])
    all_taps = all_taps / jnp.sum(all_taps, axis=-1, keepdims=True)
    band = bands(all_taps, width)
    own_rim, far_rim = resample(place, weights, offsets, [raw_before, raw_after], rim)
    cross_rim = partner(far_rim, near_bit + far_bit, members)
    near_rim = partner(own_rim, near_bit, members)
    far_main, band, own_rim = lax.optimization_barrier((far_main, band, own_rim))
    far_rim = partner(cross_rim, near_bit, members)
    mains = [own_main, near_main, far_main, partner(far_main, near_bit, members)]
    rims = [own_rim, near_rim, far_rim, cross_rim]
    start = sum_views(place, mains, rims, planes)
    before, after = z_rims(start[rim : rim + planes], rim, 2 * rim, members, blocks)
    joined = update(place, all_taps, band, mains, rims, (before, start, after), planes)
    for turn in range(1, ITERS):
        before, after = z_rims(joined, 0, 2 * rim, members, blocks)
        joined = update(place, all_taps, band, mains, rims, (before, joined, after), planes)

    columns = lax.all_to_all(joined, "vol", split_axis=1, concat_axis=0, tiled=True)
    far = partner(columns, far_bit, members)
    near = partner(columns, near_bit, members)
    parts = [columns, near, far, partner(far, near_bit, members)]
    width_x = columns.shape[1]
    result = jnp.zeros((blocks, members, planes, width_x, width), jnp.float32)
    for k in range(members):
        piece = parts[k].reshape(blocks, 1, planes, width_x, width)
        result = lax.dynamic_update_slice(result, piece, (0, me ^ k, 0, 0, 0))
    return result.reshape(blocks * depth, width_x, width)


def solution(mesh):
    placed = (
        P("view", "vol", None, None),
        P("view", None, None),
        P("view", None),
        P("view", None, None),
    )
    return jax.shard_map(
        per_device, mesh=mesh, in_specs=placed, out_specs=P(None, "vol", None), check_vma=False
    )
```

```python
import functools

import jax
import jax.numpy as jnp
from jax import lax
from jax.experimental import pallas as pl
from jax.experimental.pallas import tpu as pltpu
from jax.sharding import PartitionSpec as P

ITERS = 2
CORES = 2
SUBLANES = 8
VMEM = pl.BlockSpec(memory_space=pltpu.VMEM)
SMEM = pl.BlockSpec(memory_space=pltpu.SMEM)
PARAMS = pltpu.CompilerParams(vmem_limit_bytes=48 * 1024 * 1024)


def halves(value):
    high = value.astype(jnp.bfloat16)
    low = (value - high.astype(jnp.float32)).astype(jnp.bfloat16)
    return high, low


def resample_kernel(place_ref, weights_ref, offsets_ref, *refs):
    sources, (own_ref, far_ref, wide) = refs[:-3], refs[-3:]
    weights = weights_ref[0]
    band, rows = weights.shape
    width = wide.shape[2]
    weights = weights / jnp.sum(weights, axis=0, keepdims=True)
    first = offsets_ref[0]
    source = lax.broadcasted_iota(jnp.int32, (rows, rows), 0)
    matrix = jnp.zeros((rows, rows), jnp.float32)
    for k in range(band):
        matrix = jnp.where(source == first + k, weights[k : k + 1, :], matrix)
    matrix = matrix.T
    high = matrix.astype(jnp.bfloat16)
    rest = matrix - high.astype(jnp.float32)
    middle = rest.astype(jnp.bfloat16)
    low = (rest - middle.astype(jnp.float32)).astype(jnp.bfloat16)
    left = jnp.concatenate([high, middle, low], axis=1)
    place = lax.broadcasted_iota(jnp.int32, (rows, rows), 0)
    natural = (place % SUBLANES) * (rows // SUBLANES) + place // SUBLANES
    order = (lax.broadcasted_iota(jnp.int32, (rows, rows), 1) == natural).astype(jnp.bfloat16)
    left = jnp.dot(order, left, preferred_element_type=jnp.float32).astype(jnp.bfloat16)

    def four_planes(ref, base, first_z):
        for pair in range(2):
            z = first_z + pair * 2
            planes = jnp.concatenate([ref[0, z], ref[0, z + 1]], axis=1)
            planes = jnp.concatenate([planes, planes, planes], axis=0)
            total = jnp.dot(left, planes, preferred_element_type=jnp.float32).astype(jnp.bfloat16)
            wide[base + z] = total[:, :width]
            wide[base + z + 1] = total[:, width:]

    base = 0
    for ref in sources:
        depth = ref.shape[1]
        if depth % 8:
            for z in range(0, depth, 4):
                four_planes(ref, base, z)
        else:

            def eight_planes(step, carry, ref=ref, base=base):
                four_planes(ref, base, step * 8)
                four_planes(ref, base, step * 8 + 4)
                return carry

            lax.fori_loop(0, depth // 8, eight_planes, 0)
        base += depth
    chip = place_ref[0]
    count = own_ref.shape[1]
    step = base - count
    for z in range(count):
        own_ref[0, z] = wide[step * chip + z]
        far_ref[0, z] = wide[step * (1 - chip) + z]


def resample(place, weights, offsets, sources, count):
    views, _, rows, width = sources[0].shape
    band = weights.shape[2]
    depths = [source.shape[1] for source in sources]
    block = lambda planes: pl.BlockSpec((1, planes, rows, width), lambda v: (v, 0, 0, 0))
    shape = jax.ShapeDtypeStruct((views, count, rows, width), jnp.bfloat16)
    return pl.pallas_call(
        resample_kernel,
        grid=(views,),
        out_shape=(shape, shape),
        in_specs=[
            SMEM,
            pl.BlockSpec((1, band, rows), lambda v: (v, 0, 0)),
            pl.BlockSpec((1, 1, rows), lambda v: (v, 0, 0)),
        ]
        + [block(depth) for depth in depths],
        out_specs=(block(count), block(count)),
        scratch_shapes=[pltpu.VMEM((sum(depths), rows, width), jnp.bfloat16)],
        compiler_params=PARAMS,
    )(place, weights.transpose(0, 2, 1), offsets[:, None, :], *sources)


def bands_kernel(taps_ref, out_ref):
    view = pl.program_id(0)
    count = taps_ref.shape[2]
    width = out_ref.shape[2] // 2
    shape = (width, width)
    shift = lax.broadcasted_iota(jnp.int32, shape, 0) - lax.broadcasted_iota(jnp.int32, shape, 1)
    for way in range(2):
        band = jnp.zeros(shape, jnp.float32)
        for t in range(count):
            at = t - count // 2
            band = jnp.where(shift == (-at if way else at), taps_ref[view, 2, t], band)
        high, low = halves(band)
        out_ref[0, way, :width, :width] = high
        out_ref[0, way, width:, :width] = high
        out_ref[0, way, :width, width:] = low
        out_ref[0, way, width:, width:] = jnp.zeros_like(low)


def bands(taps, width):
    views = taps.shape[0]
    return pl.pallas_call(
        bands_kernel,
        grid=(views,),
        out_shape=jax.ShapeDtypeStruct((views, 2, 2 * width, 2 * width), jnp.bfloat16),
        in_specs=[SMEM],
        out_specs=pl.BlockSpec((1, 2, 2 * width, 2 * width), lambda v: (v, 0, 0, 0)),
        compiler_params=PARAMS,
    )(taps)


def window_plane(place_ref, main_ref, rim_ref, planes, z):
    chip, core = place_ref[0], place_ref[1]
    rim, main = rim_ref.shape[1], main_ref.shape[1]
    at = planes * core + z
    inside = jnp.clip(at - rim * (1 - chip), 0, main - 1)
    value = main_ref[0, inside].astype(jnp.float32)
    if rim <= z < rim + planes:
        return value
    edge = at - main * chip
    outside = (edge >= 0) & (edge < rim)
    other = rim_ref[0, jnp.clip(edge, 0, rim - 1)].astype(jnp.float32)
    return jnp.where(outside, other, value)


def start_kernel(views, planes, place_ref, *refs):
    count = len(refs) // 2
    windows, start_ref = list(zip(refs[:count], refs[count:-1])), refs[-1]
    step = pl.program_id(0)
    for z in range(start_ref.shape[0]):
        total = window_plane(place_ref, *windows[0], planes, z)
        for window in windows[1:]:
            total = total + window_plane(place_ref, *window, planes, z)

        @pl.when(step == 0)
        def _():
            start_ref[z] = total

        @pl.when(step > 0)
        def _():
            start_ref[z] += total

    @pl.when(step == pl.num_programs(0) - 1)
    def _():
        start_ref[...] = start_ref[...] / views


def window_specs(mains, rims):
    return [pl.BlockSpec((1,) + part.shape[1:], lambda v: (v, 0, 0, 0)) for part in mains + rims]


def sum_views(place, mains, rims, planes):
    count, _, rows, width = mains[0].shape
    rim = rims[0].shape[1]
    return pl.pallas_call(
        functools.partial(start_kernel, len(mains) * count, planes),
        grid=(count,),
        out_shape=jax.ShapeDtypeStruct((planes + 2 * rim, rows, width), jnp.float32),
        in_specs=[SMEM] + window_specs(mains, rims),
        out_specs=VMEM,
        compiler_params=PARAMS,
    )(place, *mains, *rims)


def update_kernel(count, last, place_ref, taps_ref, *refs):
    bands_ref, windows = refs[0], list(zip(refs[1 : 1 + count], refs[1 + count : 1 + 2 * count]))
    parts = refs[1 + 2 * count : 4 + 2 * count]
    out_ref, wides, lefts, ratios, backs, logs = refs[4 + 2 * count :]
    step = pl.program_id(0)
    taps = taps_ref.shape[2]
    rim = taps // 2
    planes, rows, width = out_ref.shape
    outer = planes + 2 * rim
    tiles = rows // SUBLANES
    volume = [(ref, z) for ref in parts for z in range(ref.shape[0])]
    tile = lambda k: pl.ds(k * SUBLANES, SUBLANES)
    sublane = lax.broadcasted_iota(jnp.int32, (SUBLANES, width), 0)

    @pl.when(step == 0)
    def _():
        logs[...] = jnp.zeros_like(logs)

    def correlate(gains, terms):
        total = gains[0] * terms[0]
        for t in range(1, taps):
            total = total + gains[t] * terms[t]
        return total

    def along_z(column, gains, length):
        return [correlate(gains, column[z : z + taps]) for z in range(length)]

    def along_x(source, left, gains, z):
        row = [source[z, tile(k), :] for k in range(tiles)]
        below = [jnp.where(sublane == 0, 0.0, pltpu.roll(part, 1, 0)) for part in row[tiles - rim :]]
        above = [jnp.where(sublane == SUBLANES - 1, 0.0, pltpu.roll(part, SUBLANES - 1, 0)) for part in row[:rim]]
        row = below + row + above
        for k in range(0, tiles, 2):
            pair = [correlate(gains, row[k : k + taps]), correlate(gains, row[k + 1 : k + 1 + taps])]
            high, low = halves(jnp.concatenate(pair, axis=0))
            at = pl.ds(z * rows + k * SUBLANES, 2 * SUBLANES)
            left[at, :width] = high
            left[at, width:] = low

    held = None
    for group in range(count):
        view = group * pl.num_programs(0) + step
        wide, left, ratio, back = (scratch.at[group % 2] for scratch in (wides, lefts, ratios, backs))
        gain_z = [taps_ref[view, 0, t] for t in range(taps)]
        gain_x = [taps_ref[view, 1, t] for t in range(taps)]
        for k in range(tiles):
            column = along_z([ref[z, tile(k), :] for ref, z in volume], gain_z, outer)
            for z in range(outer):
                wide[z, tile(k), :] = column[z]
        for z in range(outer):
            along_x(wide, left, gain_x, z)
        product = jnp.dot(left[...], bands_ref[group, 0, 0], preferred_element_type=jnp.float32)
        blurred = (product[:, :width] + product[:, width:]).reshape(outer, rows, width)
        for z in range(outer):
            ratio[z] = window_plane(place_ref, *windows[group], planes, z) / blurred[z]
        for k in range(tiles):
            column = along_z([ratio[z, tile(k), :] for z in range(outer)], gain_z[::-1], planes)
            for z in range(planes):
                back[z, tile(k), :] = column[z]
        for z in range(planes):
            along_x(back, left, gain_x[::-1], z)
        product = jnp.dot(left[: planes * rows, :], bands_ref[group, 0, 1], preferred_element_type=jnp.float32)
        total = (product[:, :width] + product[:, width:]).reshape(logs.shape)
        if group % 2 == 0:
            held = total
        else:
            logs[...] += jnp.log(held * total)

    @pl.when(step == pl.num_programs(0) - 1)
    def _():
        for z in range(planes):
            ref, at = volume[2 * rim + z]
            for k in range(tiles):
                value = ref[at, tile(k), :] * jnp.exp(logs[z, tile(k), :] / (count * pl.num_programs(0)))
                if last:
                    out_ref[z, pl.ds(k, SUBLANES, tiles), :] = value
                else:
                    out_ref[z, tile(k), :] = value


def update(place, taps, band, mains, rims, volume, planes, last):
    groups = len(mains)
    count, _, rows, width = mains[0].shape
    outer = planes + taps.shape[2] - 1
    band = band.reshape((groups, count) + band.shape[1:])
    return pl.pallas_call(
        functools.partial(update_kernel, groups, last),
        grid=(count,),
        out_shape=jax.ShapeDtypeStruct((planes, rows, width), jnp.float32),
        in_specs=[SMEM, SMEM, pl.BlockSpec((groups, 1) + band.shape[2:], lambda v: (0, v, 0, 0, 0))]
        + window_specs(mains, rims)
        + [VMEM] * 3,
        out_specs=VMEM,
        scratch_shapes=[
            pltpu.VMEM((2, outer, rows, width), jnp.float32),
            pltpu.VMEM((2, outer * rows, 2 * width), jnp.bfloat16),
            pltpu.VMEM((2, outer, rows, width), jnp.float32),
            pltpu.VMEM((2, planes, rows, width), jnp.float32),
            pltpu.VMEM((planes, rows, width), jnp.float32),
        ],
        compiler_params=PARAMS,
    )(place, taps, band, *mains, *rims, *volume)


def partner(value, bit, members):
    return lax.ppermute(value, "view", [(i, i ^ bit) for i in range(members)])


def z_rims(own, inner, outer, members, blocks):
    planes = own.shape[0]
    axes = ("view", "vol")
    at = lambda line: (line % members) * blocks + line // members
    total = members * blocks
    before, after = [], []
    for hop in range(inner // planes + 1, -(-outer // planes) + 1):
        near, far = max((hop - 1) * planes, inner), min(hop * planes, outer)
        up = [(at(i), at(i + hop)) for i in range(total - hop)]
        down = [(at(i + hop), at(i)) for i in range(total - hop)]
        before.append(lax.ppermute(own[hop * planes - far : hop * planes - near], axes, up))
        after.append(lax.ppermute(own[near - (hop - 1) * planes : far - (hop - 1) * planes], axes, down))
    join = lambda parts: parts[0] if len(parts) == 1 else jnp.concatenate(parts)
    return join(before[::-1]), join(after)


def per_device(raw_views, weights, offsets, psf_taps):
    views, depth, rows, width = raw_views.shape
    members, blocks = lax.axis_size("view"), lax.axis_size("vol")
    rim = (psf_taps.shape[2] - 1) // 2
    planes = depth // members
    me = lax.axis_index("view")
    place = jnp.stack([me // CORES, me % CORES]).astype(jnp.int32)

    near_bit, far_bit = 1, CORES
    cross_taps = partner(psf_taps, near_bit + far_bit, members)
    own_main, far_main = resample(place, weights, offsets, [raw_views], 2 * planes + rim)
    own_main, far_main, raw_later, cross_taps = lax.optimization_barrier(
        (own_main, far_main, raw_views, cross_taps)
    )
    far_main = partner(far_main, far_bit, members)
    up = [(i, i + 1) for i in range(blocks - 1)]
    down = [(i + 1, i) for i in range(blocks - 1)]
    raw_before = lax.ppermute(raw_later[:, depth - rim :], "vol", up)
    raw_after = lax.ppermute(raw_later[:, :rim], "vol", down)
    near_main = partner(own_main, near_bit, members)
    pair_taps = partner(jnp.stack([psf_taps, cross_taps]), near_bit, members)
    all_taps = jnp.concatenate([psf_taps, pair_taps[0], pair_taps[1], cross_taps])
    all_taps = all_taps / jnp.sum(all_taps, axis=-1, keepdims=True)
    band = bands(all_taps, width)
    own_rim, far_rim = resample(place, weights, offsets, [raw_before, raw_after], rim)
    cross_rim = partner(far_rim, near_bit + far_bit, members)
    near_rim = partner(own_rim, near_bit, members)
    far_main, band, own_rim = lax.optimization_barrier((far_main, band, own_rim))
    far_rim = partner(cross_rim, near_bit, members)
    mains = [own_main, near_main, far_main, partner(far_main, near_bit, members)]
    rims = [own_rim, near_rim, far_rim, cross_rim]
    start = sum_views(place, mains, rims, planes)
    before, after = z_rims(start[rim : rim + planes], rim, 2 * rim, members, blocks)
    joined = update(place, all_taps, band, mains, rims, (before, start, after), planes, ITERS == 1)
    for turn in range(1, ITERS):
        before, after = z_rims(joined, 0, 2 * rim, members, blocks)
        joined = update(place, all_taps, band, mains, rims, (before, joined, after), planes, turn == ITERS - 1)

    columns = lax.all_to_all(joined, "vol", split_axis=1, concat_axis=0, tiled=True)
    far = partner(columns, far_bit, members)
    near = partner(columns, near_bit, members)
    parts = [columns, near, far, partner(far, near_bit, members)]
    width_x = columns.shape[1]
    result = jnp.zeros((blocks, members, planes, width_x, width), jnp.float32)
    for k in range(members):
        piece = parts[k].reshape(blocks, 1, planes, width_x, width)
        result = lax.dynamic_update_slice(result, piece, (0, me ^ k, 0, 0, 0))
    return result.reshape(blocks * depth, width_x, width)


def solution(mesh):
    placed = (
        P("view", "vol", None, None),
        P("view", None, None),
        P("view", None),
        P("view", None, None),
    )
    return jax.shard_map(
        per_device, mesh=mesh, in_specs=placed, out_specs=P(None, "vol", None), check_vma=False
    )
```

```python
import functools

import jax
import jax.numpy as jnp
from jax import lax
from jax.experimental import pallas as pl
from jax.experimental.pallas import tpu as pltpu
from jax.sharding import PartitionSpec as P

ITERS = 2
CORES = 2
SUBLANES = 8
VMEM = pl.BlockSpec(memory_space=pltpu.VMEM)
SMEM = pl.BlockSpec(memory_space=pltpu.SMEM)
PARAMS = pltpu.CompilerParams(vmem_limit_bytes=48 * 1024 * 1024)


def halves(value):
    high = value.astype(jnp.bfloat16)
    low = (value - high.astype(jnp.float32)).astype(jnp.bfloat16)
    return high, low


def resample_kernel(plan, place_ref, weights_ref, offsets_ref, *refs):
    count = 1 + max(segment[0] for parts in plan for segment in parts[1])
    sources, outs = refs[:count], refs[count:]
    weights = weights_ref[0]
    band, rows = weights.shape
    width = sources[0].shape[3]
    weights = weights / jnp.sum(weights, axis=0, keepdims=True)
    first = offsets_ref[0]
    source = lax.broadcasted_iota(jnp.int32, (rows, rows), 0)
    matrix = jnp.zeros((rows, rows), jnp.float32)
    for k in range(band):
        matrix = jnp.where(source == first + k, weights[k : k + 1, :], matrix)
    matrix = matrix.T
    high = matrix.astype(jnp.bfloat16)
    rest = matrix - high.astype(jnp.float32)
    middle = rest.astype(jnp.bfloat16)
    low = (rest - middle.astype(jnp.float32)).astype(jnp.bfloat16)
    left = jnp.concatenate([high, middle, low], axis=1)
    place = lax.broadcasted_iota(jnp.int32, (rows, rows), 0)
    natural = (place % SUBLANES) * (rows // SUBLANES) + place // SUBLANES
    order = (lax.broadcasted_iota(jnp.int32, (rows, rows), 1) == natural).astype(jnp.bfloat16)
    left = jnp.dot(order, left, preferred_element_type=jnp.float32).astype(jnp.bfloat16)

    for out_ref, (other, segments) in zip(outs, plan):
        half = 1 - place_ref[0] if other else place_ref[0]
        for index, start, target, length in segments:
            start = start[0] + (start[1] - start[0]) * half
            target = target[0] + (target[1] - target[0]) * half
            for z in range(0, length, 2):
                planes = [sources[index][0, start + z + i] for i in range(2)]
                planes = jnp.concatenate(planes, axis=1)
                planes = jnp.concatenate([planes, planes, planes], axis=0)
                total = jnp.dot(left, planes, preferred_element_type=jnp.float32).astype(jnp.bfloat16)
                for i in range(2):
                    out_ref[0, target + z + i] = total[:, i * width : (i + 1) * width]


def resample(place, weights, offsets, sources, plan):
    views, _, rows, width = sources[0].shape
    band = weights.shape[2]
    block = lambda planes: pl.BlockSpec((1, planes, rows, width), lambda v: (v, 0, 0, 0))
    counts = [sum(segment[3] for segment in segments) for _, segments in plan]
    return pl.pallas_call(
        functools.partial(resample_kernel, plan),
        grid=(views,),
        out_shape=[jax.ShapeDtypeStruct((views, count, rows, width), jnp.bfloat16) for count in counts],
        in_specs=[
            SMEM,
            pl.BlockSpec((1, band, rows), lambda v: (v, 0, 0)),
            pl.BlockSpec((1, 1, rows), lambda v: (v, 0, 0)),
        ]
        + [block(source.shape[1]) for source in sources],
        out_specs=[block(count) for count in counts],
        compiler_params=PARAMS,
    )(place, weights.transpose(0, 2, 1), offsets[:, None, :], *sources)


def bands_kernel(taps_ref, out_ref):
    view = pl.program_id(0)
    count = taps_ref.shape[2]
    width = out_ref.shape[2] // 2
    shape = (width, width)
    shift = lax.broadcasted_iota(jnp.int32, shape, 0) - lax.broadcasted_iota(jnp.int32, shape, 1)
    for way in range(2):
        band = jnp.zeros(shape, jnp.float32)
        for t in range(count):
            at = t - count // 2
            band = jnp.where(shift == (-at if way else at), taps_ref[view, 2, t], band)
        high, low = halves(band)
        out_ref[0, way, :width, :width] = high
        out_ref[0, way, width:, :width] = high
        out_ref[0, way, :width, width:] = low
        out_ref[0, way, width:, width:] = jnp.zeros_like(low)


def bands(taps, width):
    views = taps.shape[0]
    return pl.pallas_call(
        bands_kernel,
        grid=(views,),
        out_shape=jax.ShapeDtypeStruct((views, 2, 2 * width, 2 * width), jnp.bfloat16),
        in_specs=[SMEM],
        out_specs=pl.BlockSpec((1, 2, 2 * width, 2 * width), lambda v: (v, 0, 0, 0)),
        compiler_params=PARAMS,
    )(taps)


def gather_kernel(views, planes, rim, place_ref, *refs):
    count = (len(refs) - 3) // 2
    inner, edges = refs[:count], refs[count : 2 * count]
    bricks_ref, start_ref, window = refs[2 * count :]
    step = pl.program_id(0)
    half, core = place_ref[0], place_ref[1]
    main, side = inner[0].shape[1], edges[0].shape[1]

    @pl.when(step == 0)
    def _():
        start_ref[...] = jnp.zeros_like(start_ref)

    for group in range(count):
        for z in range(main):
            window[group, side * (1 - half) + z] = inner[group][0, z]
        for z in range(side):
            window[group, main * half + z] = edges[group][0, z]
    for z in range(planes + 2 * rim):
        total = start_ref[z]
        for group in range(count):
            plane = window[group, planes * core + z]
            bricks_ref[group, 0, z] = plane
            total = total + plane.astype(jnp.float32)
        start_ref[z] = total

    @pl.when(step == pl.num_programs(0) - 1)
    def _():
        start_ref[...] = start_ref[...] / views


def gather_views(place, inner, edges, planes, rim):
    groups = len(inner)
    count, main, rows, width = inner[0].shape
    outer, side = planes + 2 * rim, edges[0].shape[1]
    return pl.pallas_call(
        functools.partial(gather_kernel, groups * count, planes, rim),
        grid=(count,),
        out_shape=[
            jax.ShapeDtypeStruct((groups, count, outer, rows, width), jnp.bfloat16),
            jax.ShapeDtypeStruct((outer, rows, width), jnp.float32),
        ],
        in_specs=[SMEM] + [pl.BlockSpec((1,) + part.shape[1:], lambda v: (v, 0, 0, 0)) for part in inner + edges],
        out_specs=[pl.BlockSpec((groups, 1, outer, rows, width), lambda v: (0, v, 0, 0, 0)), VMEM],
        scratch_shapes=[pltpu.VMEM((groups, main + side, rows, width), jnp.bfloat16)],
        compiler_params=PARAMS,
    )(place, *inner, *edges)


def update_kernel(last, taps_ref, bands_ref, bricks_ref, before_ref, own_ref, after_ref, out_ref, *scratches):
    wides, lefts, ratios, backs, logs = scratches
    parts = (before_ref, own_ref, after_ref)
    count = bricks_ref.shape[0]
    step = pl.program_id(0)
    taps = taps_ref.shape[2]
    rim = taps // 2
    planes, rows, width = out_ref.shape
    outer = planes + 2 * rim
    tiles = rows // SUBLANES
    volume = [(ref, z) for ref in parts for z in range(ref.shape[0])]
    tile = lambda k: pl.ds(k * SUBLANES, SUBLANES)
    sublane = lax.broadcasted_iota(jnp.int32, (SUBLANES, width), 0)

    @pl.when(step == 0)
    def _():
        logs[...] = jnp.zeros_like(logs)

    def correlate(gains, terms):
        total = gains[0] * terms[0]
        for t in range(1, taps):
            total = total + gains[t] * terms[t]
        return total

    def along_z(column, gains, length):
        return [correlate(gains, column[z : z + taps]) for z in range(length)]

    def along_x(source, left, gains, z):
        row = [source[z, tile(k), :] for k in range(tiles)]
        below = [jnp.where(sublane == 0, 0.0, pltpu.roll(part, 1, 0)) for part in row[tiles - rim :]]
        above = [jnp.where(sublane == SUBLANES - 1, 0.0, pltpu.roll(part, SUBLANES - 1, 0)) for part in row[:rim]]
        row = below + row + above
        for k in range(0, tiles, 2):
            pair = [correlate(gains, row[k : k + taps]), correlate(gains, row[k + 1 : k + 1 + taps])]
            high, low = halves(jnp.concatenate(pair, axis=0))
            at = pl.ds(z * rows + k * SUBLANES, 2 * SUBLANES)
            left[at, :width] = high
            left[at, width:] = low

    held = None
    for group in range(count):
        view = group * pl.num_programs(0) + step
        wide, left, ratio, back = (scratch.at[group % 2] for scratch in (wides, lefts, ratios, backs))
        gain_z = [taps_ref[view, 0, t] for t in range(taps)]
        gain_x = [taps_ref[view, 1, t] for t in range(taps)]
        for k in range(tiles):
            column = along_z([ref[z, tile(k), :] for ref, z in volume], gain_z, outer)
            for z in range(outer):
                wide[z, tile(k), :] = column[z]
        for z in range(outer):
            along_x(wide, left, gain_x, z)
        product = jnp.dot(left[...], bands_ref[group, 0, 0], preferred_element_type=jnp.float32)
        blurred = (product[:, :width] + product[:, width:]).reshape(outer, rows, width)
        for z in range(outer):
            guess = pl.reciprocal(blurred[z], approx=True)
            guess = guess * (2.0 - blurred[z] * guess)
            ratio[z] = bricks_ref[group, 0, z].astype(jnp.float32) * guess
        for k in range(tiles):
            column = along_z([ratio[z, tile(k), :] for z in range(outer)], gain_z[::-1], planes)
            for z in range(planes):
                back[z, tile(k), :] = column[z]
        for z in range(planes):
            along_x(back, left, gain_x[::-1], z)
        product = jnp.dot(left[: planes * rows, :], bands_ref[group, 0, 1], preferred_element_type=jnp.float32)
        total = (product[:, :width] + product[:, width:]).reshape(logs.shape)
        if group % 2 == 0:
            held = total
        else:
            logs[...] += jnp.log(held * total)

    @pl.when(step == pl.num_programs(0) - 1)
    def _():
        for z in range(planes):
            ref, at = volume[2 * rim + z]
            for k in range(tiles):
                value = ref[at, tile(k), :] * jnp.exp(logs[z, tile(k), :] / (count * pl.num_programs(0)))
                if last:
                    out_ref[z, pl.ds(k, SUBLANES, tiles), :] = value
                else:
                    out_ref[z, tile(k), :] = value


def update(taps, band, bricks, volume, planes, last):
    groups, count, outer, rows, width = bricks.shape
    band = band.reshape((groups, count) + band.shape[1:])
    step = lambda v: (0, v, 0, 0, 0)
    return pl.pallas_call(
        functools.partial(update_kernel, last),
        grid=(count,),
        out_shape=jax.ShapeDtypeStruct((planes, rows, width), jnp.float32),
        in_specs=[
            SMEM,
            pl.BlockSpec((groups, 1) + band.shape[2:], step),
            pl.BlockSpec((groups, 1, outer, rows, width), step),
            VMEM,
            VMEM,
            VMEM,
        ],
        out_specs=VMEM,
        scratch_shapes=[
            pltpu.VMEM((2, outer, rows, width), jnp.float32),
            pltpu.VMEM((2, outer * rows, 2 * width), jnp.bfloat16),
            pltpu.VMEM((2, outer, rows, width), jnp.float32),
            pltpu.VMEM((2, planes, rows, width), jnp.float32),
            pltpu.VMEM((planes, rows, width), jnp.float32),
        ],
        compiler_params=PARAMS,
    )(taps, band, bricks, *volume)


def place_kernel(planes, place_ref, *refs):
    parts, out_ref = refs[:-1], refs[-1]
    blocks, members = out_ref.shape[:2]
    slot = place_ref[0]
    for index, part in enumerate(parts):
        for block in range(blocks):
            at = slot ^ index
            at = members - 1 - at if block % 2 else at
            out_ref[block, at] = part[block * planes : (block + 1) * planes]


def place_parts(slot, parts, planes):
    depth, rows, width = parts[0].shape
    return pl.pallas_call(
        functools.partial(place_kernel, planes),
        out_shape=jax.ShapeDtypeStruct((depth // planes, len(parts), planes, rows, width), jnp.float32),
        in_specs=[SMEM] + [VMEM] * len(parts),
        out_specs=VMEM,
        compiler_params=PARAMS,
    )(slot, *parts)


def partner(value, bit, members):
    return lax.ppermute(value, "view", [(i, i ^ bit) for i in range(members)])


def z_rims(own, inner, outer, members, blocks):
    planes = own.shape[0]
    axes = ("view", "vol")
    def at(line):
        block, slab = divmod(line, members)
        return (members - 1 - slab if block % 2 else slab) * blocks + block

    total = members * blocks
    before, after = [], []
    for hop in range(inner // planes + 1, -(-outer // planes) + 1):
        near, far = max((hop - 1) * planes, inner), min(hop * planes, outer)
        up = [(at(i), at(i + hop)) for i in range(total - hop)]
        down = [(at(i + hop), at(i)) for i in range(total - hop)]
        before.append(lax.ppermute(own[hop * planes - far : hop * planes - near], axes, up))
        after.append(lax.ppermute(own[near - (hop - 1) * planes : far - (hop - 1) * planes], axes, down))
    join = lambda parts: parts[0] if len(parts) == 1 else jnp.concatenate(parts)
    return join(before[::-1]), join(after)


def per_device(raw_views, weights, offsets, psf_taps):
    views, depth, rows, width = raw_views.shape
    members, blocks = lax.axis_size("view"), lax.axis_size("vol")
    rim = (psf_taps.shape[2] - 1) // 2
    planes = depth // members
    me = lax.axis_index("view")
    odd = lax.axis_index("vol") % 2
    slab = jnp.where(odd == 1, members - 1 - me, me)
    place = jnp.stack([slab // CORES, slab % CORES]).astype(jnp.int32)

    near_bit, far_bit = 1, CORES
    inner = (0, (rim, 2 * planes - rim), (0, 0), 2 * planes)
    first_edge = (0, (0, depth - rim), (rim, 0), rim)
    second_edge = (1, (0, rim), (0, rim), rim)
    cross_taps = partner(psf_taps, near_bit + far_bit, members)
    (far_inner,) = resample(place, weights, offsets, [raw_views], [(True, [inner])])
    far_inner, raw_later, cross_taps = lax.optimization_barrier((far_inner, raw_views, cross_taps))
    far_inner = partner(far_inner, far_bit, members)
    up = [(i, i + 1) for i in range(blocks - 1)]
    down = [(i + 1, i) for i in range(blocks - 1)]
    raw_before = lax.ppermute(raw_later[:, depth - rim :], "vol", up)
    raw_after = lax.ppermute(raw_later[:, :rim], "vol", down)
    (own_inner,) = resample(place, weights, offsets, [raw_later], [(False, [inner])])
    near_inner = partner(own_inner, near_bit, members)
    pair_taps = partner(jnp.stack([psf_taps, cross_taps]), near_bit, members)
    all_taps = jnp.concatenate([psf_taps, pair_taps[0], pair_taps[1], cross_taps])
    all_taps = all_taps / jnp.sum(all_taps, axis=-1, keepdims=True)
    band = bands(all_taps, width)
    raw_rims = jnp.concatenate([raw_before, raw_after], axis=1)
    edge = [first_edge, second_edge]
    far_edge, own_edge = resample(place, weights, offsets, [raw_later, raw_rims], [(True, edge), (False, edge)])
    far_edge = partner(far_edge, far_bit, members)
    near_edge = partner(own_edge, near_bit, members)
    far_edge, band, own_edge = lax.optimization_barrier((far_edge, band, own_edge))
    inners = [own_inner, near_inner, far_inner, partner(far_inner, near_bit, members)]
    edges = [own_edge, near_edge, far_edge, partner(far_edge, near_bit, members)]
    bricks, start = gather_views(place, inners, edges, planes, rim)
    before, after = z_rims(start[rim : rim + planes], rim, 2 * rim, members, blocks)
    joined = update(all_taps, band, bricks, (before, start, after), planes, ITERS == 1)
    for turn in range(1, ITERS):
        before, after = z_rims(joined, 0, 2 * rim, members, blocks)
        joined = update(all_taps, band, bricks, (before, joined, after), planes, turn == ITERS - 1)

    columns = lax.all_to_all(joined, "vol", split_axis=1, concat_axis=0, tiled=True)
    far = partner(columns, far_bit, members)
    near = partner(columns, near_bit, members)
    parts = [columns, near, far, partner(far, near_bit, members)]
    result = place_parts(me.reshape(1).astype(jnp.int32), parts, planes)
    return result.reshape((blocks * depth,) + columns.shape[1:])


def solution(mesh):
    placed = (
        P("view", "vol", None, None),
        P("view", None, None),
        P("view", None),
        P("view", None, None),
    )
    return jax.shard_map(
        per_device, mesh=mesh, in_specs=placed, out_specs=P(None, "vol", None), check_vma=False
    )
```

```python
import functools

import jax
import jax.numpy as jnp
from jax import lax
from jax.experimental import pallas as pl
from jax.experimental.pallas import tpu as pltpu
from jax.sharding import PartitionSpec as P

ITERS = 2
CORES = 2
SUBLANES = 8
VMEM = pl.BlockSpec(memory_space=pltpu.VMEM)
SMEM = pl.BlockSpec(memory_space=pltpu.SMEM)
PARAMS = pltpu.CompilerParams(vmem_limit_bytes=48 * 1024 * 1024)


def halves(value):
    high = value.astype(jnp.bfloat16)
    low = (value - high.astype(jnp.float32)).astype(jnp.bfloat16)
    return high, low


def resample_kernel(plan, place_ref, weights_ref, offsets_ref, *refs):
    count = 1 + max(segment[0] for parts in plan for segment in parts[1])
    sources, outs = refs[:count], refs[count:]
    weights = weights_ref[0]
    band, rows = weights.shape
    width = sources[0].shape[3]
    weights = weights / jnp.sum(weights, axis=0, keepdims=True)
    first = offsets_ref[0]
    source = lax.broadcasted_iota(jnp.int32, (rows, rows), 0)
    matrix = jnp.zeros((rows, rows), jnp.float32)
    for k in range(band):
        matrix = jnp.where(source == first + k, weights[k : k + 1, :], matrix)
    matrix = matrix.T
    high = matrix.astype(jnp.bfloat16)
    rest = matrix - high.astype(jnp.float32)
    middle = rest.astype(jnp.bfloat16)
    low = (rest - middle.astype(jnp.float32)).astype(jnp.bfloat16)
    left = jnp.concatenate([high, middle, low], axis=1)
    place = lax.broadcasted_iota(jnp.int32, (rows, rows), 0)
    natural = (place % SUBLANES) * (rows // SUBLANES) + place // SUBLANES
    order = (lax.broadcasted_iota(jnp.int32, (rows, rows), 1) == natural).astype(jnp.bfloat16)
    left = jnp.dot(order, left, preferred_element_type=jnp.float32).astype(jnp.bfloat16)

    for out_ref, (other, segments) in zip(outs, plan):
        half = 1 - place_ref[0] if other else place_ref[0]
        for index, start, target, length in segments:
            start = start[0] + (start[1] - start[0]) * half
            target = target[0] + (target[1] - target[0]) * half
            for z in range(0, length, 2):
                planes = [sources[index][0, start + z + i] for i in range(2)]
                planes = jnp.concatenate(planes, axis=1)
                planes = jnp.concatenate([planes, planes, planes], axis=0)
                total = jnp.dot(left, planes, preferred_element_type=jnp.float32).astype(jnp.bfloat16)
                for i in range(2):
                    out_ref[0, target + z + i] = total[:, i * width : (i + 1) * width]


def resample(place, weights, offsets, sources, plan):
    views, _, rows, width = sources[0].shape
    band = weights.shape[2]
    block = lambda planes: pl.BlockSpec((1, planes, rows, width), lambda v: (v, 0, 0, 0))
    counts = [sum(segment[3] for segment in segments) for _, segments in plan]
    return pl.pallas_call(
        functools.partial(resample_kernel, plan),
        grid=(views,),
        out_shape=[jax.ShapeDtypeStruct((views, count, rows, width), jnp.bfloat16) for count in counts],
        in_specs=[
            SMEM,
            pl.BlockSpec((1, band, rows), lambda v: (v, 0, 0)),
            pl.BlockSpec((1, 1, rows), lambda v: (v, 0, 0)),
        ]
        + [block(source.shape[1]) for source in sources],
        out_specs=[block(count) for count in counts],
        compiler_params=PARAMS,
    )(place, weights.transpose(0, 2, 1), offsets[:, None, :], *sources)


def bands_kernel(taps_ref, out_ref):
    view = pl.program_id(0)
    count = taps_ref.shape[2]
    width = out_ref.shape[2] // 2
    shape = (width, width)
    shift = lax.broadcasted_iota(jnp.int32, shape, 0) - lax.broadcasted_iota(jnp.int32, shape, 1)
    for way in range(2):
        band = jnp.zeros(shape, jnp.float32)
        for t in range(count):
            at = t - count // 2
            band = jnp.where(shift == (-at if way else at), taps_ref[view, 2, t], band)
        high, low = halves(band)
        out_ref[0, way, :width, :width] = high
        out_ref[0, way, width:, :width] = high
        out_ref[0, way, :width, width:] = low
        out_ref[0, way, width:, width:] = jnp.zeros_like(low)


def bands(taps, width):
    views = taps.shape[0]
    return pl.pallas_call(
        bands_kernel,
        grid=(views,),
        out_shape=jax.ShapeDtypeStruct((views, 2, 2 * width, 2 * width), jnp.bfloat16),
        in_specs=[SMEM],
        out_specs=pl.BlockSpec((1, 2, 2 * width, 2 * width), lambda v: (v, 0, 0, 0)),
        compiler_params=PARAMS,
    )(taps)


def gather_kernel(views, planes, rim, place_ref, *refs):
    partial_ref = None
    if views is not None:
        partial_ref, refs = refs[0], refs[1:]
    groups = 2
    inner, bound, edge = refs[:groups], refs[groups : 2 * groups], refs[2 * groups : 3 * groups]
    bricks_ref, start_ref = refs[3 * groups : 3 * groups + 2]
    window = refs[-1]
    step = pl.program_id(0)
    half, core = place_ref[0], place_ref[1]
    main = inner[0].shape[1]

    @pl.when(step == 0)
    def _():
        start_ref[...] = jnp.zeros_like(start_ref) if partial_ref is None else partial_ref[...]

    for group in range(groups):
        for z in range(main):
            window[group, 2 * rim * (1 - half) + z] = inner[group][0, z]
        for z in range(rim):
            window[group, rim + (main - rim) * half + z] = bound[group][0, z]
            window[group, (main + rim) * half + z] = edge[group][0, z]
    for z in range(planes + 2 * rim):
        total = start_ref[z]
        for group in range(groups):
            plane = window[group, planes * core + z]
            bricks_ref[group, 0, z] = plane
            total = total + plane.astype(jnp.float32)
        start_ref[z] = total

    if views is not None:
        near_ref, cross_ref = refs[3 * groups + 2 : 3 * groups + 4]

        @pl.when(step == pl.num_programs(0) - 1)
        def _():
            start_ref[...] = start_ref[...] / views
            for z in range(rim):
                upward, downward = rim + planes - 2 * rim + z, 2 * rim + z
                near_ref[z] = start_ref[upward + (downward - upward) * core]
                cross_ref[z] = start_ref[downward + (upward - downward) * core]


def gather_views(place, inner, bound, edge, planes, views=None, partial=None):
    groups = len(inner)
    count, main, rows, width = inner[0].shape
    rim = edge[0].shape[1]
    outer = planes + 2 * rim
    field = lambda depth: jax.ShapeDtypeStruct((depth, rows, width), jnp.float32)
    sends = [] if views is None else [field(rim), field(rim)]
    parts = [*inner, *bound, *edge]
    return pl.pallas_call(
        functools.partial(gather_kernel, views, planes, rim),
        grid=(count,),
        out_shape=[jax.ShapeDtypeStruct((groups, count, outer, rows, width), jnp.bfloat16), field(outer)] + sends,
        in_specs=[SMEM]
        + ([] if partial is None else [VMEM])
        + [pl.BlockSpec((1,) + part.shape[1:], lambda v: (v, 0, 0, 0)) for part in parts],
        out_specs=[pl.BlockSpec((groups, 1, outer, rows, width), lambda v: (0, v, 0, 0, 0))]
        + [VMEM] * (1 + len(sends)),
        scratch_shapes=[pltpu.VMEM((groups, main + 2 * rim, rows, width), jnp.bfloat16)],
        compiler_params=PARAMS,
    )(place, *([] if partial is None else [partial]), *parts)


def update_kernel(last, paired, place_ref, taps_ref, bands_ref, *refs):
    bricks_refs, (first_ref, own_ref, second_ref, out_ref) = refs[:2], refs[2:6]
    volume, wides, lefts, ratios, backs, logs = refs[6:]
    bricks = [ref.at[group] for ref in bricks_refs for group in range(ref.shape[0])]
    count = len(bricks)
    step = pl.program_id(0)
    taps = taps_ref.shape[2]
    rim = taps // 2
    planes, rows, width = out_ref.shape
    outer = planes + 2 * rim
    tiles = rows // SUBLANES
    tile = lambda k: pl.ds(k * SUBLANES, SUBLANES)
    sublane = lax.broadcasted_iota(jnp.int32, (SUBLANES, width), 0)

    @pl.when(step == 0)
    def _():
        logs[...] = jnp.zeros_like(logs)
        side, middle = first_ref.shape[0], own_ref.shape[0]
        flip = 1 - place_ref[1] if paired else 0
        for z in range(side):
            volume[(side + middle) * flip + z] = first_ref[z]
            volume[(side + middle) * (1 - flip) + z] = second_ref[z]
        for z in range(middle):
            volume[side + z] = own_ref[z]

    def correlate(gains, terms):
        total = gains[0] * terms[0]
        for t in range(1, taps):
            total = total + gains[t] * terms[t]
        return total

    def along_z(column, gains, length):
        return [correlate(gains, column[z : z + taps]) for z in range(length)]

    def along_x(source, left, gains, z):
        row = [source[z, tile(k), :] for k in range(tiles)]
        below = [jnp.where(sublane == 0, 0.0, pltpu.roll(part, 1, 0)) for part in row[tiles - rim :]]
        above = [jnp.where(sublane == SUBLANES - 1, 0.0, pltpu.roll(part, SUBLANES - 1, 0)) for part in row[:rim]]
        row = below + row + above
        for k in range(0, tiles, 2):
            pair = [correlate(gains, row[k : k + taps]), correlate(gains, row[k + 1 : k + 1 + taps])]
            high, low = halves(jnp.concatenate(pair, axis=0))
            at = pl.ds(z * rows + k * SUBLANES, 2 * SUBLANES)
            left[at, :width] = high
            left[at, width:] = low

    held = None
    for group in range(count):
        view = group * pl.num_programs(0) + step
        wide, left, ratio, back = (scratch.at[group % 2] for scratch in (wides, lefts, ratios, backs))
        gain_z = [taps_ref[view, 0, t] for t in range(taps)]
        gain_x = [taps_ref[view, 1, t] for t in range(taps)]
        for k in range(tiles):
            column = along_z([volume[z, tile(k), :] for z in range(outer + 2 * rim)], gain_z, outer)
            for z in range(outer):
                wide[z, tile(k), :] = column[z]
        for z in range(outer):
            along_x(wide, left, gain_x, z)
        product = jnp.dot(left[...], bands_ref[group, 0, 0], preferred_element_type=jnp.float32)
        blurred = (product[:, :width] + product[:, width:]).reshape(outer, rows, width)
        for z in range(outer):
            guess = pl.reciprocal(blurred[z], approx=True)
            guess = guess * (2.0 - blurred[z] * guess)
            ratio[z] = bricks[group][0, z].astype(jnp.float32) * guess
        for k in range(tiles):
            column = along_z([ratio[z, tile(k), :] for z in range(outer)], gain_z[::-1], planes)
            for z in range(planes):
                back[z, tile(k), :] = column[z]
        for z in range(planes):
            along_x(back, left, gain_x[::-1], z)
        product = jnp.dot(left[: planes * rows, :], bands_ref[group, 0, 1], preferred_element_type=jnp.float32)
        total = (product[:, :width] + product[:, width:]).reshape(logs.shape)
        if group % 2 == 0:
            held = total
        else:
            logs[...] += jnp.log(held * total)

    @pl.when(step == pl.num_programs(0) - 1)
    def _():
        for z in range(planes):
            for k in range(tiles):
                value = volume[2 * rim + z, tile(k), :] * jnp.exp(logs[z, tile(k), :] / (count * pl.num_programs(0)))
                if last:
                    out_ref[z, pl.ds(k, SUBLANES, tiles), :] = value
                else:
                    out_ref[z, tile(k), :] = value


def update(place, taps, band, bricks, halo, own, planes, paired, last):
    _, count, outer, rows, width = bricks[0].shape
    groups = sum(part.shape[0] for part in bricks)
    band = band.reshape((groups, count) + band.shape[1:])
    step = lambda v: (0, v, 0, 0, 0)
    return pl.pallas_call(
        functools.partial(update_kernel, last, paired),
        grid=(count,),
        out_shape=jax.ShapeDtypeStruct((planes, rows, width), jnp.float32),
        in_specs=[SMEM, SMEM, pl.BlockSpec((groups, 1) + band.shape[2:], step)]
        + [pl.BlockSpec((part.shape[0], 1, outer, rows, width), step) for part in bricks]
        + [VMEM] * 3,
        out_specs=VMEM,
        scratch_shapes=[
            pltpu.VMEM((2 * outer - planes, rows, width), jnp.float32),
            pltpu.VMEM((2, outer, rows, width), jnp.float32),
            pltpu.VMEM((2, outer * rows, 2 * width), jnp.bfloat16),
            pltpu.VMEM((2, outer, rows, width), jnp.float32),
            pltpu.VMEM((2, planes, rows, width), jnp.float32),
            pltpu.VMEM((planes, rows, width), jnp.float32),
        ],
        compiler_params=PARAMS,
    )(place, taps, band, *bricks, halo[0], own, halo[1])


def place_kernel(planes, place_ref, *refs):
    parts, out_ref = refs[:-1], refs[-1]
    blocks, members = out_ref.shape[:2]
    slot = place_ref[0]
    for index, part in enumerate(parts):
        for block in range(blocks):
            at = slot ^ index
            at = members - 1 - at if block % 2 else at
            out_ref[block, at] = part[block * planes : (block + 1) * planes]


def place_parts(slot, parts, planes):
    depth, rows, width = parts[0].shape
    return pl.pallas_call(
        functools.partial(place_kernel, planes),
        out_shape=jax.ShapeDtypeStruct((depth // planes, len(parts), planes, rows, width), jnp.float32),
        in_specs=[SMEM] + [VMEM] * len(parts),
        out_specs=VMEM,
        compiler_params=PARAMS,
    )(slot, *parts)


def partner(value, bit, members):
    return lax.ppermute(value, "view", [(i, i ^ bit) for i in range(members)])


def line_device(line, members, blocks):
    block, slab = divmod(line, members)
    return (members - 1 - slab if block % 2 else slab) * blocks + block


def swap(value, pairs, members, blocks):
    at = lambda line: line_device(line, members, blocks)
    perm = [(at(i), at(j)) for i, j in pairs] + [(at(j), at(i)) for i, j in pairs]
    return lax.ppermute(value, ("view", "vol"), perm)


def z_rims(own, inner, outer, members, blocks):
    planes = own.shape[0]
    at = lambda line: line_device(line, members, blocks)
    total = members * blocks
    before, after = [], []
    for hop in range(inner // planes + 1, -(-outer // planes) + 1):
        near, far = max((hop - 1) * planes, inner), min(hop * planes, outer)
        up = [(at(i), at(i + hop)) for i in range(total - hop)]
        down = [(at(i + hop), at(i)) for i in range(total - hop)]
        before.append(lax.ppermute(own[hop * planes - far : hop * planes - near], ("view", "vol"), up))
        after.append(lax.ppermute(own[near - (hop - 1) * planes : far - (hop - 1) * planes], ("view", "vol"), down))
    join = lambda parts: parts[0] if len(parts) == 1 else jnp.concatenate(parts)
    return join(before[::-1]), join(after)


def per_device(raw_views, weights, offsets, psf_taps):
    views, depth, rows, width = raw_views.shape
    members, blocks = lax.axis_size("view"), lax.axis_size("vol")
    rim = (psf_taps.shape[2] - 1) // 2
    planes = depth // members
    me = lax.axis_index("view")
    odd = lax.axis_index("vol") % 2
    slab = jnp.where(odd == 1, members - 1 - me, me)
    place = jnp.stack([slab // CORES, slab % CORES]).astype(jnp.int32)

    near_bit, far_bit = 1, CORES
    near = lambda value: partner(value, near_bit, members)
    far = lambda value: partner(value, far_bit, members)
    seams = [(members * block + members - 1 - i, members * (block + 1) + i) for block in range(blocks - 1) for i in range(CORES)]
    across = lambda value: swap(value, seams, members, blocks)
    bound = [(0, (0, depth - rim), (0, 0), rim)]
    inner = [(0, (rim, 2 * planes - rim), (0, 0), 2 * planes)]

    cross_taps = partner(psf_taps, near_bit + far_bit, members)
    (far_bound,) = resample(place, weights, offsets, [raw_views], [(True, bound)])
    far_bound, raw_later, cross_taps = lax.optimization_barrier((far_bound, raw_views, cross_taps))
    far_bound = far(far_bound)
    (far_inner,) = resample(place, weights, offsets, [raw_later], [(True, inner)])
    own_bound, own_inner = resample(place, weights, offsets, [raw_later], [(False, bound), (False, inner)])
    far_inner, far_bound, own_bound, own_inner = lax.optimization_barrier(
        (far_inner, far_bound, own_bound, own_inner)
    )
    far_inner = far(far_inner)
    own_edge, far_edge = across(own_bound), across(far_bound)
    pair_taps = near(jnp.stack([psf_taps, cross_taps]))
    all_taps = jnp.concatenate([psf_taps, pair_taps[0], pair_taps[1], cross_taps])
    all_taps = all_taps / jnp.sum(all_taps, axis=-1, keepdims=True)
    band = bands(all_taps, width)
    home, partial = gather_views(
        place, [own_inner, near(own_inner)], [own_bound, near(own_bound)], [own_edge, near(own_edge)], planes
    )
    far_bounds, far_edges = [far_bound, near(far_bound)], [far_edge, near(far_edge)]
    far_inner, band, home, partial, far_bounds, far_edges = lax.optimization_barrier(
        (far_inner, band, home, partial, far_bounds, far_edges)
    )
    away, start, near_send, cross_send = gather_views(
        place, [far_inner, near(far_inner)], far_bounds, far_edges, planes, members * views, partial
    )
    bricks = [home, away]
    lines = members * blocks
    gaps = [(i, i + 1) for i in range(1, lines - 1, 2)]
    paired = planes == 2 * rim
    if paired:
        halo = (near(near_send), swap(cross_send, gaps, members, blocks))
    else:
        halo = z_rims(start[rim : rim + planes], rim, 2 * rim, members, blocks)
    joined = update(place, all_taps, band, bricks, halo, start, planes, paired, ITERS == 1)
    for turn in range(1, ITERS):
        if paired:
            halo = (near(joined), swap(joined, gaps, members, blocks))
        else:
            halo = z_rims(joined, 0, 2 * rim, members, blocks)
        joined = update(place, all_taps, band, bricks, halo, joined, planes, paired, turn == ITERS - 1)

    columns = lax.all_to_all(joined, "vol", split_axis=1, concat_axis=0, tiled=True)
    far_columns = far(columns)
    parts = [columns, near(columns), far_columns, near(far_columns)]
    result = place_parts(me.reshape(1).astype(jnp.int32), parts, planes)
    return result.reshape((blocks * depth,) + columns.shape[1:])


def solution(mesh):
    placed = (
        P("view", "vol", None, None),
        P("view", None, None),
        P("view", None),
        P("view", None, None),
    )
    return jax.shard_map(
        per_device, mesh=mesh, in_specs=placed, out_specs=P(None, "vol", None), check_vma=False
    )
```

```python
import functools

import jax
import jax.numpy as jnp
from jax import lax
from jax.experimental import pallas as pl
from jax.experimental.pallas import tpu as pltpu
from jax.sharding import PartitionSpec as P

ITERS = 2
CORES = 2
VMEM = pl.BlockSpec(memory_space=pltpu.VMEM)
SMEM = pl.BlockSpec(memory_space=pltpu.SMEM)
PARAMS = pltpu.CompilerParams(vmem_limit_bytes=48 * 1024 * 1024)


def halves(value):
    high = value.astype(jnp.bfloat16)
    low = (value - high.astype(jnp.float32)).astype(jnp.bfloat16)
    return high, low


def resample_kernel(plan, place_ref, weights_ref, offsets_ref, *refs):
    count = 1 + max(segment[0] for parts in plan for segment in parts[1])
    sources, outs = refs[:count], refs[count:]
    weights = weights_ref[0]
    band, rows = weights.shape
    width = sources[0].shape[3]
    weights = weights / jnp.sum(weights, axis=0, keepdims=True)
    first = offsets_ref[0]
    source = lax.broadcasted_iota(jnp.int32, (rows, rows), 0)
    matrix = jnp.zeros((rows, rows), jnp.float32)
    for k in range(band):
        matrix = jnp.where(source == first + k, weights[k : k + 1, :], matrix)
    matrix = matrix.T
    high = matrix.astype(jnp.bfloat16)
    rest = matrix - high.astype(jnp.float32)
    middle = rest.astype(jnp.bfloat16)
    low = (rest - middle.astype(jnp.float32)).astype(jnp.bfloat16)
    left = jnp.concatenate([high, middle, low], axis=1)
    for out_ref, (other, segments) in zip(outs, plan):
        half = 1 - place_ref[0] if other else place_ref[0]
        for index, start, target, length in segments:
            start = start[0] + (start[1] - start[0]) * half
            target = target[0] + (target[1] - target[0]) * half
            for z in range(0, length, 2):
                planes = [sources[index][0, start + z + i] for i in range(2)]
                planes = jnp.concatenate(planes, axis=1)
                planes = jnp.concatenate([planes, planes, planes], axis=0)
                total = jnp.dot(left, planes, preferred_element_type=jnp.float32).astype(jnp.bfloat16)
                for i in range(2):
                    out_ref[0, target + z + i] = total[:, i * width : (i + 1) * width]


def resample(place, weights, offsets, sources, plan):
    views, _, rows, width = sources[0].shape
    band = weights.shape[2]
    block = lambda planes: pl.BlockSpec((1, planes, rows, width), lambda v: (v, 0, 0, 0))
    counts = [sum(segment[3] for segment in segments) for _, segments in plan]
    return pl.pallas_call(
        functools.partial(resample_kernel, plan),
        grid=(views,),
        out_shape=[jax.ShapeDtypeStruct((views, count, rows, width), jnp.bfloat16) for count in counts],
        in_specs=[
            SMEM,
            pl.BlockSpec((1, band, rows), lambda v: (v, 0, 0)),
            pl.BlockSpec((1, 1, rows), lambda v: (v, 0, 0)),
        ]
        + [block(source.shape[1]) for source in sources],
        out_specs=[block(count) for count in counts],
        compiler_params=PARAMS,
    )(place, weights.transpose(0, 2, 1), offsets[:, None, :], *sources)


def bands_kernel(taps_ref, left_ref, right_ref):
    view = pl.program_id(0)
    count = taps_ref.shape[2]
    rows, width = left_ref.shape[2], right_ref.shape[2] // 2

    def band(size, axis, way):
        shape = (size, size)
        shift = lax.broadcasted_iota(jnp.int32, shape, 0) - lax.broadcasted_iota(jnp.int32, shape, 1)
        total = jnp.zeros(shape, jnp.float32)
        for t in range(count):
            at = t - count // 2
            total = jnp.where(shift == (-at if way else at), taps_ref[view, axis, t], total)
        return halves(total)

    for way in range(2):
        high, low = band(rows, 1, 1 - way)
        left_ref[0, way] = jnp.concatenate([high, high, low], axis=1)
        high, low = band(width, 2, way)
        right_ref[0, way, :width, :width] = high
        right_ref[0, way, width:, :width] = high
        right_ref[0, way, :width, width:] = low
        right_ref[0, way, width:, width:] = jnp.zeros_like(low)


def bands(taps, rows, width):
    views = taps.shape[0]
    shapes = [(2, rows, 3 * rows), (2, 2 * width, 2 * width)]
    return pl.pallas_call(
        bands_kernel,
        grid=(views,),
        out_shape=[jax.ShapeDtypeStruct((views,) + shape, jnp.bfloat16) for shape in shapes],
        in_specs=[SMEM],
        out_specs=[pl.BlockSpec((1,) + shape, lambda v: (v, 0, 0, 0)) for shape in shapes],
        compiler_params=PARAMS,
    )(taps)


def gather_kernel(views, planes, rim, place_ref, *refs):
    partial_ref = None
    if views is not None:
        partial_ref, refs = refs[0], refs[1:]
    groups = 2
    inner, bound, edge = refs[:groups], refs[groups : 2 * groups], refs[2 * groups : 3 * groups]
    bricks_ref, start_ref = refs[3 * groups : 3 * groups + 2]
    window = refs[-1]
    step = pl.program_id(0)
    half, core = place_ref[0], place_ref[1]
    main = inner[0].shape[1]

    @pl.when(step == 0)
    def _():
        start_ref[...] = jnp.zeros_like(start_ref) if partial_ref is None else partial_ref[...]

    for group in range(groups):
        for z in range(main):
            window[group, 2 * rim * (1 - half) + z] = inner[group][0, z]
        for z in range(rim):
            window[group, rim + (main - rim) * half + z] = bound[group][0, z]
            window[group, (main + rim) * half + z] = edge[group][0, z]
    for z in range(planes + 2 * rim):
        total = start_ref[z]
        for group in range(groups):
            plane = window[group, planes * core + z]
            bricks_ref[group, 0, z] = plane
            total = total + plane.astype(jnp.float32)
        start_ref[z] = total

    if views is not None:
        near_ref, cross_ref = refs[3 * groups + 2 : 3 * groups + 4]

        @pl.when(step == pl.num_programs(0) - 1)
        def _():
            start_ref[...] = start_ref[...] / views
            for z in range(rim):
                upward, downward = rim + planes - 2 * rim + z, 2 * rim + z
                near_ref[z] = start_ref[upward + (downward - upward) * core]
                cross_ref[z] = start_ref[downward + (upward - downward) * core]


def gather_views(place, inner, bound, edge, planes, views=None, partial=None):
    groups = len(inner)
    count, main, rows, width = inner[0].shape
    rim = edge[0].shape[1]
    outer = planes + 2 * rim
    field = lambda depth: jax.ShapeDtypeStruct((depth, rows, width), jnp.float32)
    sends = [] if views is None else [field(rim), field(rim)]
    parts = [*inner, *bound, *edge]
    return pl.pallas_call(
        functools.partial(gather_kernel, views, planes, rim),
        grid=(count,),
        out_shape=[jax.ShapeDtypeStruct((groups, count, outer, rows, width), jnp.bfloat16), field(outer)] + sends,
        in_specs=[SMEM]
        + ([] if partial is None else [VMEM])
        + [pl.BlockSpec((1,) + part.shape[1:], lambda v: (v, 0, 0, 0)) for part in parts],
        out_specs=[pl.BlockSpec((groups, 1, outer, rows, width), lambda v: (0, v, 0, 0, 0))]
        + [VMEM] * (1 + len(sends)),
        scratch_shapes=[pltpu.VMEM((groups, main + 2 * rim, rows, width), jnp.bfloat16)],
        compiler_params=PARAMS,
    )(place, *([] if partial is None else [partial]), *parts)


def update_kernel(paired, place_ref, taps_ref, lefts_ref, rights_ref, *refs):
    bricks_refs, (first_ref, own_ref, second_ref, out_ref) = refs[:2], refs[2:6]
    volume, fields, flats, ratios, logs = refs[6:]
    bricks = [ref.at[group] for ref in bricks_refs for group in range(ref.shape[0])]
    count = len(bricks)
    step = pl.program_id(0)
    taps = taps_ref.shape[2]
    rim = taps // 2
    planes, rows, width = out_ref.shape
    outer = planes + 2 * rim

    @pl.when(step == 0)
    def _():
        logs[...] = jnp.zeros_like(logs)
        side, middle = first_ref.shape[0], own_ref.shape[0]
        flip = 1 - place_ref[1] if paired else 0
        for z in range(side):
            volume[(side + middle) * flip + z] = first_ref[z]
            volume[(side + middle) * (1 - flip) + z] = second_ref[z]
        for z in range(middle):
            volume[side + z] = own_ref[z]

    def along_z(source, field, gains, length):
        for k in range(0, rows, 16):
            pair = []
            for half in range(2):
                column = [source[z, pl.ds(k + 8 * half, 8), :] for z in range(length + 2 * rim)]
                sums = []
                for z in range(length):
                    total = column[z + rim]
                    for t in range(taps):
                        if t != rim:
                            total = total + gains[t] * column[z + t]
                    sums.append(total)
                pair.append(sums)
            for z in range(length):
                high, low = halves(jnp.concatenate([pair[0][z], pair[1][z]], axis=0))
                field[0, z, pl.ds(k, 16), :] = high
                field[1, z, pl.ds(k, 16), :] = low

    def along_x(field, flat, matrix, length):
        for z in range(0, length, 2):
            high, low = [jnp.concatenate([field[part, z], field[part, z + 1]], axis=1) for part in range(2)]
            right = jnp.concatenate([high, low, high], axis=0)
            high, low = halves(jnp.dot(matrix, right, preferred_element_type=jnp.float32))
            for i in range(2):
                at = pl.ds((z + i) * rows, rows)
                flat[at, :width] = high[:, i * width : (i + 1) * width]
                flat[at, width:] = low[:, i * width : (i + 1) * width]

    def along_y(flat, matrix, length):
        product = jnp.dot(flat[: length * rows, :], matrix, preferred_element_type=jnp.float32)
        return (product[:, :width] + product[:, width:]).reshape(length, rows, width)

    held = None
    for group in range(count):
        view = group * pl.num_programs(0) + step
        field, flat, ratio = (scratch.at[group % 2] for scratch in (fields, flats, ratios))
        gains = [taps_ref[view, 0, t] for t in range(taps)]
        along_z(volume, field, gains, outer)
        along_x(field, flat, lefts_ref[group, 0, 0], outer)
        blurred = along_y(flat, rights_ref[group, 0, 0], outer)
        for z in range(outer):
            guess = pl.reciprocal(blurred[z], approx=True)
            guess = guess * (2.0 - blurred[z] * guess)
            ratio[z] = bricks[group][0, z].astype(jnp.float32) * guess
        along_z(ratio, field, gains[::-1], planes)
        along_x(field, flat, lefts_ref[group, 0, 1], planes)
        total = along_y(flat, rights_ref[group, 0, 1], planes)
        if group % 2 == 0:
            held = total
        else:
            logs[...] += jnp.log(held * total)

    @pl.when(step == pl.num_programs(0) - 1)
    def _():
        for z in range(planes):
            out_ref[z] = volume[2 * rim + z] * jnp.exp(logs[z] / (count * pl.num_programs(0)))


def update(place, taps, band, bricks, halo, own, planes, paired):
    _, count, outer, rows, width = bricks[0].shape
    groups = sum(part.shape[0] for part in bricks)
    band = [part.reshape((groups, count) + part.shape[1:]) for part in band]
    step = lambda v: (0, v, 0, 0, 0)
    return pl.pallas_call(
        functools.partial(update_kernel, paired),
        grid=(count,),
        out_shape=jax.ShapeDtypeStruct((planes, rows, width), jnp.float32),
        in_specs=[SMEM, SMEM]
        + [pl.BlockSpec((groups, 1) + part.shape[2:], step) for part in band]
        + [pl.BlockSpec((part.shape[0], 1, outer, rows, width), step) for part in bricks]
        + [VMEM] * 3,
        out_specs=VMEM,
        scratch_shapes=[
            pltpu.VMEM((2 * outer - planes, rows, width), jnp.float32),
            pltpu.VMEM((2, 2, outer, rows, width), jnp.bfloat16),
            pltpu.VMEM((2, outer * rows, 2 * width), jnp.bfloat16),
            pltpu.VMEM((2, outer, rows, width), jnp.float32),
            pltpu.VMEM((planes, rows, width), jnp.float32),
        ],
        compiler_params=PARAMS,
    )(place, taps, *band, *bricks, halo[0], own, halo[1])


def place_kernel(planes, place_ref, *refs):
    parts, out_ref = refs[:-1], refs[-1]
    blocks, members = out_ref.shape[:2]
    slot = place_ref[0]
    for index, part in enumerate(parts):
        for block in range(blocks):
            at = slot ^ index
            at = members - 1 - at if block % 2 else at
            out_ref[block, at] = part[block * planes : (block + 1) * planes]


def place_parts(slot, parts, planes):
    depth, rows, width = parts[0].shape
    return pl.pallas_call(
        functools.partial(place_kernel, planes),
        out_shape=jax.ShapeDtypeStruct((depth // planes, len(parts), planes, rows, width), jnp.float32),
        in_specs=[SMEM] + [VMEM] * len(parts),
        out_specs=VMEM,
        compiler_params=PARAMS,
    )(slot, *parts)


def partner(value, bit, members):
    return lax.ppermute(value, "view", [(i, i ^ bit) for i in range(members)])


def line_device(line, members, blocks):
    block, slab = divmod(line, members)
    return (members - 1 - slab if block % 2 else slab) * blocks + block


def swap(value, pairs, members, blocks):
    at = lambda line: line_device(line, members, blocks)
    perm = [(at(i), at(j)) for i, j in pairs] + [(at(j), at(i)) for i, j in pairs]
    return lax.ppermute(value, ("view", "vol"), perm)


def z_rims(own, inner, outer, members, blocks):
    planes = own.shape[0]
    at = lambda line: line_device(line, members, blocks)
    total = members * blocks
    before, after = [], []
    for hop in range(inner // planes + 1, -(-outer // planes) + 1):
        near, far = max((hop - 1) * planes, inner), min(hop * planes, outer)
        up = [(at(i), at(i + hop)) for i in range(total - hop)]
        down = [(at(i + hop), at(i)) for i in range(total - hop)]
        before.append(lax.ppermute(own[hop * planes - far : hop * planes - near], ("view", "vol"), up))
        after.append(lax.ppermute(own[near - (hop - 1) * planes : far - (hop - 1) * planes], ("view", "vol"), down))
    join = lambda parts: parts[0] if len(parts) == 1 else jnp.concatenate(parts)
    return join(before[::-1]), join(after)


def per_device(raw_views, weights, offsets, psf_taps):
    views, depth, rows, width = raw_views.shape
    members, blocks = lax.axis_size("view"), lax.axis_size("vol")
    rim = (psf_taps.shape[2] - 1) // 2
    planes = depth // members
    me = lax.axis_index("view")
    odd = lax.axis_index("vol") % 2
    slab = jnp.where(odd == 1, members - 1 - me, me)
    place = jnp.stack([slab // CORES, slab % CORES]).astype(jnp.int32)

    near_bit, far_bit = 1, CORES
    near = lambda value: partner(value, near_bit, members)
    far = lambda value: partner(value, far_bit, members)
    seams = [(members * block + members - 1 - i, members * (block + 1) + i) for block in range(blocks - 1) for i in range(CORES)]
    across = lambda value: swap(value, seams, members, blocks)
    bound = [(0, (0, depth - rim), (0, 0), rim)]
    inner = [(0, (rim, 2 * planes - rim), (0, 0), 2 * planes)]

    cross_taps = partner(psf_taps, near_bit + far_bit, members)
    (far_bound,) = resample(place, weights, offsets, [raw_views], [(True, bound)])
    far_bound, raw_later, cross_taps = lax.optimization_barrier((far_bound, raw_views, cross_taps))
    far_bound = far(far_bound)
    (far_inner,) = resample(place, weights, offsets, [raw_later], [(True, inner)])
    own_bound, own_inner = resample(place, weights, offsets, [raw_later], [(False, bound), (False, inner)])
    far_inner, far_bound, own_bound, own_inner = lax.optimization_barrier(
        (far_inner, far_bound, own_bound, own_inner)
    )
    far_inner = far(far_inner)
    own_edge, far_edge = across(own_bound), across(far_bound)
    pair_taps = near(jnp.stack([psf_taps, cross_taps]))
    all_taps = jnp.concatenate([psf_taps, pair_taps[0], pair_taps[1], cross_taps])
    all_taps = all_taps / jnp.sum(all_taps, axis=-1, keepdims=True)
    centre = all_taps[:, :1, rim : rim + 1]
    all_taps = jnp.concatenate([all_taps[:, :1] / centre, all_taps[:, 1:2], all_taps[:, 2:] * centre], axis=1)
    band = bands(all_taps, rows, width)
    home, partial = gather_views(
        place, [own_inner, near(own_inner)], [own_bound, near(own_bound)], [own_edge, near(own_edge)], planes
    )
    far_bounds, far_edges = [far_bound, near(far_bound)], [far_edge, near(far_edge)]
    far_inner, band, home, partial, far_bounds, far_edges = lax.optimization_barrier(
        (far_inner, band, home, partial, far_bounds, far_edges)
    )
    away, start, near_send, cross_send = gather_views(
        place, [far_inner, near(far_inner)], far_bounds, far_edges, planes, members * views, partial
    )
    bricks = [home, away]
    lines = members * blocks
    gaps = [(i, i + 1) for i in range(1, lines - 1, 2)]
    paired = planes == 2 * rim
    if paired:
        halo = (near(near_send), swap(cross_send, gaps, members, blocks))
    else:
        halo = z_rims(start[rim : rim + planes], rim, 2 * rim, members, blocks)
    joined = update(place, all_taps, band, bricks, halo, start, planes, paired)
    for turn in range(1, ITERS):
        if paired:
            halo = (near(joined), swap(joined, gaps, members, blocks))
        else:
            halo = z_rims(joined, 0, 2 * rim, members, blocks)
        joined = update(place, all_taps, band, bricks, halo, joined, planes, paired)

    columns = lax.all_to_all(joined, "vol", split_axis=1, concat_axis=0, tiled=True)
    far_columns = far(columns)
    parts = [columns, near(columns), far_columns, near(far_columns)]
    result = place_parts(me.reshape(1).astype(jnp.int32), parts, planes)
    return result.reshape((blocks * depth,) + columns.shape[1:])


def solution(mesh):
    placed = (
        P("view", "vol", None, None),
        P("view", None, None),
        P("view", None),
        P("view", None, None),
    )
    return jax.shard_map(
        per_device, mesh=mesh, in_specs=placed, out_specs=P(None, "vol", None), check_vma=False
    )
```

```python
import functools

import jax
import jax.numpy as jnp
from jax import lax
from jax.experimental import pallas as pl
from jax.experimental.pallas import tpu as pltpu
from jax.sharding import PartitionSpec as P

ITERS = 2
CORES = 2
VMEM = pl.BlockSpec(memory_space=pltpu.VMEM)
SMEM = pl.BlockSpec(memory_space=pltpu.SMEM)
PARAMS = pltpu.CompilerParams(vmem_limit_bytes=48 * 1024 * 1024)


def halves(value):
    high = value.astype(jnp.bfloat16)
    low = (value - high.astype(jnp.float32)).astype(jnp.bfloat16)
    return high, low


def resample_kernel(plan, place_ref, weights_ref, offsets_ref, *refs):
    count = 1 + max(segment[0] for parts in plan for segment in parts[1])
    sources, outs = refs[:count], refs[count:]
    weights = weights_ref[0]
    band, rows = weights.shape
    width = sources[0].shape[3]
    weights = weights / jnp.sum(weights, axis=0, keepdims=True)
    first = offsets_ref[0]
    source = lax.broadcasted_iota(jnp.int32, (rows, rows), 0)
    matrix = jnp.zeros((rows, rows), jnp.float32)
    for k in range(band):
        matrix = jnp.where(source == first + k, weights[k : k + 1, :], matrix)
    matrix = matrix.T
    high = matrix.astype(jnp.bfloat16)
    rest = matrix - high.astype(jnp.float32)
    middle = rest.astype(jnp.bfloat16)
    low = (rest - middle.astype(jnp.float32)).astype(jnp.bfloat16)
    left = jnp.concatenate([high, middle, low], axis=1)
    for out_ref, (other, segments) in zip(outs, plan):
        half = 1 - place_ref[0] if other else place_ref[0]
        for index, start, target, length in segments:
            start = start[0] + (start[1] - start[0]) * half
            target = target[0] + (target[1] - target[0]) * half
            for z in range(0, length, 2):
                planes = [sources[index][0, start + z + i] for i in range(2)]
                planes = jnp.concatenate(planes, axis=1)
                planes = jnp.concatenate([planes, planes, planes], axis=0)
                total = jnp.dot(left, planes, preferred_element_type=jnp.float32).astype(jnp.bfloat16)
                for i in range(2):
                    out_ref[0, target + z + i] = total[:, i * width : (i + 1) * width]


def resample(place, weights, offsets, sources, plan):
    views, _, rows, width = sources[0].shape
    band = weights.shape[2]
    block = lambda planes: pl.BlockSpec((1, planes, rows, width), lambda v: (v, 0, 0, 0))
    counts = [sum(segment[3] for segment in segments) for _, segments in plan]
    return pl.pallas_call(
        functools.partial(resample_kernel, plan),
        grid=(views,),
        out_shape=[jax.ShapeDtypeStruct((views, count, rows, width), jnp.bfloat16) for count in counts],
        in_specs=[
            SMEM,
            pl.BlockSpec((1, band, rows), lambda v: (v, 0, 0)),
            pl.BlockSpec((1, 1, rows), lambda v: (v, 0, 0)),
        ]
        + [block(source.shape[1]) for source in sources],
        out_specs=[block(count) for count in counts],
        compiler_params=PARAMS,
    )(place, weights.transpose(0, 2, 1), offsets[:, None, :], *sources)


def bands_kernel(taps_ref, left_ref, right_ref):
    view = pl.program_id(0)
    count = taps_ref.shape[2]
    rows, width = left_ref.shape[2], right_ref.shape[2] // 2

    def band(size, axis, way):
        shape = (size, size)
        shift = lax.broadcasted_iota(jnp.int32, shape, 0) - lax.broadcasted_iota(jnp.int32, shape, 1)
        total = jnp.zeros(shape, jnp.float32)
        for t in range(count):
            at = t - count // 2
            total = jnp.where(shift == (-at if way else at), taps_ref[view, axis, t], total)
        return halves(total)

    for way in range(2):
        high, low = band(rows, 1, 1 - way)
        left_ref[0, way] = jnp.concatenate([high, high, low], axis=1)
        high, low = band(width, 2, way)
        right_ref[0, way, :width, :width] = high
        right_ref[0, way, width:, :width] = high
        right_ref[0, way, :width, width:] = low
        right_ref[0, way, width:, width:] = jnp.zeros_like(low)


def bands(taps, rows, width):
    views = taps.shape[0]
    shapes = [(2, rows, 3 * rows), (2, 2 * width, 2 * width)]
    return pl.pallas_call(
        bands_kernel,
        grid=(views,),
        out_shape=[jax.ShapeDtypeStruct((views,) + shape, jnp.bfloat16) for shape in shapes],
        in_specs=[SMEM],
        out_specs=[pl.BlockSpec((1,) + shape, lambda v: (v, 0, 0, 0)) for shape in shapes],
        compiler_params=PARAMS,
    )(taps)


def gather_kernel(views, planes, rim, place_ref, *refs):
    partial_ref = None
    if views is not None:
        partial_ref, refs = refs[0], refs[1:]
    groups = 2
    inner, bound, edge = refs[:groups], refs[groups : 2 * groups], refs[2 * groups : 3 * groups]
    bricks_ref, start_ref = refs[3 * groups : 3 * groups + 2]
    window = refs[-1]
    step = pl.program_id(0)
    half, core = place_ref[0], place_ref[1]
    main = inner[0].shape[1]

    @pl.when(step == 0)
    def _():
        start_ref[...] = jnp.zeros_like(start_ref) if partial_ref is None else partial_ref[...]

    for group in range(groups):
        for z in range(main):
            window[group, 2 * rim * (1 - half) + z] = inner[group][0, z]
        for z in range(rim):
            window[group, rim + (main - rim) * half + z] = bound[group][0, z]
            window[group, (main + rim) * half + z] = edge[group][0, z]
    for z in range(planes + 2 * rim):
        total = start_ref[z]
        for group in range(groups):
            plane = window[group, planes * core + z]
            bricks_ref[group, 0, z] = plane
            total = total + plane.astype(jnp.float32)
        start_ref[z] = total

    if views is not None:
        near_ref, cross_ref = refs[3 * groups + 2 : 3 * groups + 4]

        @pl.when(step == pl.num_programs(0) - 1)
        def _():
            start_ref[...] = start_ref[...] / views
            for z in range(rim):
                upward, downward = rim + planes - 2 * rim + z, 2 * rim + z
                near_ref[z] = start_ref[upward + (downward - upward) * core]
                cross_ref[z] = start_ref[downward + (upward - downward) * core]


def gather_views(place, inner, bound, edge, planes, views=None, partial=None):
    groups = len(inner)
    count, main, rows, width = inner[0].shape
    rim = edge[0].shape[1]
    outer = planes + 2 * rim
    field = lambda depth: jax.ShapeDtypeStruct((depth, rows, width), jnp.float32)
    sends = [] if views is None else [field(rim), field(rim)]
    parts = [*inner, *bound, *edge]
    return pl.pallas_call(
        functools.partial(gather_kernel, views, planes, rim),
        grid=(count,),
        out_shape=[jax.ShapeDtypeStruct((groups, count, outer, rows, width), jnp.bfloat16), field(outer)] + sends,
        in_specs=[SMEM]
        + ([] if partial is None else [VMEM])
        + [pl.BlockSpec((1,) + part.shape[1:], lambda v: (v, 0, 0, 0)) for part in parts],
        out_specs=[pl.BlockSpec((groups, 1, outer, rows, width), lambda v: (0, v, 0, 0, 0))]
        + [VMEM] * (1 + len(sends)),
        scratch_shapes=[pltpu.VMEM((groups, main + 2 * rim, rows, width), jnp.bfloat16)],
        compiler_params=PARAMS,
    )(place, *([] if partial is None else [partial]), *parts)


def update_kernel(paired, place_ref, taps_ref, lefts_ref, rights_ref, *refs):
    bricks_refs, (first_ref, own_ref, second_ref, out_ref) = refs[:2], refs[2:6]
    volume, ratios, held, logs = refs[6:]
    bricks = [ref.at[group] for ref in bricks_refs for group in range(ref.shape[0])]
    count = len(bricks)
    step = pl.program_id(0)
    taps = taps_ref.shape[2]
    rim = taps // 2
    planes, rows, width = out_ref.shape
    outer = planes + 2 * rim

    @pl.when(step == 0)
    def _():
        logs[...] = jnp.zeros_like(logs)
        side, middle = first_ref.shape[0], own_ref.shape[0]
        flip = 1 - place_ref[1] if paired else 0
        for z in range(side):
            volume[(side + middle) * flip + z] = first_ref[z]
            volume[(side + middle) * (1 - flip) + z] = second_ref[z]
        for z in range(middle):
            volume[side + z] = own_ref[z]

    def along_z(source, gains, z):
        tiles = []
        for k in range(0, rows, 8):
            column = [source[z + t, pl.ds(k, 8), :] for t in range(taps)]
            total = column[rim]
            for t in range(taps):
                if t != rim:
                    total = total + gains[t] * column[t]
            tiles.append(total)
        return jnp.concatenate(tiles, axis=0)

    def chain(source, gains, left, right, z):
        high, low = halves(jnp.concatenate([along_z(source, gains, z + i) for i in range(2)], axis=1))
        stacked = jnp.concatenate([high, low, high], axis=0)
        parts = halves(jnp.dot(left, stacked, preferred_element_type=jnp.float32))
        flat = jnp.concatenate(
            [jnp.concatenate([part[:, i * width : (i + 1) * width] for part in parts], axis=1) for i in range(2)], axis=0
        )
        product = jnp.dot(flat, right, preferred_element_type=jnp.float32)
        total = product[:, :width] + product[:, width:]
        return total[:rows], total[rows:]

    for group in range(count):
        view = group * pl.num_programs(0) + step
        ratio = ratios.at[group % 2]
        gains = [taps_ref[view, 0, t] for t in range(taps)]
        for z in range(0, outer, 2):
            pair = chain(volume, gains, lefts_ref[group, 0, 0], rights_ref[group, 0, 0], z)
            for i, blurred in enumerate(pair):
                guess = pl.reciprocal(blurred, approx=True)
                guess = guess * (2.0 - blurred * guess)
                ratio[z + i] = bricks[group][0, z + i].astype(jnp.float32) * guess
        for z in range(0, planes, 2):
            pair = chain(ratio, gains[::-1], lefts_ref[group, 0, 1], rights_ref[group, 0, 1], z)
            for i, back in enumerate(pair):
                if group % 2 == 0:
                    held[z + i] = back
                else:
                    logs[z + i] += jnp.log(held[z + i] * back)

    @pl.when(step == pl.num_programs(0) - 1)
    def _():
        for z in range(planes):
            out_ref[z] = volume[2 * rim + z] * jnp.exp(logs[z] / (count * pl.num_programs(0)))


def update(place, taps, band, bricks, halo, own, planes, paired):
    _, count, outer, rows, width = bricks[0].shape
    groups = sum(part.shape[0] for part in bricks)
    band = [part.reshape((groups, count) + part.shape[1:]) for part in band]
    step = lambda v: (0, v, 0, 0, 0)
    return pl.pallas_call(
        functools.partial(update_kernel, paired),
        grid=(count,),
        out_shape=jax.ShapeDtypeStruct((planes, rows, width), jnp.float32),
        in_specs=[SMEM, SMEM]
        + [pl.BlockSpec((groups, 1) + part.shape[2:], step) for part in band]
        + [pl.BlockSpec((part.shape[0], 1, outer, rows, width), step) for part in bricks]
        + [VMEM] * 3,
        out_specs=VMEM,
        scratch_shapes=[
            pltpu.VMEM((2 * outer - planes, rows, width), jnp.float32),
            pltpu.VMEM((2, outer, rows, width), jnp.float32),
            pltpu.VMEM((planes, rows, width), jnp.float32),
            pltpu.VMEM((planes, rows, width), jnp.float32),
        ],
        compiler_params=PARAMS,
    )(place, taps, *band, *bricks, halo[0], own, halo[1])


def place_kernel(planes, place_ref, *refs):
    parts, out_ref = refs[:-1], refs[-1]
    blocks, members = out_ref.shape[:2]
    slot = place_ref[0]
    for index, part in enumerate(parts):
        for block in range(blocks):
            at = slot ^ index
            at = members - 1 - at if block % 2 else at
            out_ref[block, at] = part[block * planes : (block + 1) * planes]


def place_parts(slot, parts, planes):
    depth, rows, width = parts[0].shape
    return pl.pallas_call(
        functools.partial(place_kernel, planes),
        out_shape=jax.ShapeDtypeStruct((depth // planes, len(parts), planes, rows, width), jnp.float32),
        in_specs=[SMEM] + [VMEM] * len(parts),
        out_specs=VMEM,
        compiler_params=PARAMS,
    )(slot, *parts)


def partner(value, bit, members):
    return lax.ppermute(value, "view", [(i, i ^ bit) for i in range(members)])


def line_device(line, members, blocks):
    block, slab = divmod(line, members)
    return (members - 1 - slab if block % 2 else slab) * blocks + block


def swap(value, pairs, members, blocks):
    at = lambda line: line_device(line, members, blocks)
    perm = [(at(i), at(j)) for i, j in pairs] + [(at(j), at(i)) for i, j in pairs]
    return lax.ppermute(value, ("view", "vol"), perm)


def z_rims(own, inner, outer, members, blocks):
    planes = own.shape[0]
    at = lambda line: line_device(line, members, blocks)
    total = members * blocks
    before, after = [], []
    for hop in range(inner // planes + 1, -(-outer // planes) + 1):
        near, far = max((hop - 1) * planes, inner), min(hop * planes, outer)
        up = [(at(i), at(i + hop)) for i in range(total - hop)]
        down = [(at(i + hop), at(i)) for i in range(total - hop)]
        before.append(lax.ppermute(own[hop * planes - far : hop * planes - near], ("view", "vol"), up))
        after.append(lax.ppermute(own[near - (hop - 1) * planes : far - (hop - 1) * planes], ("view", "vol"), down))
    join = lambda parts: parts[0] if len(parts) == 1 else jnp.concatenate(parts)
    return join(before[::-1]), join(after)


def per_device(raw_views, weights, offsets, psf_taps):
    views, depth, rows, width = raw_views.shape
    members, blocks = lax.axis_size("view"), lax.axis_size("vol")
    rim = (psf_taps.shape[2] - 1) // 2
    planes = depth // members
    me = lax.axis_index("view")
    odd = lax.axis_index("vol") % 2
    slab = jnp.where(odd == 1, members - 1 - me, me)
    place = jnp.stack([slab // CORES, slab % CORES]).astype(jnp.int32)

    near_bit, far_bit = 1, CORES
    near = lambda value: partner(value, near_bit, members)
    far = lambda value: partner(value, far_bit, members)
    seams = [(members * block + members - 1 - i, members * (block + 1) + i) for block in range(blocks - 1) for i in range(CORES)]
    across = lambda value: swap(value, seams, members, blocks)
    bound = [(0, (0, depth - rim), (0, 0), rim)]
    inner = [(0, (rim, 2 * planes - rim), (0, 0), 2 * planes)]

    cross_taps = partner(psf_taps, near_bit + far_bit, members)
    (far_bound,) = resample(place, weights, offsets, [raw_views], [(True, bound)])
    far_bound, raw_later, cross_taps = lax.optimization_barrier((far_bound, raw_views, cross_taps))
    far_bound = far(far_bound)
    (far_inner,) = resample(place, weights, offsets, [raw_later], [(True, inner)])
    far_inner = far(far_inner)
    far_bound, raw_later = lax.optimization_barrier((far_bound, raw_later))
    own_bound, own_inner = resample(place, weights, offsets, [raw_later], [(False, bound), (False, inner)])
    own_edge, far_edge = across(own_bound), across(far_bound)
    pair_taps = near(jnp.stack([psf_taps, cross_taps]))
    all_taps = jnp.concatenate([psf_taps, pair_taps[0], pair_taps[1], cross_taps])
    all_taps = all_taps / jnp.sum(all_taps, axis=-1, keepdims=True)
    centre = all_taps[:, :1, rim : rim + 1]
    all_taps = jnp.concatenate([all_taps[:, :1] / centre, all_taps[:, 1:2], all_taps[:, 2:] * centre], axis=1)
    band = bands(all_taps, rows, width)
    home, partial = gather_views(
        place, [own_inner, near(own_inner)], [own_bound, near(own_bound)], [own_edge, near(own_edge)], planes
    )
    far_bounds, far_edges = [far_bound, near(far_bound)], [far_edge, near(far_edge)]
    far_inner, band, home, partial, far_bounds, far_edges = lax.optimization_barrier(
        (far_inner, band, home, partial, far_bounds, far_edges)
    )
    away, start, near_send, cross_send = gather_views(
        place, [far_inner, near(far_inner)], far_bounds, far_edges, planes, members * views, partial
    )
    bricks = [home, away]
    lines = members * blocks
    gaps = [(i, i + 1) for i in range(1, lines - 1, 2)]
    paired = planes == 2 * rim
    if paired:
        halo = (near(near_send), swap(cross_send, gaps, members, blocks))
    else:
        halo = z_rims(start[rim : rim + planes], rim, 2 * rim, members, blocks)
    joined = update(place, all_taps, band, bricks, halo, start, planes, paired)
    for turn in range(1, ITERS):
        if paired:
            halo = (near(joined), swap(joined, gaps, members, blocks))
        else:
            halo = z_rims(joined, 0, 2 * rim, members, blocks)
        joined = update(place, all_taps, band, bricks, halo, joined, planes, paired)

    columns = lax.all_to_all(joined, "vol", split_axis=1, concat_axis=0, tiled=True)
    far_columns = far(columns)
    parts = [columns, near(columns), far_columns, near(far_columns)]
    result = place_parts(me.reshape(1).astype(jnp.int32), parts, planes)
    return result.reshape((blocks * depth,) + columns.shape[1:])


def solution(mesh):
    placed = (
        P("view", "vol", None, None),
        P("view", None, None),
        P("view", None),
        P("view", None, None),
    )
    return jax.shard_map(
        per_device, mesh=mesh, in_specs=placed, out_specs=P(None, "vol", None), check_vma=False
    )
```

```python
import functools

import jax
import jax.numpy as jnp
from jax import lax
from jax.experimental import pallas as pl
from jax.experimental.pallas import tpu as pltpu
from jax.sharding import PartitionSpec as P

ITERS = 2
CORES = 2
VMEM = pl.BlockSpec(memory_space=pltpu.VMEM)
SMEM = pl.BlockSpec(memory_space=pltpu.SMEM)
PARAMS = pltpu.CompilerParams(vmem_limit_bytes=48 * 1024 * 1024)


def halves(value):
    high = value.astype(jnp.bfloat16)
    low = (value - high.astype(jnp.float32)).astype(jnp.bfloat16)
    return high, low


def resample_kernel(plan, place_ref, weights_ref, offsets_ref, *refs):
    count = 1 + max(segment[0] for parts in plan for segment in parts[1])
    sources, outs = refs[:count], refs[count:]
    weights = weights_ref[0]
    band, rows = weights.shape
    width = sources[0].shape[3]
    weights = weights / jnp.sum(weights, axis=0, keepdims=True)
    first = offsets_ref[0]
    source = lax.broadcasted_iota(jnp.int32, (rows, rows), 0)
    matrix = jnp.zeros((rows, rows), jnp.float32)
    for k in range(band):
        matrix = jnp.where(source == first + k, weights[k : k + 1, :], matrix)
    matrix = matrix.T
    high = matrix.astype(jnp.bfloat16)
    rest = matrix - high.astype(jnp.float32)
    middle = rest.astype(jnp.bfloat16)
    low = (rest - middle.astype(jnp.float32)).astype(jnp.bfloat16)
    left = jnp.concatenate([high, middle, low], axis=1)
    for out_ref, (other, segments) in zip(outs, plan):
        half = 1 - place_ref[0] if other else place_ref[0]
        for index, start, target, length in segments:
            start = start[0] + (start[1] - start[0]) * half
            target = target[0] + (target[1] - target[0]) * half
            for z in range(0, length, 2):
                planes = [sources[index][0, start + z + i] for i in range(2)]
                planes = jnp.concatenate(planes, axis=1)
                planes = jnp.concatenate([planes, planes, planes], axis=0)
                total = jnp.dot(left, planes, preferred_element_type=jnp.float32).astype(jnp.bfloat16)
                for i in range(2):
                    out_ref[0, target + z + i] = total[:, i * width : (i + 1) * width]


def resample(place, weights, offsets, sources, plan):
    views, _, rows, width = sources[0].shape
    band = weights.shape[2]
    block = lambda planes: pl.BlockSpec((1, planes, rows, width), lambda v: (v, 0, 0, 0))
    counts = [sum(segment[3] for segment in segments) for _, segments in plan]
    return pl.pallas_call(
        functools.partial(resample_kernel, plan),
        grid=(views,),
        out_shape=[jax.ShapeDtypeStruct((views, count, rows, width), jnp.bfloat16) for count in counts],
        in_specs=[
            SMEM,
            pl.BlockSpec((1, band, rows), lambda v: (v, 0, 0)),
            pl.BlockSpec((1, 1, rows), lambda v: (v, 0, 0)),
        ]
        + [block(source.shape[1]) for source in sources],
        out_specs=[block(count) for count in counts],
        compiler_params=PARAMS,
    )(place, weights.transpose(0, 2, 1), offsets[:, None, :], *sources)


def bands_kernel(taps_ref, left_ref, right_ref):
    view = pl.program_id(0)
    count = taps_ref.shape[2]
    rows, width = left_ref.shape[2], right_ref.shape[2]

    def band(size, axis, way):
        shape = (size, size)
        shift = lax.broadcasted_iota(jnp.int32, shape, 0) - lax.broadcasted_iota(jnp.int32, shape, 1)
        total = jnp.zeros(shape, jnp.float32)
        for t in range(count):
            at = t - count // 2
            total = jnp.where(shift == (-at if way else at), taps_ref[view, axis, t], total)
        return halves(total)

    for way in range(2):
        high, low = band(rows, 1, 1 - way)
        left_ref[0, way] = jnp.concatenate([high, high, low], axis=1)
        right_ref[0, way] = jnp.concatenate(band(width, 2, way), axis=1)


def bands(taps, rows, width):
    views = taps.shape[0]
    shapes = [(2, rows, 3 * rows), (2, width, 2 * width)]
    return pl.pallas_call(
        bands_kernel,
        grid=(views,),
        out_shape=[jax.ShapeDtypeStruct((views,) + shape, jnp.bfloat16) for shape in shapes],
        in_specs=[SMEM],
        out_specs=[pl.BlockSpec((1,) + shape, lambda v: (v, 0, 0, 0)) for shape in shapes],
        compiler_params=PARAMS,
    )(taps)


def gather_kernel(views, planes, rim, place_ref, *refs):
    partial_ref = None
    if views is not None:
        partial_ref, refs = refs[0], refs[1:]
    groups = 2
    inner, bound, edge = refs[:groups], refs[groups : 2 * groups], refs[2 * groups : 3 * groups]
    bricks_ref, start_ref = refs[3 * groups : 3 * groups + 2]
    window = refs[-1]
    step = pl.program_id(0)
    half, core = place_ref[0], place_ref[1]
    main = inner[0].shape[1]

    @pl.when(step == 0)
    def _():
        start_ref[...] = jnp.zeros_like(start_ref) if partial_ref is None else partial_ref[...]

    for group in range(groups):
        for z in range(main):
            window[group, 2 * rim * (1 - half) + z] = inner[group][0, z]
        for z in range(rim):
            window[group, rim + (main - rim) * half + z] = bound[group][0, z]
            window[group, (main + rim) * half + z] = edge[group][0, z]
    for z in range(planes + 2 * rim):
        total = start_ref[z]
        for group in range(groups):
            plane = window[group, planes * core + z]
            bricks_ref[group, 0, z] = plane
            total = total + plane.astype(jnp.float32)
        start_ref[z] = total

    if views is not None:
        near_ref, cross_ref = refs[3 * groups + 2 : 3 * groups + 4]

        @pl.when(step == pl.num_programs(0) - 1)
        def _():
            start_ref[...] = start_ref[...] / views
            for z in range(rim):
                upward, downward = rim + planes - 2 * rim + z, 2 * rim + z
                near_ref[z] = start_ref[upward + (downward - upward) * core]
                cross_ref[z] = start_ref[downward + (upward - downward) * core]


def gather_views(place, inner, bound, edge, planes, side, views=None, partial=None):
    groups = len(inner)
    count, main, rows, width = inner[0].shape
    rim = edge[0].shape[1]
    take = lambda part: 0 if part.shape[0] == count else side * count
    outer = planes + 2 * rim
    field = lambda depth: jax.ShapeDtypeStruct((depth, rows, width), jnp.float32)
    sends = [] if views is None else [field(rim), field(rim)]
    parts = [*inner, *bound, *edge]
    return pl.pallas_call(
        functools.partial(gather_kernel, views, planes, rim),
        grid=(count,),
        out_shape=[jax.ShapeDtypeStruct((groups, count, outer, rows, width), jnp.bfloat16), field(outer)] + sends,
        in_specs=[SMEM]
        + ([] if partial is None else [VMEM])
        + [pl.BlockSpec((1,) + part.shape[1:], lambda v, base=take(part): (v + base, 0, 0, 0)) for part in parts],
        out_specs=[pl.BlockSpec((groups, 1, outer, rows, width), lambda v: (0, v, 0, 0, 0))]
        + [VMEM] * (1 + len(sends)),
        scratch_shapes=[pltpu.VMEM((groups, main + 2 * rim, rows, width), jnp.bfloat16)],
        compiler_params=PARAMS,
    )(place, *([] if partial is None else [partial]), *parts)


def update_kernel(paired, place_ref, taps_ref, lefts_ref, rights_ref, *refs):
    bricks_refs, (first_ref, own_ref, second_ref, out_ref) = refs[:2], refs[2:6]
    volume, ratios, held, logs = refs[6:]
    bricks = [ref.at[group] for ref in bricks_refs for group in range(ref.shape[0])]
    count = len(bricks)
    step = pl.program_id(0)
    taps = taps_ref.shape[2]
    rim = taps // 2
    planes, rows, width = out_ref.shape
    outer = planes + 2 * rim

    @pl.when(step == 0)
    def _():
        logs[...] = jnp.zeros_like(logs)
        side, middle = first_ref.shape[0], own_ref.shape[0]
        flip = 1 - place_ref[1] if paired else 0
        for z in range(side):
            volume[(side + middle) * flip + z] = first_ref[z]
            volume[(side + middle) * (1 - flip) + z] = second_ref[z]
        for z in range(middle):
            volume[side + z] = own_ref[z]

    def along_z(source, gains, z, length):
        sums = [[] for _ in range(length)]
        for k in range(0, rows, 8):
            column = [source[z + t, pl.ds(k, 8), :] for t in range(length + 2 * rim)]
            for i in range(length):
                total = column[i + rim]
                for t in range(taps):
                    if t != rim:
                        total = total + gains[t] * column[i + t]
                sums[i].append(total)
        return [jnp.concatenate(tiles, axis=0) for tiles in sums]

    def chain(source, gains, left, right, z, length):
        fields = along_z(source, gains, z, length)
        flats = []
        for i in range(0, length, 2):
            high, low = halves(jnp.concatenate(fields[i : i + 2], axis=1))
            stacked = jnp.concatenate([high, low, high], axis=0)
            parts = halves(jnp.dot(left, stacked, preferred_element_type=jnp.float32))
            for j in range(2):
                flats.append(jnp.concatenate([part[:, j * width : (j + 1) * width] for part in parts], axis=1))
        right = jnp.concatenate(
            [right, jnp.concatenate([right[:, :width], jnp.zeros((width, width), jnp.bfloat16)], axis=1)], axis=0
        )
        product = jnp.dot(jnp.concatenate(flats, axis=0), right, preferred_element_type=jnp.float32)
        total = product[:, :width] + product[:, width:]
        return [total[i * rows : (i + 1) * rows] for i in range(length)]

    def chunks(length):
        size = 2 if length % 4 else 4
        return [(z, size) for z in range(0, length, size)]

    for group in range(count):
        view = group * pl.num_programs(0) + step
        ratio = ratios.at[group % 2]
        gains = [taps_ref[view, 0, t] for t in range(taps)]
        for z, size in chunks(outer):
            fields = chain(volume, gains, lefts_ref[group, 0, 0], rights_ref[group, 0, 0], z, size)
            for i, blurred in enumerate(fields):
                guess = pl.reciprocal(blurred, approx=True)
                guess = guess * (2.0 - blurred * guess)
                ratio[z + i] = bricks[group][0, z + i].astype(jnp.float32) * guess
        for z, size in chunks(planes):
            fields = chain(ratio, gains[::-1], lefts_ref[group, 0, 1], rights_ref[group, 0, 1], z, size)
            for i, back in enumerate(fields):
                if group % 2 == 0:
                    held[z + i] = back
                else:
                    logs[z + i] += jnp.log(held[z + i] * back)

    @pl.when(step == pl.num_programs(0) - 1)
    def _():
        for z in range(planes):
            out_ref[z] = volume[2 * rim + z] * jnp.exp(logs[z] / (count * pl.num_programs(0)))


def update(place, taps, band, bricks, halo, own, planes, paired):
    _, count, outer, rows, width = bricks[0].shape
    groups = sum(part.shape[0] for part in bricks)
    band = [part.reshape((groups, count) + part.shape[1:]) for part in band]
    step = lambda v: (0, v, 0, 0, 0)
    return pl.pallas_call(
        functools.partial(update_kernel, paired),
        grid=(count,),
        out_shape=jax.ShapeDtypeStruct((planes, rows, width), jnp.float32),
        in_specs=[SMEM, SMEM]
        + [pl.BlockSpec((groups, 1) + part.shape[2:], step) for part in band]
        + [pl.BlockSpec((part.shape[0], 1, outer, rows, width), step) for part in bricks]
        + [VMEM] * 3,
        out_specs=VMEM,
        scratch_shapes=[
            pltpu.VMEM((2 * outer - planes, rows, width), jnp.float32),
            pltpu.VMEM((2, outer, rows, width), jnp.float32),
            pltpu.VMEM((planes, rows, width), jnp.float32),
            pltpu.VMEM((planes, rows, width), jnp.float32),
        ],
        compiler_params=PARAMS,
    )(place, taps, *band, *bricks, halo[0], own, halo[1])


def place_kernel(planes, place_ref, *refs):
    parts, out_ref = refs[:-1], refs[-1]
    blocks, members = out_ref.shape[:2]
    slot = place_ref[0]
    for index, part in enumerate(parts):
        for block in range(blocks):
            at = slot ^ index
            at = members - 1 - at if block % 2 else at
            out_ref[block, at] = part[block * planes : (block + 1) * planes]


def place_parts(slot, parts, planes):
    depth, rows, width = parts[0].shape
    return pl.pallas_call(
        functools.partial(place_kernel, planes),
        out_shape=jax.ShapeDtypeStruct((depth // planes, len(parts), planes, rows, width), jnp.float32),
        in_specs=[SMEM] + [VMEM] * len(parts),
        out_specs=VMEM,
        compiler_params=PARAMS,
    )(slot, *parts)


def partner(value, bit, members):
    return lax.ppermute(value, "view", [(i, i ^ bit) for i in range(members)])


def line_device(line, members, blocks):
    block, slab = divmod(line, members)
    return (members - 1 - slab if block % 2 else slab) * blocks + block


def swap(value, pairs, members, blocks):
    at = lambda line: line_device(line, members, blocks)
    perm = [(at(i), at(j)) for i, j in pairs] + [(at(j), at(i)) for i, j in pairs]
    return lax.ppermute(value, ("view", "vol"), perm)


def z_rims(own, inner, outer, members, blocks):
    planes = own.shape[0]
    at = lambda line: line_device(line, members, blocks)
    total = members * blocks
    before, after = [], []
    for hop in range(inner // planes + 1, -(-outer // planes) + 1):
        near, far = max((hop - 1) * planes, inner), min(hop * planes, outer)
        up = [(at(i), at(i + hop)) for i in range(total - hop)]
        down = [(at(i + hop), at(i)) for i in range(total - hop)]
        before.append(lax.ppermute(own[hop * planes - far : hop * planes - near], ("view", "vol"), up))
        after.append(lax.ppermute(own[near - (hop - 1) * planes : far - (hop - 1) * planes], ("view", "vol"), down))
    join = lambda parts: parts[0] if len(parts) == 1 else jnp.concatenate(parts)
    return join(before[::-1]), join(after)


def per_device(raw_views, weights, offsets, psf_taps):
    views, depth, rows, width = raw_views.shape
    members, blocks = lax.axis_size("view"), lax.axis_size("vol")
    rim = (psf_taps.shape[2] - 1) // 2
    planes = depth // members
    me = lax.axis_index("view")
    odd = lax.axis_index("vol") % 2
    slab = jnp.where(odd == 1, members - 1 - me, me)
    place = jnp.stack([slab // CORES, slab % CORES]).astype(jnp.int32)

    near_bit, far_bit = 1, CORES
    near = lambda value: partner(value, near_bit, members)
    far = lambda value: partner(value, far_bit, members)
    seams = [(members * block + members - 1 - i, members * (block + 1) + i) for block in range(blocks - 1) for i in range(CORES)]
    across = lambda value: swap(value, seams, members, blocks)
    bound = [(0, (0, depth - rim), (0, 0), rim)]
    inner = [(0, (rim, 2 * planes - rim), (0, 0), 2 * planes)]

    cross_taps = partner(psf_taps, near_bit + far_bit, members)
    (far_bound,) = resample(place, weights, offsets, [raw_views], [(True, bound)])
    far_bound, raw_later, cross_taps = lax.optimization_barrier((far_bound, raw_views, cross_taps))
    far_bound = far(far_bound)
    far_inner, own_bound, own_inner = resample(
        place, weights, offsets, [raw_later], [(True, inner), (False, bound), (False, inner)]
    )
    far_inner = far(far_inner)
    near_inner = near(own_inner)
    pair_taps = near(jnp.stack([psf_taps, cross_taps]))
    all_taps = jnp.concatenate([psf_taps, pair_taps[0], pair_taps[1], cross_taps])
    all_taps = all_taps / jnp.sum(all_taps, axis=-1, keepdims=True)
    centre = all_taps[:, :1, rim : rim + 1]
    all_taps = jnp.concatenate([all_taps[:, :1] / centre, all_taps[:, 1:2], all_taps[:, 2:] * centre], axis=1)
    band = bands(all_taps, rows, width)
    bounds = jnp.concatenate([own_bound, far_bound])
    edges = across(bounds)
    edges, band = lax.optimization_barrier((edges, band))
    bounds, edges = [bounds, near(bounds)], [edges, near(edges)]
    home, partial = gather_views(place, [own_inner, near_inner], bounds, edges, planes, 0)
    far_inner, home, partial = lax.optimization_barrier((far_inner, home, partial))
    away, start, near_send, cross_send = gather_views(
        place, [far_inner, near(far_inner)], bounds, edges, planes, 1, members * views, partial
    )
    bricks = [home, away]
    lines = members * blocks
    gaps = [(i, i + 1) for i in range(1, lines - 1, 2)]
    paired = planes == 2 * rim
    if paired:
        halo = (near(near_send), swap(cross_send, gaps, members, blocks))
    else:
        halo = z_rims(start[rim : rim + planes], rim, 2 * rim, members, blocks)
    joined = update(place, all_taps, band, bricks, halo, start, planes, paired)
    for turn in range(1, ITERS):
        if paired:
            halo = (near(joined), swap(joined, gaps, members, blocks))
        else:
            halo = z_rims(joined, 0, 2 * rim, members, blocks)
        joined = update(place, all_taps, band, bricks, halo, joined, planes, paired)

    columns = lax.all_to_all(joined, "vol", split_axis=1, concat_axis=0, tiled=True)
    far_columns = far(columns)
    parts = [columns, near(columns), far_columns, near(far_columns)]
    result = place_parts(me.reshape(1).astype(jnp.int32), parts, planes)
    return result.reshape((blocks * depth,) + columns.shape[1:])


def solution(mesh):
    placed = (
        P("view", "vol", None, None),
        P("view", None, None),
        P("view", None),
        P("view", None, None),
    )
    return jax.shard_map(
        per_device, mesh=mesh, in_specs=placed, out_specs=P(None, "vol", None), check_vma=False
    )
```

```python
import functools

import jax
import jax.numpy as jnp
from jax import lax
from jax.experimental import pallas as pl
from jax.experimental.pallas import tpu as pltpu
from jax.sharding import PartitionSpec as P

ITERS = 2
CORES = 2
VMEM = pl.BlockSpec(memory_space=pltpu.VMEM)
SMEM = pl.BlockSpec(memory_space=pltpu.SMEM)
PARAMS = pltpu.CompilerParams(vmem_limit_bytes=24 * 1024 * 1024)


def halves(value):
    high = value.astype(jnp.bfloat16)
    low = (value - high.astype(jnp.float32)).astype(jnp.bfloat16)
    return high, low


def row_matrix(weights, first):
    band, rows = weights.shape
    weights = weights / jnp.sum(weights, axis=0, keepdims=True)
    source = lax.broadcasted_iota(jnp.int32, (rows, rows), 0)
    matrix = jnp.zeros((rows, rows), jnp.float32)
    for k in range(band):
        matrix = jnp.where(source == first + k, weights[k : k + 1, :], matrix)
    matrix = matrix.T
    high = matrix.astype(jnp.bfloat16)
    rest = matrix - high.astype(jnp.float32)
    middle = rest.astype(jnp.bfloat16)
    low = (rest - middle.astype(jnp.float32)).astype(jnp.bfloat16)
    return jnp.concatenate([high, middle, low], axis=1)


def two_rows(left, first, second):
    planes = jnp.concatenate([first, second], axis=1)
    planes = jnp.concatenate([planes, planes, planes], axis=0)
    total = jnp.dot(left, planes, preferred_element_type=jnp.float32).astype(jnp.bfloat16)
    width = first.shape[1]
    return total[:, :width], total[:, width:]


def bound_kernel(place_ref, weights_hbm, offsets_hbm, raw_hbm, out_ref, weights_ref, offsets_ref, planes_ref, sems):
    view = pl.program_id(0)
    depth, rim = raw_hbm.shape[1], out_ref.shape[1]

    @pl.when(view == 0)
    def _():
        start = (depth - rim) * (1 - place_ref[0])
        pairs = [(weights_hbm, weights_ref), (offsets_hbm, offsets_ref), (raw_hbm.at[:, pl.ds(start, rim)], planes_ref)]
        copies = [pltpu.make_async_copy(*pair, sems.at[i]) for i, pair in enumerate(pairs)]
        for copy in copies:
            copy.start()
        for copy in copies:
            copy.wait()

    left = row_matrix(weights_ref[view], offsets_ref[pl.ds(view, 1), :])
    for z in range(0, rim, 2):
        out_ref[0, z], out_ref[0, z + 1] = two_rows(left, planes_ref[view, z], planes_ref[view, z + 1])


def resample_bound(place, weights, offsets, raw, rim):
    views, _, rows, width = raw.shape
    shape = (views, rim, rows, width)
    weights = weights.transpose(0, 2, 1)
    return pl.pallas_call(
        bound_kernel,
        grid=(views,),
        out_shape=jax.ShapeDtypeStruct(shape, jnp.bfloat16),
        in_specs=[SMEM] + [pl.BlockSpec(memory_space=pltpu.HBM)] * 3,
        out_specs=pl.BlockSpec((1,) + shape[1:], lambda v: (v, 0, 0, 0)),
        scratch_shapes=[
            pltpu.VMEM(weights.shape, jnp.float32),
            pltpu.VMEM(offsets.shape, jnp.int32),
            pltpu.VMEM(shape, jnp.bfloat16),
            pltpu.SemaphoreType.DMA((3,)),
        ],
        compiler_params=pltpu.CompilerParams(vmem_limit_bytes=63 * 1024 * 1024),
    )(place, weights, offsets, raw)


def resample_kernel(plan, place_ref, weights_ref, offsets_ref, raw_ref, *outs):
    left = row_matrix(weights_ref[0], offsets_ref[pl.ds(pl.program_id(0), 1), :])
    for out_ref, (other, starts) in zip(outs, plan):
        half = 1 - place_ref[0] if other else place_ref[0]
        start = starts[0] + (starts[1] - starts[0]) * half
        for z in range(0, out_ref.shape[1], 2):
            out_ref[0, z], out_ref[0, z + 1] = two_rows(left, raw_ref[0, start + z], raw_ref[0, start + z + 1])


def resample(place, weights, offsets, raw, counts, plan):
    views, depth, rows, width = raw.shape
    block = lambda planes: pl.BlockSpec((1, planes, rows, width), lambda v: (v, 0, 0, 0))
    return pl.pallas_call(
        functools.partial(resample_kernel, plan),
        grid=(views,),
        out_shape=[jax.ShapeDtypeStruct((views, count, rows, width), jnp.bfloat16) for count in counts],
        in_specs=[
            SMEM,
            pl.BlockSpec((1, weights.shape[2], rows), lambda v: (v, 0, 0)),
            VMEM,
            block(depth),
        ],
        out_specs=[block(count) for count in counts],
        compiler_params=PARAMS,
    )(place, weights.transpose(0, 2, 1), offsets, raw)


def bands_kernel(taps_ref, left_ref, right_ref):
    view = pl.program_id(0)
    count = taps_ref.shape[2]
    rows, width = left_ref.shape[2], right_ref.shape[2]

    def band(size, axis, way):
        shape = (size, size)
        shift = lax.broadcasted_iota(jnp.int32, shape, 0) - lax.broadcasted_iota(jnp.int32, shape, 1)
        total = jnp.zeros(shape, jnp.float32)
        for t in range(count):
            at = t - count // 2
            total = jnp.where(shift == (-at if way else at), taps_ref[view, axis, t], total)
        return halves(total)

    for way in range(2):
        high, low = band(rows, 1, 1 - way)
        left_ref[0, way] = jnp.concatenate([high, high, low], axis=1)
        right_ref[0, way] = jnp.concatenate(band(width, 2, way), axis=1)


def bands(taps, rows, width):
    views = taps.shape[0]
    shapes = [(2, rows, 3 * rows), (2, width, 2 * width)]
    return pl.pallas_call(
        bands_kernel,
        grid=(views,),
        out_shape=[jax.ShapeDtypeStruct((views,) + shape, jnp.bfloat16) for shape in shapes],
        in_specs=[SMEM],
        out_specs=[pl.BlockSpec((1,) + shape, lambda v: (v, 0, 0, 0)) for shape in shapes],
        compiler_params=PARAMS,
    )(taps)


def gather_kernel(views, planes, rim, place_ref, *refs):
    partial_ref = None
    if views is not None:
        partial_ref, refs = refs[0], refs[1:]
    groups = 2
    inner, bound, edge = refs[:groups], refs[groups : 2 * groups], refs[2 * groups : 3 * groups]
    bricks_ref, start_ref = refs[3 * groups : 3 * groups + 2]
    window = refs[-1]
    step = pl.program_id(0)
    half, core = place_ref[0], place_ref[1]
    main = inner[0].shape[1]

    @pl.when(step == 0)
    def _():
        start_ref[...] = jnp.zeros_like(start_ref) if partial_ref is None else partial_ref[...]

    for group in range(groups):
        for z in range(main):
            window[group, 2 * rim * (1 - half) + z] = inner[group][0, z]
        for z in range(rim):
            window[group, rim + (main - rim) * half + z] = bound[group][0, z]
            window[group, (main + rim) * half + z] = edge[group][0, z]
    for z in range(planes + 2 * rim):
        total = start_ref[z]
        for group in range(groups):
            plane = window[group, planes * core + z]
            bricks_ref[group, 0, z] = plane
            total = total + plane.astype(jnp.float32)
        start_ref[z] = total

    if views is not None:
        near_ref, cross_ref = refs[3 * groups + 2 : 3 * groups + 4]

        @pl.when(step == pl.num_programs(0) - 1)
        def _():
            start_ref[...] = start_ref[...] / views
            for z in range(rim):
                upward, downward = rim + planes - 2 * rim + z, 2 * rim + z
                near_ref[z] = start_ref[upward + (downward - upward) * core]
                cross_ref[z] = start_ref[downward + (upward - downward) * core]


def gather_views(place, inner, bound, edge, planes, side, views=None, partial=None):
    groups = len(inner)
    count, main, rows, width = inner[0].shape
    rim = edge[0].shape[1]
    take = lambda part: 0 if part.shape[0] == count else side * count
    outer = planes + 2 * rim
    field = lambda depth: jax.ShapeDtypeStruct((depth, rows, width), jnp.float32)
    sends = [] if views is None else [field(rim), field(rim)]
    parts = [*inner, *bound, *edge]
    return pl.pallas_call(
        functools.partial(gather_kernel, views, planes, rim),
        grid=(count,),
        out_shape=[jax.ShapeDtypeStruct((groups, count, outer, rows, width), jnp.bfloat16), field(outer)] + sends,
        in_specs=[SMEM]
        + ([] if partial is None else [VMEM])
        + [pl.BlockSpec((1,) + part.shape[1:], lambda v, base=take(part): (v + base, 0, 0, 0)) for part in parts],
        out_specs=[pl.BlockSpec((groups, 1, outer, rows, width), lambda v: (0, v, 0, 0, 0))]
        + [VMEM] * (1 + len(sends)),
        scratch_shapes=[pltpu.VMEM((groups, main + 2 * rim, rows, width), jnp.bfloat16)],
        compiler_params=PARAMS,
    )(place, *([] if partial is None else [partial]), *parts)


def update_kernel(paired, place_ref, taps_ref, lefts_ref, rights_ref, *refs):
    bricks_refs, (first_ref, own_ref, second_ref, out_ref) = refs[:2], refs[2:6]
    volume, ratios, held, logs = refs[6:]
    bricks = [ref.at[group] for ref in bricks_refs for group in range(ref.shape[0])]
    count = len(bricks)
    step = pl.program_id(0)
    taps = taps_ref.shape[2]
    rim = taps // 2
    planes, rows, width = out_ref.shape
    outer = planes + 2 * rim

    @pl.when(step == 0)
    def _():
        logs[...] = jnp.zeros_like(logs)
        side, middle = first_ref.shape[0], own_ref.shape[0]
        flip = 1 - place_ref[1] if paired else 0
        for z in range(side):
            volume[(side + middle) * flip + z] = first_ref[z]
            volume[(side + middle) * (1 - flip) + z] = second_ref[z]
        for z in range(middle):
            volume[side + z] = own_ref[z]

    def along_z(source, gains, z, length):
        sums = [[] for _ in range(length)]
        for k in range(0, rows, 8):
            column = [source[z + t, pl.ds(k, 8), :] for t in range(length + 2 * rim)]
            for i in range(length):
                total = column[i + rim]
                for t in range(taps):
                    if t != rim:
                        total = total + gains[t] * column[i + t]
                sums[i].append(total)
        return [jnp.concatenate(tiles, axis=0) for tiles in sums]

    def chain(source, gains, left, right, z, length):
        fields = along_z(source, gains, z, length)
        flats = []
        for i in range(0, length, 2):
            high, low = halves(jnp.concatenate(fields[i : i + 2], axis=1))
            stacked = jnp.concatenate([high, low, high], axis=0)
            parts = halves(jnp.dot(left, stacked, preferred_element_type=jnp.float32))
            for j in range(2):
                flats.append(jnp.concatenate([part[:, j * width : (j + 1) * width] for part in parts], axis=1))
        right = jnp.concatenate(
            [right, jnp.concatenate([right[:, :width], jnp.zeros((width, width), jnp.bfloat16)], axis=1)], axis=0
        )
        product = jnp.dot(jnp.concatenate(flats, axis=0), right, preferred_element_type=jnp.float32)
        total = product[:, :width] + product[:, width:]
        return [total[i * rows : (i + 1) * rows] for i in range(length)]

    def chunks(length):
        size = 2 if length % 4 else 4
        return [(z, size) for z in range(0, length, size)]

    for group in range(count):
        view = group * pl.num_programs(0) + step
        ratio = ratios.at[group % 2]
        gains = [taps_ref[view, 0, t] for t in range(taps)]
        for z, size in chunks(outer):
            fields = chain(volume, gains, lefts_ref[group, 0, 0], rights_ref[group, 0, 0], z, size)
            for i, blurred in enumerate(fields):
                guess = pl.reciprocal(blurred, approx=True)
                guess = guess * (2.0 - blurred * guess)
                ratio[z + i] = bricks[group][0, z + i].astype(jnp.float32) * guess
        for z, size in chunks(planes):
            fields = chain(ratio, gains[::-1], lefts_ref[group, 0, 1], rights_ref[group, 0, 1], z, size)
            for i, back in enumerate(fields):
                if group % 2 == 0:
                    held[z + i] = back
                else:
                    logs[z + i] += jnp.log(held[z + i] * back)

    @pl.when(step == pl.num_programs(0) - 1)
    def _():
        for z in range(planes):
            out_ref[z] = volume[2 * rim + z] * jnp.exp(logs[z] / (count * pl.num_programs(0)))


def update(place, taps, band, bricks, halo, own, planes, paired):
    _, count, outer, rows, width = bricks[0].shape
    groups = sum(part.shape[0] for part in bricks)
    band = [part.reshape((groups, count) + part.shape[1:]) for part in band]
    step = lambda v: (0, v, 0, 0, 0)
    return pl.pallas_call(
        functools.partial(update_kernel, paired),
        grid=(count,),
        out_shape=jax.ShapeDtypeStruct((planes, rows, width), jnp.float32),
        in_specs=[SMEM, SMEM]
        + [pl.BlockSpec((groups, 1) + part.shape[2:], step) for part in band]
        + [pl.BlockSpec((part.shape[0], 1, outer, rows, width), step) for part in bricks]
        + [VMEM] * 3,
        out_specs=VMEM,
        scratch_shapes=[
            pltpu.VMEM((2 * outer - planes, rows, width), jnp.float32),
            pltpu.VMEM((2, outer, rows, width), jnp.float32),
            pltpu.VMEM((planes, rows, width), jnp.float32),
            pltpu.VMEM((planes, rows, width), jnp.float32),
        ],
        compiler_params=PARAMS,
    )(place, taps, *band, *bricks, halo[0], own, halo[1])


def place_kernel(planes, place_ref, *refs):
    parts, out_ref = refs[:-1], refs[-1]
    blocks, members = out_ref.shape[:2]
    slot = place_ref[0]
    for index, part in enumerate(parts):
        for block in range(blocks):
            at = slot ^ index
            at = members - 1 - at if block % 2 else at
            out_ref[block, at] = part[block * planes : (block + 1) * planes]


def place_parts(slot, parts, planes):
    depth, rows, width = parts[0].shape
    return pl.pallas_call(
        functools.partial(place_kernel, planes),
        out_shape=jax.ShapeDtypeStruct((depth // planes, len(parts), planes, rows, width), jnp.float32),
        in_specs=[SMEM] + [VMEM] * len(parts),
        out_specs=VMEM,
        compiler_params=PARAMS,
    )(slot, *parts)


def partner(value, bit, members):
    return lax.ppermute(value, "view", [(i, i ^ bit) for i in range(members)])


def line_device(line, members, blocks):
    block, slab = divmod(line, members)
    return (members - 1 - slab if block % 2 else slab) * blocks + block


def swap(value, pairs, members, blocks):
    at = lambda line: line_device(line, members, blocks)
    perm = [(at(i), at(j)) for i, j in pairs] + [(at(j), at(i)) for i, j in pairs]
    return lax.ppermute(value, ("view", "vol"), perm)


def z_rims(own, inner, outer, members, blocks):
    planes = own.shape[0]
    at = lambda line: line_device(line, members, blocks)
    total = members * blocks
    before, after = [], []
    for hop in range(inner // planes + 1, -(-outer // planes) + 1):
        near, far = max((hop - 1) * planes, inner), min(hop * planes, outer)
        up = [(at(i), at(i + hop)) for i in range(total - hop)]
        down = [(at(i + hop), at(i)) for i in range(total - hop)]
        before.append(lax.ppermute(own[hop * planes - far : hop * planes - near], ("view", "vol"), up))
        after.append(lax.ppermute(own[near - (hop - 1) * planes : far - (hop - 1) * planes], ("view", "vol"), down))
    join = lambda parts: parts[0] if len(parts) == 1 else jnp.concatenate(parts)
    return join(before[::-1]), join(after)


def per_device(raw_views, weights, offsets, psf_taps):
    views, depth, rows, width = raw_views.shape
    members, blocks = lax.axis_size("view"), lax.axis_size("vol")
    rim = (psf_taps.shape[2] - 1) // 2
    planes = depth // members
    me = lax.axis_index("view")
    odd = lax.axis_index("vol") % 2
    slab = jnp.where(odd == 1, members - 1 - me, me)
    place = jnp.stack([slab // CORES, slab % CORES]).astype(jnp.int32)

    near_bit, far_bit = 1, CORES
    near = lambda value: partner(value, near_bit, members)
    far = lambda value: partner(value, far_bit, members)
    seams = [(members * block + members - 1 - i, members * (block + 1) + i) for block in range(blocks - 1) for i in range(CORES)]
    across = lambda value: swap(value, seams, members, blocks)
    bound, inner = (0, depth - rim), (rim, 2 * planes - rim)

    cross_taps = partner(psf_taps, near_bit + far_bit, members)
    far_bound = resample_bound(place, weights, offsets, raw_views, rim)
    far_bound, raw_later, cross_taps = lax.optimization_barrier((far_bound, raw_views, cross_taps))
    far_bound = far(far_bound)
    far_inner, own_bound, own_inner = resample(
        place,
        weights,
        offsets,
        raw_later,
        (2 * planes, rim, 2 * planes),
        [(True, inner), (False, bound), (False, inner)],
    )
    far_inner, cross_taps = lax.optimization_barrier((far_inner, cross_taps))
    far_inner = far(far_inner)
    near_inner = near(own_inner)
    pair_taps = near(jnp.stack([psf_taps, cross_taps]))
    all_taps = jnp.concatenate([psf_taps, pair_taps[0], pair_taps[1], cross_taps])
    all_taps = all_taps / jnp.sum(all_taps, axis=-1, keepdims=True)
    centre = all_taps[:, :1, rim : rim + 1]
    all_taps = jnp.concatenate([all_taps[:, :1] / centre, all_taps[:, 1:2], all_taps[:, 2:] * centre], axis=1)
    band = bands(all_taps, rows, width)
    bounds = jnp.concatenate([own_bound, far_bound])
    edges = across(bounds)
    edges, band = lax.optimization_barrier((edges, band))
    bounds, edges = [bounds, near(bounds)], [edges, near(edges)]
    home, partial = gather_views(place, [own_inner, near_inner], bounds, edges, planes, 0)
    far_inner, home, partial = lax.optimization_barrier((far_inner, home, partial))
    away, start, near_send, cross_send = gather_views(
        place, [far_inner, near(far_inner)], bounds, edges, planes, 1, members * views, partial
    )
    bricks = [home, away]
    lines = members * blocks
    gaps = [(i, i + 1) for i in range(1, lines - 1, 2)]
    paired = planes == 2 * rim
    if paired:
        halo = (near(near_send), swap(cross_send, gaps, members, blocks))
    else:
        halo = z_rims(start[rim : rim + planes], rim, 2 * rim, members, blocks)
    joined = update(place, all_taps, band, bricks, halo, start, planes, paired)
    for turn in range(1, ITERS):
        if paired:
            halo = (near(joined), swap(joined, gaps, members, blocks))
        else:
            halo = z_rims(joined, 0, 2 * rim, members, blocks)
        joined = update(place, all_taps, band, bricks, halo, joined, planes, paired)

    columns = lax.all_to_all(joined, "vol", split_axis=1, concat_axis=0, tiled=True)
    far_columns = far(columns)
    parts = [columns, near(columns), far_columns, near(far_columns)]
    result = place_parts(me.reshape(1).astype(jnp.int32), parts, planes)
    return result.reshape((blocks * depth,) + columns.shape[1:])


def solution(mesh):
    placed = (
        P("view", "vol", None, None),
        P("view", None, None),
        P("view", None),
        P("view", None, None),
    )
    return jax.shard_map(
        per_device, mesh=mesh, in_specs=placed, out_specs=P(None, "vol", None), check_vma=False
    )
```

```python
import functools

import jax
import jax.numpy as jnp
from jax import lax
from jax.experimental import pallas as pl
from jax.experimental.pallas import tpu as pltpu
from jax.sharding import PartitionSpec as P

ITERS = 2
CORES = 2
VMEM = pl.BlockSpec(memory_space=pltpu.VMEM)
SMEM = pl.BlockSpec(memory_space=pltpu.SMEM)
PARAMS = pltpu.CompilerParams(vmem_limit_bytes=24 * 1024 * 1024)


def halves(value):
    high = value.astype(jnp.bfloat16)
    low = (value - high.astype(jnp.float32)).astype(jnp.bfloat16)
    return high, low


def slab_index():
    me, odd = lax.axis_index("view"), lax.axis_index("vol") % 2
    return me + odd * (lax.axis_size("view") - 1 - 2 * me)


def row_matrix(weights, first):
    band, rows = weights.shape
    weights = weights / jnp.sum(weights, axis=0, keepdims=True)
    source = lax.broadcasted_iota(jnp.int32, (rows, rows), 0)
    matrix = jnp.zeros((rows, rows), jnp.float32)
    for k in range(band):
        matrix = jnp.where(source == first + k, weights[k : k + 1, :], matrix)
    matrix = matrix.T
    high = matrix.astype(jnp.bfloat16)
    rest = matrix - high.astype(jnp.float32)
    middle = rest.astype(jnp.bfloat16)
    low = (rest - middle.astype(jnp.float32)).astype(jnp.bfloat16)
    return jnp.concatenate([high, middle, low], axis=1)


def two_rows(left, first, second):
    planes = jnp.concatenate([first, second], axis=1)
    planes = jnp.concatenate([planes, planes, planes], axis=0)
    total = jnp.dot(left, planes, preferred_element_type=jnp.float32).astype(jnp.bfloat16)
    width = first.shape[1]
    return total[:, :width], total[:, width:]


def bound_kernel(weights_hbm, offsets_hbm, raw_hbm, out_ref, weights_ref, offsets_ref, planes_ref, sems):
    view = pl.program_id(0)
    depth, rim = raw_hbm.shape[1], out_ref.shape[1]

    @pl.when(view == 0)
    def _():
        start = (depth - rim) * (1 - slab_index() // CORES)
        pairs = [(weights_hbm, weights_ref), (offsets_hbm, offsets_ref), (raw_hbm.at[:, pl.ds(start, rim)], planes_ref)]
        copies = [pltpu.make_async_copy(*pair, sems.at[i]) for i, pair in enumerate(pairs)]
        for copy in copies:
            copy.start()
        for copy in copies:
            copy.wait()

    left = row_matrix(weights_ref[view], offsets_ref[pl.ds(view, 1), :])
    for z in range(0, rim, 2):
        out_ref[0, z], out_ref[0, z + 1] = two_rows(left, planes_ref[view, z], planes_ref[view, z + 1])


def resample_bound(weights, offsets, raw, rim):
    views, _, rows, width = raw.shape
    shape = (views, rim, rows, width)
    weights = weights.transpose(0, 2, 1)
    return pl.pallas_call(
        bound_kernel,
        grid=(views,),
        out_shape=jax.ShapeDtypeStruct(shape, jnp.bfloat16),
        in_specs=[pl.BlockSpec(memory_space=pltpu.HBM)] * 3,
        out_specs=pl.BlockSpec((1,) + shape[1:], lambda v: (v, 0, 0, 0)),
        scratch_shapes=[
            pltpu.VMEM(weights.shape, jnp.float32),
            pltpu.VMEM(offsets.shape, jnp.int32),
            pltpu.VMEM(shape, jnp.bfloat16),
            pltpu.SemaphoreType.DMA((3,)),
        ],
        compiler_params=pltpu.CompilerParams(vmem_limit_bytes=63 * 1024 * 1024),
    )(weights, offsets, raw)


def resample_kernel(plan, place_ref, weights_ref, offsets_ref, raw_ref, *outs):
    left = row_matrix(weights_ref[0], offsets_ref[pl.ds(pl.program_id(0), 1), :])
    for out_ref, (other, starts) in zip(outs, plan):
        half = 1 - place_ref[0] if other else place_ref[0]
        start = starts[0] + (starts[1] - starts[0]) * half
        for z in range(0, out_ref.shape[1], 2):
            out_ref[0, z], out_ref[0, z + 1] = two_rows(left, raw_ref[0, start + z], raw_ref[0, start + z + 1])


def resample(place, weights, offsets, raw, counts, plan):
    views, depth, rows, width = raw.shape
    block = lambda planes: pl.BlockSpec((1, planes, rows, width), lambda v: (v, 0, 0, 0))
    return pl.pallas_call(
        functools.partial(resample_kernel, plan),
        grid=(views,),
        out_shape=[jax.ShapeDtypeStruct((views, count, rows, width), jnp.bfloat16) for count in counts],
        in_specs=[
            SMEM,
            pl.BlockSpec((1, weights.shape[2], rows), lambda v: (v, 0, 0)),
            VMEM,
            block(depth),
        ],
        out_specs=[block(count) for count in counts],
        compiler_params=PARAMS,
    )(place, weights.transpose(0, 2, 1), offsets, raw)


def bands_kernel(taps_ref, left_ref, right_ref):
    view = pl.program_id(0)
    count = taps_ref.shape[2]
    rows, width = left_ref.shape[2], right_ref.shape[2]

    def band(size, axis, way):
        shape = (size, size)
        shift = lax.broadcasted_iota(jnp.int32, shape, 0) - lax.broadcasted_iota(jnp.int32, shape, 1)
        total = jnp.zeros(shape, jnp.float32)
        for t in range(count):
            at = t - count // 2
            total = jnp.where(shift == (-at if way else at), taps_ref[view, axis, t], total)
        return halves(total)

    for way in range(2):
        high, low = band(rows, 1, 1 - way)
        left_ref[0, way] = jnp.concatenate([high, high, low], axis=1)
        right_ref[0, way] = jnp.concatenate(band(width, 2, way), axis=1)


def bands(taps, rows, width):
    views = taps.shape[0]
    shapes = [(2, rows, 3 * rows), (2, width, 2 * width)]
    return pl.pallas_call(
        bands_kernel,
        grid=(views,),
        out_shape=[jax.ShapeDtypeStruct((views,) + shape, jnp.bfloat16) for shape in shapes],
        in_specs=[SMEM],
        out_specs=[pl.BlockSpec((1,) + shape, lambda v: (v, 0, 0, 0)) for shape in shapes],
        compiler_params=PARAMS,
    )(taps)


def gather_kernel(views, planes, rim, place_ref, *refs):
    partial_ref = None
    if views is not None:
        partial_ref, refs = refs[0], refs[1:]
    groups = 2
    extra = 2 if views is None else 4
    inner, (bound, edge) = refs[: -2 * groups - extra - 1], [
        refs[i - groups - extra - 1 : i - extra - 1] for i in (-groups, 0)
    ]
    pieces = len(inner) // groups
    bricks_ref, start_ref = refs[-extra - 1 : 1 - extra]
    window = refs[-1]
    step = pl.program_id(0)
    half, core = place_ref[0], place_ref[1]
    piece = inner[0].shape[1]
    main = pieces * piece

    @pl.when(step == 0)
    def _():
        start_ref[...] = jnp.zeros_like(start_ref) if partial_ref is None else partial_ref[...]

    for group in range(groups):
        for z in range(main):
            window[group, 2 * rim * (1 - half) + z] = inner[group * pieces + z // piece][0, z % piece]
        for z in range(rim):
            window[group, rim + (main - rim) * half + z] = bound[group][0, z]
            window[group, (main + rim) * half + z] = edge[group][0, z]
    for z in range(planes + 2 * rim):
        total = start_ref[z]
        for group in range(groups):
            plane = window[group, planes * core + z]
            bricks_ref[group, 0, z] = plane
            total = total + plane.astype(jnp.float32)
        start_ref[z] = total

    if views is not None:
        near_ref, cross_ref = refs[-3:-1]

        @pl.when(step == pl.num_programs(0) - 1)
        def _():
            start_ref[...] = start_ref[...] / views
            for z in range(rim):
                upward, downward = rim + planes - 2 * rim + z, 2 * rim + z
                near_ref[z] = start_ref[upward + (downward - upward) * core]
                cross_ref[z] = start_ref[downward + (upward - downward) * core]


def gather_views(place, inner, bound, edge, planes, side, views=None, partial=None):
    groups = len(bound)
    count, main, rows, width = inner[0].shape
    main = main * len(inner) // groups
    rim = edge[0].shape[1]
    take = lambda part: 0 if part.shape[0] == count else side * count
    outer = planes + 2 * rim
    field = lambda depth: jax.ShapeDtypeStruct((depth, rows, width), jnp.float32)
    sends = [] if views is None else [field(rim), field(rim)]
    parts = [*inner, *bound, *edge]
    return pl.pallas_call(
        functools.partial(gather_kernel, views, planes, rim),
        grid=(count,),
        out_shape=[jax.ShapeDtypeStruct((groups, count, outer, rows, width), jnp.bfloat16), field(outer)] + sends,
        in_specs=[SMEM]
        + ([] if partial is None else [VMEM])
        + [pl.BlockSpec((1,) + part.shape[1:], lambda v, base=take(part): (v + base, 0, 0, 0)) for part in parts],
        out_specs=[pl.BlockSpec((groups, 1, outer, rows, width), lambda v: (0, v, 0, 0, 0))]
        + [VMEM] * (1 + len(sends)),
        scratch_shapes=[pltpu.VMEM((groups, main + 2 * rim, rows, width), jnp.bfloat16)],
        compiler_params=PARAMS,
    )(place, *([] if partial is None else [partial]), *parts)


def update_kernel(paired, place_ref, taps_ref, lefts_ref, rights_ref, *refs):
    bricks_refs, (first_ref, own_ref, second_ref, out_ref) = refs[:2], refs[2:6]
    volume, ratios, logs = refs[6:]
    bricks = [ref.at[group] for ref in bricks_refs for group in range(ref.shape[0])]
    count = len(bricks)
    step = pl.program_id(0)
    taps = taps_ref.shape[2]
    rim = taps // 2
    planes, rows, width = out_ref.shape
    outer = planes + 2 * rim

    @pl.when(step == 0)
    def _():
        logs[...] = jnp.zeros_like(logs)
        side, middle = first_ref.shape[0], own_ref.shape[0]
        flip = 1 - place_ref[1] if paired else 0
        for z in range(side):
            volume[(side + middle) * flip + z] = first_ref[z]
            volume[(side + middle) * (1 - flip) + z] = second_ref[z]
        for z in range(middle):
            volume[side + z] = own_ref[z]

    def along_z(source, gains, z, length):
        sums = [[] for _ in range(length)]
        for k in range(0, rows, 8):
            column = [source[z + t, pl.ds(k, 8), :] for t in range(length + 2 * rim)]
            for i in range(length):
                total = column[i + rim]
                for t in range(taps):
                    if t != rim:
                        total = total + gains[t] * column[i + t]
                sums[i].append(total)
        return [jnp.concatenate(tiles, axis=0) for tiles in sums]

    def chain(source, gains, left, right, z, length):
        fields = along_z(source, gains, z, length)
        flats = []
        for i in range(0, length, 2):
            high, low = halves(jnp.concatenate(fields[i : i + 2], axis=1))
            stacked = jnp.concatenate([high, low, high], axis=0)
            parts = halves(jnp.dot(left, stacked, preferred_element_type=jnp.float32))
            for j in range(2):
                flats.append(jnp.concatenate([part[:, j * width : (j + 1) * width] for part in parts], axis=1))
        right = jnp.concatenate(
            [right, jnp.concatenate([right[:, :width], jnp.zeros((width, width), jnp.bfloat16)], axis=1)], axis=0
        )
        product = jnp.dot(jnp.concatenate(flats, axis=0), right, preferred_element_type=jnp.float32)
        total = product[:, :width] + product[:, width:]
        return [total[i * rows : (i + 1) * rows] for i in range(length)]

    def chunks(length):
        size = 2 if length % 4 else 4
        return [(z, size) for z in range(0, length, size)]

    for first in range(0, count, 2):
        pair = (first, first + 1)
        gains = [[taps_ref[group * pl.num_programs(0) + step, 0, t] for t in range(taps)] for group in pair]
        for z, size in chunks(outer):
            for group, gain in zip(pair, gains):
                fields = chain(volume, gain, lefts_ref[group, 0, 0], rights_ref[group, 0, 0], z, size)
                for i, blurred in enumerate(fields):
                    guess = pl.reciprocal(blurred, approx=True)
                    guess = guess * (2.0 - blurred * guess)
                    ratios[group, z + i] = bricks[group][0, z + i].astype(jnp.float32) * guess
        for z, size in chunks(planes):
            backs = [
                chain(ratios.at[group], gain[::-1], lefts_ref[group, 0, 1], rights_ref[group, 0, 1], z, size)
                for group, gain in zip(pair, gains)
            ]
            for i in range(size):
                logs[z + i] += jnp.log(backs[0][i] * backs[1][i])

    @pl.when(step == pl.num_programs(0) - 1)
    def _():
        for z in range(planes):
            out_ref[z] = volume[2 * rim + z] * jnp.exp(logs[z] / (count * pl.num_programs(0)))


def update(place, taps, band, bricks, halo, own, planes, paired):
    _, count, outer, rows, width = bricks[0].shape
    groups = sum(part.shape[0] for part in bricks)
    band = [part.reshape((groups, count) + part.shape[1:]) for part in band]
    step = lambda v: (0, v, 0, 0, 0)
    return pl.pallas_call(
        functools.partial(update_kernel, paired),
        grid=(count,),
        out_shape=jax.ShapeDtypeStruct((planes, rows, width), jnp.float32),
        in_specs=[SMEM, SMEM]
        + [pl.BlockSpec((groups, 1) + part.shape[2:], step) for part in band]
        + [pl.BlockSpec((part.shape[0], 1, outer, rows, width), step) for part in bricks]
        + [VMEM] * 3,
        out_specs=VMEM,
        scratch_shapes=[
            pltpu.VMEM((2 * outer - planes, rows, width), jnp.float32),
            pltpu.VMEM((groups, outer, rows, width), jnp.float32),
            pltpu.VMEM((planes, rows, width), jnp.float32),
        ],
        compiler_params=PARAMS,
    )(place, taps, *band, *bricks, halo[0], own, halo[1])


def place_kernel(planes, place_ref, *refs):
    parts, out_ref = refs[:-1], refs[-1]
    blocks, members = out_ref.shape[:2]
    slot = place_ref[0]
    for index, part in enumerate(parts):
        for block in range(blocks):
            at = slot ^ index
            at = members - 1 - at if block % 2 else at
            out_ref[block, at] = part[block * planes : (block + 1) * planes]


def place_parts(slot, parts, planes):
    depth, rows, width = parts[0].shape
    return pl.pallas_call(
        functools.partial(place_kernel, planes),
        out_shape=jax.ShapeDtypeStruct((depth // planes, len(parts), planes, rows, width), jnp.float32),
        in_specs=[SMEM] + [VMEM] * len(parts),
        out_specs=VMEM,
        compiler_params=PARAMS,
    )(slot, *parts)


def partner(value, bit, members):
    return lax.ppermute(value, "view", [(i, i ^ bit) for i in range(members)])


def line_device(line, members, blocks):
    block, slab = divmod(line, members)
    return (members - 1 - slab if block % 2 else slab) * blocks + block


def swap(value, pairs, members, blocks):
    at = lambda line: line_device(line, members, blocks)
    perm = [(at(i), at(j)) for i, j in pairs] + [(at(j), at(i)) for i, j in pairs]
    return lax.ppermute(value, ("view", "vol"), perm)


def z_rims(own, inner, outer, members, blocks):
    planes = own.shape[0]
    at = lambda line: line_device(line, members, blocks)
    total = members * blocks
    before, after = [], []
    for hop in range(inner // planes + 1, -(-outer // planes) + 1):
        near, far = max((hop - 1) * planes, inner), min(hop * planes, outer)
        up = [(at(i), at(i + hop)) for i in range(total - hop)]
        down = [(at(i + hop), at(i)) for i in range(total - hop)]
        before.append(lax.ppermute(own[hop * planes - far : hop * planes - near], ("view", "vol"), up))
        after.append(lax.ppermute(own[near - (hop - 1) * planes : far - (hop - 1) * planes], ("view", "vol"), down))
    join = lambda parts: parts[0] if len(parts) == 1 else jnp.concatenate(parts)
    return join(before[::-1]), join(after)


def per_device(raw_views, weights, offsets, psf_taps):
    views, depth, rows, width = raw_views.shape
    members, blocks = lax.axis_size("view"), lax.axis_size("vol")
    rim = (psf_taps.shape[2] - 1) // 2
    planes = depth // members
    me = lax.axis_index("view")
    slab = slab_index()
    place = jnp.stack([slab // CORES, slab % CORES]).astype(jnp.int32)

    near_bit, far_bit = 1, CORES
    near = lambda value: partner(value, near_bit, members)
    far = lambda value: partner(value, far_bit, members)
    seams = [(members * block + members - 1 - i, members * (block + 1) + i) for block in range(blocks - 1) for i in range(CORES)]
    across = lambda value: swap(value, seams, members, blocks)
    bound, inner = (0, depth - rim), (rim, 2 * planes - rim)

    cross_taps = partner(psf_taps, near_bit + far_bit, members)
    far_bound = resample_bound(weights, offsets, raw_views, rim)
    far_bound, raw_later, cross_taps = lax.optimization_barrier((far_bound, raw_views, cross_taps))
    far_bound = far(far_bound)
    far_inner, own_bound, own_inner = resample(
        place,
        weights,
        offsets,
        raw_later,
        (2 * planes, rim, 2 * planes),
        [(True, inner), (False, bound), (False, inner)],
    )
    far_inner, cross_taps = lax.optimization_barrier((far_inner, cross_taps))
    far_inner = far(far_inner)
    near_inner = near(own_inner)
    pair_taps = near(jnp.stack([psf_taps, cross_taps]))
    all_taps = jnp.concatenate([psf_taps, pair_taps[0], pair_taps[1], cross_taps])
    all_taps = all_taps / jnp.sum(all_taps, axis=-1, keepdims=True)
    centre = all_taps[:, :1, rim : rim + 1]
    all_taps = jnp.concatenate([all_taps[:, :1] / centre, all_taps[:, 1:2], all_taps[:, 2:] * centre], axis=1)
    band = bands(all_taps, rows, width)
    bounds = jnp.concatenate([own_bound, far_bound])
    edges = across(bounds)
    edges, band = lax.optimization_barrier((edges, band))
    bounds, edges = [bounds, near(bounds)], [edges, near(edges)]
    home, partial = gather_views(place, [own_inner, near_inner], bounds, edges, planes, 0)
    far_inner, home, partial = lax.optimization_barrier((far_inner, home, partial))
    away, start, near_send, cross_send = gather_views(
        place, [far_inner, near(far_inner)], bounds, edges, planes, 1, members * views, partial
    )
    bricks = [home, away]
    lines = members * blocks
    gaps = [(i, i + 1) for i in range(1, lines - 1, 2)]
    paired = planes == 2 * rim
    if paired:
        halo = (near(near_send), swap(cross_send, gaps, members, blocks))
    else:
        halo = z_rims(start[rim : rim + planes], rim, 2 * rim, members, blocks)
    joined = update(place, all_taps, band, bricks, halo, start, planes, paired)
    for turn in range(1, ITERS):
        if paired:
            halo = (near(joined), swap(joined, gaps, members, blocks))
        else:
            halo = z_rims(joined, 0, 2 * rim, members, blocks)
        joined = update(place, all_taps, band, bricks, halo, joined, planes, paired)

    columns = lax.all_to_all(joined, "vol", split_axis=1, concat_axis=0, tiled=True)
    far_columns = far(columns)
    parts = [columns, near(columns), far_columns, near(far_columns)]
    result = place_parts(me.reshape(1).astype(jnp.int32), parts, planes)
    return result.reshape((blocks * depth,) + columns.shape[1:])


def solution(mesh):
    placed = (
        P("view", "vol", None, None),
        P("view", None, None),
        P("view", None),
        P("view", None, None),
    )
    return jax.shard_map(
        per_device, mesh=mesh, in_specs=placed, out_specs=P(None, "vol", None), check_vma=False
    )
```

```python
import functools

import jax
import jax.numpy as jnp
from jax import lax
from jax.experimental import pallas as pl
from jax.experimental.pallas import tpu as pltpu
from jax.sharding import PartitionSpec as P

ITERS = 2
CORES = 2
VMEM = pl.BlockSpec(memory_space=pltpu.VMEM)
SMEM = pl.BlockSpec(memory_space=pltpu.SMEM)
PARAMS = pltpu.CompilerParams(vmem_limit_bytes=24 * 1024 * 1024)


def halves(value):
    high = value.astype(jnp.bfloat16)
    low = (value - high.astype(jnp.float32)).astype(jnp.bfloat16)
    return high, low


def slab_index():
    me, odd = lax.axis_index("view"), lax.axis_index("vol") % 2
    return me + odd * (lax.axis_size("view") - 1 - 2 * me)


def row_matrix(weights, first):
    band, rows = weights.shape
    weights = weights / jnp.sum(weights, axis=0, keepdims=True)
    source = lax.broadcasted_iota(jnp.int32, (rows, rows), 0)
    matrix = jnp.zeros((rows, rows), jnp.float32)
    for k in range(band):
        matrix = jnp.where(source == first + k, weights[k : k + 1, :], matrix)
    matrix = matrix.T
    high = matrix.astype(jnp.bfloat16)
    rest = matrix - high.astype(jnp.float32)
    middle = rest.astype(jnp.bfloat16)
    low = (rest - middle.astype(jnp.float32)).astype(jnp.bfloat16)
    return jnp.concatenate([high, middle, low], axis=1)


def two_rows(left, first, second):
    planes = jnp.concatenate([first, second], axis=1)
    planes = jnp.concatenate([planes, planes, planes], axis=0)
    total = jnp.dot(left, planes, preferred_element_type=jnp.float32).astype(jnp.bfloat16)
    width = first.shape[1]
    return total[:, :width], total[:, width:]


def bound_kernel(weights_hbm, offsets_hbm, raw_hbm, out_ref, weights_ref, offsets_ref, planes_ref, sems):
    view = pl.program_id(0)
    depth, rim = raw_hbm.shape[1], out_ref.shape[1]

    @pl.when(view == 0)
    def _():
        start = (depth - rim) * (1 - slab_index() // CORES)
        pairs = [(weights_hbm, weights_ref), (offsets_hbm, offsets_ref), (raw_hbm.at[:, pl.ds(start, rim)], planes_ref)]
        copies = [pltpu.make_async_copy(*pair, sems.at[i]) for i, pair in enumerate(pairs)]
        for copy in copies:
            copy.start()
        for copy in copies:
            copy.wait()

    left = row_matrix(weights_ref[view], offsets_ref[pl.ds(view, 1), :])
    for z in range(0, rim, 2):
        out_ref[0, z], out_ref[0, z + 1] = two_rows(left, planes_ref[view, z], planes_ref[view, z + 1])


def resample_bound(weights, offsets, raw, rim):
    views, _, rows, width = raw.shape
    shape = (views, rim, rows, width)
    weights = weights.transpose(0, 2, 1)
    return pl.pallas_call(
        bound_kernel,
        grid=(views,),
        out_shape=jax.ShapeDtypeStruct(shape, jnp.bfloat16),
        in_specs=[pl.BlockSpec(memory_space=pltpu.HBM)] * 3,
        out_specs=pl.BlockSpec((1,) + shape[1:], lambda v: (v, 0, 0, 0)),
        scratch_shapes=[
            pltpu.VMEM(weights.shape, jnp.float32),
            pltpu.VMEM(offsets.shape, jnp.int32),
            pltpu.VMEM(shape, jnp.bfloat16),
            pltpu.SemaphoreType.DMA((3,)),
        ],
        compiler_params=pltpu.CompilerParams(vmem_limit_bytes=63 * 1024 * 1024),
    )(weights, offsets, raw)


def resample_kernel(plan, place_ref, weights_ref, offsets_ref, raw_ref, *outs):
    left = row_matrix(weights_ref[0], offsets_ref[pl.ds(pl.program_id(0), 1), :])
    for out_ref, (other, starts) in zip(outs, plan):
        half = 1 - place_ref[0] if other else place_ref[0]
        start = starts[0] + (starts[1] - starts[0]) * half
        for z in range(0, out_ref.shape[1], 2):
            out_ref[0, z], out_ref[0, z + 1] = two_rows(left, raw_ref[0, start + z], raw_ref[0, start + z + 1])


def resample(place, weights, offsets, raw, counts, plan):
    views, depth, rows, width = raw.shape
    block = lambda planes: pl.BlockSpec((1, planes, rows, width), lambda v: (v, 0, 0, 0))
    return pl.pallas_call(
        functools.partial(resample_kernel, plan),
        grid=(views,),
        out_shape=[jax.ShapeDtypeStruct((views, count, rows, width), jnp.bfloat16) for count in counts],
        in_specs=[
            SMEM,
            pl.BlockSpec((1, weights.shape[2], rows), lambda v: (v, 0, 0)),
            VMEM,
            block(depth),
        ],
        out_specs=[block(count) for count in counts],
        compiler_params=PARAMS,
    )(place, weights.transpose(0, 2, 1), offsets, raw)


def bands_kernel(taps_ref, left_ref, right_ref):
    view = pl.program_id(0)
    count = taps_ref.shape[2]
    rows, width = left_ref.shape[2], right_ref.shape[2]

    def band(size, axis, way):
        shape = (size, size)
        shift = lax.broadcasted_iota(jnp.int32, shape, 0) - lax.broadcasted_iota(jnp.int32, shape, 1)
        total = jnp.zeros(shape, jnp.float32)
        for t in range(count):
            at = t - count // 2
            total = jnp.where(shift == (-at if way else at), taps_ref[view, axis, t], total)
        return halves(total)

    for way in range(2):
        high, low = band(rows, 1, 1 - way)
        left_ref[0, way] = jnp.concatenate([high, high, low], axis=1)
        right_ref[0, way] = jnp.concatenate(band(width, 2, way), axis=1)


def bands(taps, rows, width):
    views = taps.shape[0]
    shapes = [(2, rows, 3 * rows), (2, width, 2 * width)]
    return pl.pallas_call(
        bands_kernel,
        grid=(views,),
        out_shape=[jax.ShapeDtypeStruct((views,) + shape, jnp.bfloat16) for shape in shapes],
        in_specs=[SMEM],
        out_specs=[pl.BlockSpec((1,) + shape, lambda v: (v, 0, 0, 0)) for shape in shapes],
        compiler_params=PARAMS,
    )(taps)


def gather_kernel(views, planes, rim, place_ref, *refs):
    partial_ref = None
    if views is not None:
        partial_ref, refs = refs[0], refs[1:]
    groups = 2
    extra = 2 if views is None else 4
    inner, (bound, edge) = refs[: -2 * groups - extra - 1], [
        refs[i - groups - extra - 1 : i - extra - 1] for i in (-groups, 0)
    ]
    pieces = len(inner) // groups
    bricks_ref, start_ref = refs[-extra - 1 : 1 - extra]
    window = refs[-1]
    step = pl.program_id(0)
    half, core = place_ref[0], place_ref[1]
    piece = inner[0].shape[1]
    main = pieces * piece

    @pl.when(step == 0)
    def _():
        start_ref[...] = jnp.zeros_like(start_ref) if partial_ref is None else partial_ref[...]

    for group in range(groups):
        for z in range(main):
            window[group, 2 * rim * (1 - half) + z] = inner[group * pieces + z // piece][0, z % piece]
        for z in range(rim):
            window[group, rim + (main - rim) * half + z] = bound[group][0, z]
            window[group, (main + rim) * half + z] = edge[group][0, z]
    for z in range(planes + 2 * rim):
        total = start_ref[z]
        for group in range(groups):
            plane = window[group, planes * core + z]
            bricks_ref[group, 0, z] = plane
            total = total + plane.astype(jnp.float32)
        start_ref[z] = total

    if views is not None:
        near_ref, cross_ref = refs[-3:-1]

        @pl.when(step == pl.num_programs(0) - 1)
        def _():
            start_ref[...] = start_ref[...] / views
            for z in range(rim):
                upward, downward = rim + planes - 2 * rim + z, 2 * rim + z
                near_ref[z] = start_ref[upward + (downward - upward) * core]
                cross_ref[z] = start_ref[downward + (upward - downward) * core]


def gather_views(place, inner, bound, edge, planes, side, views=None, partial=None):
    groups = len(bound)
    count, main, rows, width = inner[0].shape
    main = main * len(inner) // groups
    rim = edge[0].shape[1]
    take = lambda part: 0 if part.shape[0] == count else side * count
    outer = planes + 2 * rim
    field = lambda depth: jax.ShapeDtypeStruct((depth, rows, width), jnp.float32)
    sends = [] if views is None else [field(rim), field(rim)]
    parts = [*inner, *bound, *edge]
    return pl.pallas_call(
        functools.partial(gather_kernel, views, planes, rim),
        grid=(count,),
        out_shape=[jax.ShapeDtypeStruct((groups, count, outer, rows, width), jnp.bfloat16), field(outer)] + sends,
        in_specs=[SMEM]
        + ([] if partial is None else [VMEM])
        + [pl.BlockSpec((1,) + part.shape[1:], lambda v, base=take(part): (v + base, 0, 0, 0)) for part in parts],
        out_specs=[pl.BlockSpec((groups, 1, outer, rows, width), lambda v: (0, v, 0, 0, 0))]
        + [VMEM] * (1 + len(sends)),
        scratch_shapes=[pltpu.VMEM((groups, main + 2 * rim, rows, width), jnp.bfloat16)],
        compiler_params=PARAMS,
    )(place, *([] if partial is None else [partial]), *parts)


def update_kernel(paired, place_ref, taps_ref, lefts_ref, rights_ref, *refs):
    bricks_refs, (first_ref, own_ref, second_ref, out_ref) = refs[:2], refs[2:6]
    volume, ratios, logs = refs[6:]
    bricks = [ref.at[group] for ref in bricks_refs for group in range(ref.shape[0])]
    count = len(bricks)
    step = pl.program_id(0)
    taps = taps_ref.shape[2]
    rim = taps // 2
    planes, rows, width = out_ref.shape
    outer = planes + 2 * rim

    @pl.when(step == 0)
    def _():
        logs[...] = jnp.zeros_like(logs)
        side, middle = first_ref.shape[0], own_ref.shape[0]
        flip = 1 - place_ref[1] if paired else 0
        for z in range(side):
            volume[(side + middle) * flip + z] = first_ref[z]
            volume[(side + middle) * (1 - flip) + z] = second_ref[z]
        for z in range(middle):
            volume[side + z] = own_ref[z]

    def along_z(source, gains, z, length):
        sums = [[] for _ in range(length)]
        for k in range(0, rows, 8):
            column = [source[z + t, pl.ds(k, 8), :] for t in range(length + 2 * rim)]
            for i in range(length):
                total = column[i + rim]
                for t in range(taps):
                    if t != rim:
                        total = total + gains[t] * column[i + t]
                sums[i].append(total)
        return [jnp.concatenate(tiles, axis=0) for tiles in sums]

    def chain(source, gains, left, right, z, length):
        fields = along_z(source, gains, z, length)
        flats = []
        for i in range(0, length, 2):
            high, low = halves(jnp.concatenate(fields[i : i + 2], axis=1))
            stacked = jnp.concatenate([high, low, high], axis=0)
            parts = halves(jnp.dot(left, stacked, preferred_element_type=jnp.float32))
            for j in range(2):
                flats.append(jnp.concatenate([part[:, j * width : (j + 1) * width] for part in parts], axis=1))
        right = jnp.concatenate(
            [right, jnp.concatenate([right[:, :width], jnp.zeros((width, width), jnp.bfloat16)], axis=1)], axis=0
        )
        product = jnp.dot(jnp.concatenate(flats, axis=0), right, preferred_element_type=jnp.float32)
        total = product[:, :width] + product[:, width:]
        return [total[i * rows : (i + 1) * rows] for i in range(length)]

    def chunks(length):
        size = 2 if length % 4 else 4
        return [(z, size) for z in range(0, length, size)]

    gains = [[taps_ref[group * pl.num_programs(0) + step, 0, t] for t in range(taps)] for group in range(count)]
    for z, size in chunks(outer):
        for group, gain in enumerate(gains):
            fields = chain(volume, gain, lefts_ref[group, 0, 0], rights_ref[group, 0, 0], z, size)
            for i, blurred in enumerate(fields):
                guess = pl.reciprocal(blurred, approx=True)
                guess = guess * (2.0 - blurred * guess)
                ratios[group, z + i] = bricks[group][0, z + i].astype(jnp.float32) * guess
    for z, size in chunks(planes):
        for first in range(0, count, 2):
            backs = [
                chain(ratios.at[group], gains[group][::-1], lefts_ref[group, 0, 1], rights_ref[group, 0, 1], z, size)
                for group in (first, first + 1)
            ]
            for i in range(size):
                logs[z + i] += jnp.log(backs[0][i] * backs[1][i])

    @pl.when(step == pl.num_programs(0) - 1)
    def _():
        for z in range(planes):
            out_ref[z] = volume[2 * rim + z] * jnp.exp(logs[z] / (count * pl.num_programs(0)))


def update(place, taps, band, bricks, halo, own, planes, paired):
    _, count, outer, rows, width = bricks[0].shape
    groups = sum(part.shape[0] for part in bricks)
    band = [part.reshape((groups, count) + part.shape[1:]) for part in band]
    step = lambda v: (0, v, 0, 0, 0)
    return pl.pallas_call(
        functools.partial(update_kernel, paired),
        grid=(count,),
        out_shape=jax.ShapeDtypeStruct((planes, rows, width), jnp.float32),
        in_specs=[SMEM, SMEM]
        + [pl.BlockSpec((groups, 1) + part.shape[2:], step) for part in band]
        + [pl.BlockSpec((part.shape[0], 1, outer, rows, width), step) for part in bricks]
        + [VMEM] * 3,
        out_specs=VMEM,
        scratch_shapes=[
            pltpu.VMEM((2 * outer - planes, rows, width), jnp.float32),
            pltpu.VMEM((groups, outer, rows, width), jnp.float32),
            pltpu.VMEM((planes, rows, width), jnp.float32),
        ],
        compiler_params=PARAMS,
    )(place, taps, *band, *bricks, halo[0], own, halo[1])


def place_kernel(planes, place_ref, *refs):
    parts, out_ref = refs[:-1], refs[-1]
    blocks, members = out_ref.shape[:2]
    slot = place_ref[0]
    for index, part in enumerate(parts):
        for block in range(blocks):
            at = slot ^ index
            at = members - 1 - at if block % 2 else at
            out_ref[block, at] = part[block * planes : (block + 1) * planes]


def place_parts(slot, parts, planes):
    depth, rows, width = parts[0].shape
    return pl.pallas_call(
        functools.partial(place_kernel, planes),
        out_shape=jax.ShapeDtypeStruct((depth // planes, len(parts), planes, rows, width), jnp.float32),
        in_specs=[SMEM] + [VMEM] * len(parts),
        out_specs=VMEM,
        compiler_params=PARAMS,
    )(slot, *parts)


def partner(value, bit, members):
    return lax.ppermute(value, "view", [(i, i ^ bit) for i in range(members)])


def line_device(line, members, blocks):
    block, slab = divmod(line, members)
    return (members - 1 - slab if block % 2 else slab) * blocks + block


def swap(value, pairs, members, blocks):
    at = lambda line: line_device(line, members, blocks)
    perm = [(at(i), at(j)) for i, j in pairs] + [(at(j), at(i)) for i, j in pairs]
    return lax.ppermute(value, ("view", "vol"), perm)


def z_rims(own, inner, outer, members, blocks):
    planes = own.shape[0]
    at = lambda line: line_device(line, members, blocks)
    total = members * blocks
    before, after = [], []
    for hop in range(inner // planes + 1, -(-outer // planes) + 1):
        near, far = max((hop - 1) * planes, inner), min(hop * planes, outer)
        up = [(at(i), at(i + hop)) for i in range(total - hop)]
        down = [(at(i + hop), at(i)) for i in range(total - hop)]
        before.append(lax.ppermute(own[hop * planes - far : hop * planes - near], ("view", "vol"), up))
        after.append(lax.ppermute(own[near - (hop - 1) * planes : far - (hop - 1) * planes], ("view", "vol"), down))
    join = lambda parts: parts[0] if len(parts) == 1 else jnp.concatenate(parts)
    return join(before[::-1]), join(after)


def per_device(raw_views, weights, offsets, psf_taps):
    views, depth, rows, width = raw_views.shape
    members, blocks = lax.axis_size("view"), lax.axis_size("vol")
    rim = (psf_taps.shape[2] - 1) // 2
    planes = depth // members
    me = lax.axis_index("view")
    slab = slab_index()
    place = jnp.stack([slab // CORES, slab % CORES]).astype(jnp.int32)

    near_bit, far_bit = 1, CORES
    near = lambda value: partner(value, near_bit, members)
    far = lambda value: partner(value, far_bit, members)
    seams = [(members * block + members - 1 - i, members * (block + 1) + i) for block in range(blocks - 1) for i in range(CORES)]
    across = lambda value: swap(value, seams, members, blocks)
    bound, inner = (0, depth - rim), (rim, 2 * planes - rim)

    cross_taps = partner(psf_taps, near_bit + far_bit, members)
    far_bound = resample_bound(weights, offsets, raw_views, rim)
    far_bound, raw_later, cross_taps = lax.optimization_barrier((far_bound, raw_views, cross_taps))
    far_bound = far(far_bound)
    far_inner, own_bound, own_inner = resample(
        place,
        weights,
        offsets,
        raw_later,
        (2 * planes, rim, 2 * planes),
        [(True, inner), (False, bound), (False, inner)],
    )
    far_inner, cross_taps = lax.optimization_barrier((far_inner, cross_taps))
    far_inner = far(far_inner)
    near_inner = near(own_inner)
    pair_taps = near(jnp.stack([psf_taps, cross_taps]))
    all_taps = jnp.concatenate([psf_taps, pair_taps[0], pair_taps[1], cross_taps])
    all_taps = all_taps / jnp.sum(all_taps, axis=-1, keepdims=True)
    centre = all_taps[:, :1, rim : rim + 1]
    all_taps = jnp.concatenate([all_taps[:, :1] / centre, all_taps[:, 1:2], all_taps[:, 2:] * centre], axis=1)
    band = bands(all_taps, rows, width)
    bounds = jnp.concatenate([own_bound, far_bound])
    edges = across(bounds)
    edges, band = lax.optimization_barrier((edges, band))
    bounds, edges = [bounds, near(bounds)], [edges, near(edges)]
    home, partial = gather_views(place, [own_inner, near_inner], bounds, edges, planes, 0)
    far_inner, home, partial = lax.optimization_barrier((far_inner, home, partial))
    away, start, near_send, cross_send = gather_views(
        place, [far_inner, near(far_inner)], bounds, edges, planes, 1, members * views, partial
    )
    bricks = [home, away]
    lines = members * blocks
    gaps = [(i, i + 1) for i in range(1, lines - 1, 2)]
    paired = planes == 2 * rim
    if paired:
        halo = (near(near_send), swap(cross_send, gaps, members, blocks))
    else:
        halo = z_rims(start[rim : rim + planes], rim, 2 * rim, members, blocks)
    joined = update(place, all_taps, band, bricks, halo, start, planes, paired)
    for turn in range(1, ITERS):
        if paired:
            halo = (near(joined), swap(joined, gaps, members, blocks))
        else:
            halo = z_rims(joined, 0, 2 * rim, members, blocks)
        joined = update(place, all_taps, band, bricks, halo, joined, planes, paired)

    columns = lax.all_to_all(joined, "vol", split_axis=1, concat_axis=0, tiled=True)
    far_columns = far(columns)
    parts = [columns, near(columns), far_columns, near(far_columns)]
    result = place_parts(me.reshape(1).astype(jnp.int32), parts, planes)
    return result.reshape((blocks * depth,) + columns.shape[1:])


def solution(mesh):
    placed = (
        P("view", "vol", None, None),
        P("view", None, None),
        P("view", None),
        P("view", None, None),
    )
    return jax.shard_map(
        per_device, mesh=mesh, in_specs=placed, out_specs=P(None, "vol", None), check_vma=False
    )
```

```python
import functools

import jax
import jax.numpy as jnp
from jax import lax
from jax.experimental import pallas as pl
from jax.experimental.pallas import tpu as pltpu
from jax.sharding import PartitionSpec as P

ITERS = 2
CORES = 2
VMEM = pl.BlockSpec(memory_space=pltpu.VMEM)
SMEM = pl.BlockSpec(memory_space=pltpu.SMEM)
PARAMS = pltpu.CompilerParams(vmem_limit_bytes=24 * 1024 * 1024)


def halves(value):
    high = value.astype(jnp.bfloat16)
    low = (value - high.astype(jnp.float32)).astype(jnp.bfloat16)
    return high, low


def slab_index():
    me, odd = lax.axis_index("view"), lax.axis_index("vol") % 2
    return me + odd * (lax.axis_size("view") - 1 - 2 * me)


def row_matrix(weights, first):
    band, rows = weights.shape
    weights = weights / jnp.sum(weights, axis=0, keepdims=True)
    source = lax.broadcasted_iota(jnp.int32, (rows, rows), 0)
    matrix = jnp.zeros((rows, rows), jnp.float32)
    for k in range(band):
        matrix = jnp.where(source == first + k, weights[k : k + 1, :], matrix)
    matrix = matrix.T
    high = matrix.astype(jnp.bfloat16)
    rest = matrix - high.astype(jnp.float32)
    middle = rest.astype(jnp.bfloat16)
    low = (rest - middle.astype(jnp.float32)).astype(jnp.bfloat16)
    return jnp.concatenate([high, middle, low], axis=1)


def two_rows(left, first, second):
    planes = jnp.concatenate([first, second], axis=1)
    planes = jnp.concatenate([planes, planes, planes], axis=0)
    total = jnp.dot(left, planes, preferred_element_type=jnp.float32).astype(jnp.bfloat16)
    width = first.shape[1]
    return total[:, :width], total[:, width:]


def bound_kernel(weights_hbm, offsets_hbm, raw_hbm, out_ref, weights_ref, offsets_ref, planes_ref, sems):
    view = pl.program_id(0)
    depth, rim = raw_hbm.shape[1], out_ref.shape[1]

    @pl.when(view == 0)
    def _():
        start = (depth - rim) * (1 - slab_index() // CORES)
        pairs = [(weights_hbm, weights_ref), (offsets_hbm, offsets_ref), (raw_hbm.at[:, pl.ds(start, rim)], planes_ref)]
        copies = [pltpu.make_async_copy(*pair, sems.at[i]) for i, pair in enumerate(pairs)]
        for copy in copies:
            copy.start()
        for copy in copies:
            copy.wait()

    left = row_matrix(weights_ref[view], offsets_ref[pl.ds(view, 1), :])
    for z in range(0, rim, 2):
        out_ref[0, z], out_ref[0, z + 1] = two_rows(left, planes_ref[view, z], planes_ref[view, z + 1])


def resample_bound(weights, offsets, raw, rim):
    views, _, rows, width = raw.shape
    shape = (views, rim, rows, width)
    weights = weights.transpose(0, 2, 1)
    return pl.pallas_call(
        bound_kernel,
        grid=(views,),
        out_shape=jax.ShapeDtypeStruct(shape, jnp.bfloat16),
        in_specs=[pl.BlockSpec(memory_space=pltpu.HBM)] * 3,
        out_specs=pl.BlockSpec((1,) + shape[1:], lambda v: (v, 0, 0, 0)),
        scratch_shapes=[
            pltpu.VMEM(weights.shape, jnp.float32),
            pltpu.VMEM(offsets.shape, jnp.int32),
            pltpu.VMEM(shape, jnp.bfloat16),
            pltpu.SemaphoreType.DMA((3,)),
        ],
        compiler_params=pltpu.CompilerParams(vmem_limit_bytes=63 * 1024 * 1024),
    )(weights, offsets, raw)


def resample_kernel(plan, place_ref, weights_ref, offsets_ref, raw_ref, *outs):
    left = row_matrix(weights_ref[0], offsets_ref[pl.ds(pl.program_id(0), 1), :])
    for out_ref, (other, starts) in zip(outs, plan):
        half = 1 - place_ref[0] if other else place_ref[0]
        start = starts[0] + (starts[1] - starts[0]) * half
        for z in range(0, out_ref.shape[1], 2):
            out_ref[0, z], out_ref[0, z + 1] = two_rows(left, raw_ref[0, start + z], raw_ref[0, start + z + 1])


def resample(place, weights, offsets, raw, counts, plan):
    views, depth, rows, width = raw.shape
    block = lambda planes: pl.BlockSpec((1, planes, rows, width), lambda v: (v, 0, 0, 0))
    return pl.pallas_call(
        functools.partial(resample_kernel, plan),
        grid=(views,),
        out_shape=[jax.ShapeDtypeStruct((views, count, rows, width), jnp.bfloat16) for count in counts],
        in_specs=[
            SMEM,
            pl.BlockSpec((1, weights.shape[2], rows), lambda v: (v, 0, 0)),
            VMEM,
            block(depth),
        ],
        out_specs=[block(count) for count in counts],
        compiler_params=PARAMS,
    )(place, weights.transpose(0, 2, 1), offsets, raw)


def bands_kernel(taps_ref, left_ref, right_ref):
    view = pl.program_id(0)
    count = taps_ref.shape[2]
    rows, width = left_ref.shape[2], right_ref.shape[2]

    def band(size, axis, way):
        shape = (size, size)
        shift = lax.broadcasted_iota(jnp.int32, shape, 0) - lax.broadcasted_iota(jnp.int32, shape, 1)
        total = jnp.zeros(shape, jnp.float32)
        for t in range(count):
            at = t - count // 2
            total = jnp.where(shift == (-at if way else at), taps_ref[view, axis, t], total)
        return halves(total)

    for way in range(2):
        high, low = band(rows, 1, 1 - way)
        left_ref[0, way] = jnp.concatenate([high, high, low], axis=1)
        right_ref[0, way] = jnp.concatenate(band(width, 2, way), axis=1)


def bands(taps, rows, width):
    views = taps.shape[0]
    shapes = [(2, rows, 3 * rows), (2, width, 2 * width)]
    return pl.pallas_call(
        bands_kernel,
        grid=(views,),
        out_shape=[jax.ShapeDtypeStruct((views,) + shape, jnp.bfloat16) for shape in shapes],
        in_specs=[SMEM],
        out_specs=[pl.BlockSpec((1,) + shape, lambda v: (v, 0, 0, 0)) for shape in shapes],
        compiler_params=PARAMS,
    )(taps)


def gather_kernel(views, planes, rim, place_ref, *refs):
    partial_ref = None
    if views is not None:
        partial_ref, refs = refs[0], refs[1:]
    groups = 2
    extra = 2 if views is None else 4
    inner, (bound, edge) = refs[: -2 * groups - extra - 1], [
        refs[i - groups - extra - 1 : i - extra - 1] for i in (-groups, 0)
    ]
    pieces = len(inner) // groups
    bricks_ref, start_ref = refs[-extra - 1 : 1 - extra]
    window = refs[-1]
    step = pl.program_id(0)
    half, core = place_ref[0], place_ref[1]
    piece = inner[0].shape[1]
    main = pieces * piece

    @pl.when(step == 0)
    def _():
        start_ref[...] = jnp.zeros_like(start_ref) if partial_ref is None else partial_ref[...]

    for group in range(groups):
        for z in range(main):
            window[group, 2 * rim * (1 - half) + z] = inner[group * pieces + z // piece][0, z % piece]
        for z in range(rim):
            window[group, rim + (main - rim) * half + z] = bound[group][0, z]
            window[group, (main + rim) * half + z] = edge[group][0, z]
    for z in range(planes + 2 * rim):
        total = start_ref[z]
        for group in range(groups):
            plane = window[group, planes * core + z]
            bricks_ref[group, 0, z] = plane
            total = total + plane.astype(jnp.float32)
        start_ref[z] = total

    if views is not None:
        near_ref, cross_ref = refs[-3:-1]

        @pl.when(step == pl.num_programs(0) - 1)
        def _():
            start_ref[...] = start_ref[...] / views
            for z in range(rim):
                upward, downward = rim + planes - 2 * rim + z, 2 * rim + z
                near_ref[z] = start_ref[upward + (downward - upward) * core]
                cross_ref[z] = start_ref[downward + (upward - downward) * core]


def gather_views(place, inner, bound, edge, planes, side, views=None, partial=None):
    groups = len(bound)
    count, main, rows, width = inner[0].shape
    main = main * len(inner) // groups
    rim = edge[0].shape[1]
    take = lambda part: 0 if part.shape[0] == count else side * count
    outer = planes + 2 * rim
    field = lambda depth: jax.ShapeDtypeStruct((depth, rows, width), jnp.float32)
    sends = [] if views is None else [field(rim), field(rim)]
    parts = [*inner, *bound, *edge]
    return pl.pallas_call(
        functools.partial(gather_kernel, views, planes, rim),
        grid=(count,),
        out_shape=[jax.ShapeDtypeStruct((groups, count, outer, rows, width), jnp.bfloat16), field(outer)] + sends,
        in_specs=[SMEM]
        + ([] if partial is None else [VMEM])
        + [pl.BlockSpec((1,) + part.shape[1:], lambda v, base=take(part): (v + base, 0, 0, 0)) for part in parts],
        out_specs=[pl.BlockSpec((groups, 1, outer, rows, width), lambda v: (0, v, 0, 0, 0))]
        + [VMEM] * (1 + len(sends)),
        scratch_shapes=[pltpu.VMEM((groups, main + 2 * rim, rows, width), jnp.bfloat16)],
        compiler_params=PARAMS,
    )(place, *([] if partial is None else [partial]), *parts)


def update_kernel(paired, place_ref, taps_ref, lefts_ref, rights_ref, *refs):
    bricks_refs, (first_ref, own_ref, second_ref, out_ref) = refs[:2], refs[2:6]
    volume, ratios, logs = refs[6:]
    bricks = [ref.at[group] for ref in bricks_refs for group in range(ref.shape[0])]
    count = len(bricks)
    step = pl.program_id(0)
    taps = taps_ref.shape[2]
    rim = taps // 2
    planes, rows, width = out_ref.shape
    outer = planes + 2 * rim

    @pl.when(step == 0)
    def _():
        logs[...] = jnp.zeros_like(logs)
        side, middle = first_ref.shape[0], own_ref.shape[0]
        flip = 1 - place_ref[1] if paired else 0
        for z in range(side):
            volume[(side + middle) * flip + z] = first_ref[z]
            volume[(side + middle) * (1 - flip) + z] = second_ref[z]
        for z in range(middle):
            volume[side + z] = own_ref[z]

    def along_z(source, gains, z, length):
        sums = [[] for _ in range(length)]
        for k in range(0, rows, 8):
            column = [source[z + t, pl.ds(k, 8), :] for t in range(length + 2 * rim)]
            for i in range(length):
                total = column[i + rim]
                for t in range(taps):
                    if t != rim:
                        total = total + gains[t] * column[i + t]
                sums[i].append(total)
        return [jnp.concatenate(tiles, axis=0) for tiles in sums]

    def chain(source, gains, left, right, z, length):
        fields = along_z(source, gains, z, length)
        flats = []
        for i in range(0, length, 2):
            high, low = halves(jnp.concatenate(fields[i : i + 2], axis=1))
            stacked = jnp.concatenate([high, low, high], axis=0)
            parts = halves(jnp.dot(left, stacked, preferred_element_type=jnp.float32))
            for j in range(2):
                flats.append(jnp.concatenate([part[:, j * width : (j + 1) * width] for part in parts], axis=1))
        right = jnp.concatenate(
            [right, jnp.concatenate([right[:, :width], jnp.zeros((width, width), jnp.bfloat16)], axis=1)], axis=0
        )
        product = jnp.dot(jnp.concatenate(flats, axis=0), right, preferred_element_type=jnp.float32)
        total = product[:, :width] + product[:, width:]
        return [total[i * rows : (i + 1) * rows] for i in range(length)]

    def chunks(length):
        size = next(size for size in (8, 4, 2) if length % size == 0 and length > size or size == 2)
        return [(z, size) for z in range(0, length, size)]

    for first in range(0, count, 2):
        pair = (first, first + 1)
        gains = [[taps_ref[group * pl.num_programs(0) + step, 0, t] for t in range(taps)] for group in pair]
        for z, size in chunks(outer):
            for group, gain in zip(pair, gains):
                fields = chain(volume, gain, lefts_ref[group, 0, 0], rights_ref[group, 0, 0], z, size)
                for i, blurred in enumerate(fields):
                    guess = pl.reciprocal(blurred, approx=True)
                    guess = guess * (2.0 - blurred * guess)
                    ratios[group, z + i] = bricks[group][0, z + i].astype(jnp.float32) * guess
        for z, size in chunks(planes):
            backs = [
                chain(ratios.at[group], gain[::-1], lefts_ref[group, 0, 1], rights_ref[group, 0, 1], z, size)
                for group, gain in zip(pair, gains)
            ]
            for i in range(size):
                logs[z + i] += jnp.log(backs[0][i] * backs[1][i])

    @pl.when(step == pl.num_programs(0) - 1)
    def _():
        for z in range(planes):
            out_ref[z] = volume[2 * rim + z] * jnp.exp(logs[z] / (count * pl.num_programs(0)))


def update(place, taps, band, bricks, halo, own, planes, paired):
    _, count, outer, rows, width = bricks[0].shape
    groups = sum(part.shape[0] for part in bricks)
    band = [part.reshape((groups, count) + part.shape[1:]) for part in band]
    step = lambda v: (0, v, 0, 0, 0)
    return pl.pallas_call(
        functools.partial(update_kernel, paired),
        grid=(count,),
        out_shape=jax.ShapeDtypeStruct((planes, rows, width), jnp.float32),
        in_specs=[SMEM, SMEM]
        + [pl.BlockSpec((groups, 1) + part.shape[2:], step) for part in band]
        + [pl.BlockSpec((part.shape[0], 1, outer, rows, width), step) for part in bricks]
        + [VMEM] * 3,
        out_specs=VMEM,
        scratch_shapes=[
            pltpu.VMEM((2 * outer - planes, rows, width), jnp.float32),
            pltpu.VMEM((groups, outer, rows, width), jnp.float32),
            pltpu.VMEM((planes, rows, width), jnp.float32),
        ],
        compiler_params=PARAMS,
    )(place, taps, *band, *bricks, halo[0], own, halo[1])


def place_kernel(planes, place_ref, *refs):
    parts, out_ref = refs[:-1], refs[-1]
    blocks, members = out_ref.shape[:2]
    slot = place_ref[0]
    for index, part in enumerate(parts):
        for block in range(blocks):
            at = slot ^ index
            at = members - 1 - at if block % 2 else at
            out_ref[block, at] = part[block * planes : (block + 1) * planes]


def place_parts(slot, parts, planes):
    depth, rows, width = parts[0].shape
    return pl.pallas_call(
        functools.partial(place_kernel, planes),
        out_shape=jax.ShapeDtypeStruct((depth // planes, len(parts), planes, rows, width), jnp.float32),
        in_specs=[SMEM] + [VMEM] * len(parts),
        out_specs=VMEM,
        compiler_params=PARAMS,
    )(slot, *parts)


def partner(value, bit, members):
    return lax.ppermute(value, "view", [(i, i ^ bit) for i in range(members)])


def line_device(line, members, blocks):
    block, slab = divmod(line, members)
    return (members - 1 - slab if block % 2 else slab) * blocks + block


def swap(value, pairs, members, blocks):
    at = lambda line: line_device(line, members, blocks)
    perm = [(at(i), at(j)) for i, j in pairs] + [(at(j), at(i)) for i, j in pairs]
    return lax.ppermute(value, ("view", "vol"), perm)


def z_rims(own, inner, outer, members, blocks):
    planes = own.shape[0]
    at = lambda line: line_device(line, members, blocks)
    total = members * blocks
    before, after = [], []
    for hop in range(inner // planes + 1, -(-outer // planes) + 1):
        near, far = max((hop - 1) * planes, inner), min(hop * planes, outer)
        up = [(at(i), at(i + hop)) for i in range(total - hop)]
        down = [(at(i + hop), at(i)) for i in range(total - hop)]
        before.append(lax.ppermute(own[hop * planes - far : hop * planes - near], ("view", "vol"), up))
        after.append(lax.ppermute(own[near - (hop - 1) * planes : far - (hop - 1) * planes], ("view", "vol"), down))
    join = lambda parts: parts[0] if len(parts) == 1 else jnp.concatenate(parts)
    return join(before[::-1]), join(after)


def per_device(raw_views, weights, offsets, psf_taps):
    views, depth, rows, width = raw_views.shape
    members, blocks = lax.axis_size("view"), lax.axis_size("vol")
    rim = (psf_taps.shape[2] - 1) // 2
    planes = depth // members
    me = lax.axis_index("view")
    slab = slab_index()
    place = jnp.stack([slab // CORES, slab % CORES]).astype(jnp.int32)

    near_bit, far_bit = 1, CORES
    near = lambda value: partner(value, near_bit, members)
    far = lambda value: partner(value, far_bit, members)
    seams = [(members * block + members - 1 - i, members * (block + 1) + i) for block in range(blocks - 1) for i in range(CORES)]
    across = lambda value: swap(value, seams, members, blocks)
    bound, inner = (0, depth - rim), (rim, 2 * planes - rim)

    cross_taps = partner(psf_taps, near_bit + far_bit, members)
    far_bound = resample_bound(weights, offsets, raw_views, rim)
    far_bound, raw_later, cross_taps = lax.optimization_barrier((far_bound, raw_views, cross_taps))
    far_bound = far(far_bound)
    far_inner, own_bound, own_inner = resample(
        place,
        weights,
        offsets,
        raw_later,
        (2 * planes, rim, 2 * planes),
        [(True, inner), (False, bound), (False, inner)],
    )
    far_inner, cross_taps = lax.optimization_barrier((far_inner, cross_taps))
    far_inner = far(far_inner)
    near_inner = near(own_inner)
    pair_taps = near(jnp.stack([psf_taps, cross_taps]))
    all_taps = jnp.concatenate([psf_taps, pair_taps[0], pair_taps[1], cross_taps])
    all_taps = all_taps / jnp.sum(all_taps, axis=-1, keepdims=True)
    centre = all_taps[:, :1, rim : rim + 1]
    all_taps = jnp.concatenate([all_taps[:, :1] / centre, all_taps[:, 1:2], all_taps[:, 2:] * centre], axis=1)
    band = bands(all_taps, rows, width)
    bounds = jnp.concatenate([own_bound, far_bound])
    edges = across(bounds)
    edges, band = lax.optimization_barrier((edges, band))
    bounds, edges = [bounds, near(bounds)], [edges, near(edges)]
    home, partial = gather_views(place, [own_inner, near_inner], bounds, edges, planes, 0)
    far_inner, home, partial = lax.optimization_barrier((far_inner, home, partial))
    away, start, near_send, cross_send = gather_views(
        place, [far_inner, near(far_inner)], bounds, edges, planes, 1, members * views, partial
    )
    bricks = [home, away]
    lines = members * blocks
    gaps = [(i, i + 1) for i in range(1, lines - 1, 2)]
    paired = planes == 2 * rim
    if paired:
        halo = (near(near_send), swap(cross_send, gaps, members, blocks))
    else:
        halo = z_rims(start[rim : rim + planes], rim, 2 * rim, members, blocks)
    joined = update(place, all_taps, band, bricks, halo, start, planes, paired)
    for turn in range(1, ITERS):
        if paired:
            halo = (near(joined), swap(joined, gaps, members, blocks))
        else:
            halo = z_rims(joined, 0, 2 * rim, members, blocks)
        joined = update(place, all_taps, band, bricks, halo, joined, planes, paired)

    columns = lax.all_to_all(joined, "vol", split_axis=1, concat_axis=0, tiled=True)
    far_columns = far(columns)
    parts = [columns, near(columns), far_columns, near(far_columns)]
    result = place_parts(me.reshape(1).astype(jnp.int32), parts, planes)
    return result.reshape((blocks * depth,) + columns.shape[1:])


def solution(mesh):
    placed = (
        P("view", "vol", None, None),
        P("view", None, None),
        P("view", None),
        P("view", None, None),
    )
    return jax.shard_map(
        per_device, mesh=mesh, in_specs=placed, out_specs=P(None, "vol", None), check_vma=False
    )
```
